256 devices in a mesh: ctx: 8 (over x_lo, y), exp: 32 (over z, x_hi, core).
Axes of the slice: x: 4 (x_hi: 2, x_lo: 2; x = x_hi * 2 + x_lo), y: 4, z: 8, core: 2. Of those that a mesh axis runs over, the one named last changes fastest.
Arguments:
- hidden_in: bfloat16 [32, 1024, 2048], P('exp', 'ctx'), may hold values from -3 to 3
- query: bfloat16 [32, 1024, 4096], P('exp', 'ctx'), may hold values from -96 to 96
- keyval: bfloat16 [32, 1024, 512], P('exp', 'ctx'), may hold values from -5 to 5
- out_proj: bfloat16 [4096, 2048], P('exp'), may hold values from -0.375 to 0.375
- norm_gain: bfloat16 [2048], replicated, may hold values from 0.099609375 to 1.8984375
- expert_ids: int32 [32, 1024, 8], P('exp', 'ctx'), may hold values from 0 to 31, all different within a row; in each aligned block of 128 rows (0 to 127, 128 to 255, ..., all dimensions but the last counted through in order) at most 34 rows name the same one
- gate_weights: float32 [32, 1024, 8], P('exp', 'ctx'), may hold values from 0.1 to 0.4
- w_gate: bfloat16 [32, 2048, 768], P('exp'), may hold values from -0.125 to 0.125
- w_up: bfloat16 [32, 2048, 768], P('exp'), may hold values from -0.125 to 0.125
- w_down: bfloat16 [32, 768, 2048], P('exp'), may hold values from -0.21875 to 0.21875
Outputs:
- layer_out: bfloat16 [32, 1024, 2048], P('exp', 'ctx')
The draws below stay inside these ranges and needn't reach their ends.
Inputs may be any that keep to these rules, and one draw needn't show every extreme that they name: `expert_ids`: in each aligned block of 128 tokens (the tokens of one device) no expert is named by more than 34 tokens, a bound that some block reaches; a token names 8 different experts.
All inputs are finite; a program needn't handle non-finite values.
Results may differ from the reference program's by a relative error of at most 0.014.
Values may be sent and summed in bfloat16 or wider, within the bound.
A program may use at most 128 MiB of HBM per device.

```python
import math
import jax
import jax.numpy as jnp
import numpy as np
from jax import lax

D = 2048
QH = 32
KVH = 2
HD = 128
EF = 768
TOP = 8
TOK_DEV = 128
EXPERTS = 32
LENGTH = 1024
SEQS = 32
CAP = 34


def shared_keyval(key):
    key_value = jax.random.normal(key, (SEQS, LENGTH, 2 * KVH * HD), jnp.float32)
    return jnp.clip(key_value, -5.0, 5.0)


def draw_keyval(key, part):
    return shared_keyval(key).astype(jnp.bfloat16)


def draw_query(key, part):
    key = jax.random.fold_in(key, 7)
    query_key = jax.random.fold_in(key, 0)
    queries = jnp.clip(2.0 * jax.random.normal(query_key, (SEQS, LENGTH, QH * HD), jnp.float32), -12.0, 12.0)
    return queries.astype(jnp.bfloat16)


def levels(own_key, shape, shards, low, top_value):
    factor_of, own = 1.0, jax.random.fold_in(own_key, 6)
    for position, shards_of in shards:
        draws = jnp.exp(jax.random.uniform(jax.random.fold_in(own, position), (shards_of,), jnp.float32, low / len(shards), top_value / len(shards)))
        factor_of = factor_of * jnp.repeat(draws, shape[position] // shards_of).reshape([-1 if axis == position else 1 for axis in range(len(shape))])
    return factor_of


def assign_block(rng, own, number, rows, amount, top, most, skew):
    order = jax.random.permutation(rng, amount)
    heavy_load, common = load_shares(amount, rows * top, most, skew, True), load_shares(amount, rows * top, most, skew, False)
    places = jnp.arange(amount)

    def named(lengths, rotation):
        used = int((lengths > 0).sum())
        fixed = max(1, used // 4)
        shifted = fixed + (places - fixed + rotation * (used - fixed)) % max(1, amount - fixed)
        return jnp.zeros((amount,), jnp.int32).at[order[jnp.where(places < fixed, places, shifted)]].set(jnp.asarray(lengths, jnp.int32))

    lengths = jnp.where(number % 4 == 0, named(heavy_load, number // 4), named(common, number - number // 4 - 1))
    mixed = jax.random.permutation(jax.random.fold_in(own, 3), amount)
    giver, receiver = mixed[0:amount // 2 * 2:2], mixed[1:amount // 2 * 2:2]
    margin = jnp.minimum(lengths[giver] - 1, most - lengths[receiver]) // 2
    margin = jnp.where((giver == order[0]) | (receiver == order[0]) | (lengths[receiver] == 0), 0, jnp.maximum(margin, 0))
    shifted = jax.random.randint(jax.random.fold_in(own, 4), (amount // 2,), 0, 1 << 20) % (margin + 1)
    lengths = lengths.at[giver].add(-shifted).at[receiver].add(shifted)
    items = jnp.searchsorted(jnp.cumsum(lengths), jnp.arange(rows * top), side="right").astype(jnp.int32)
    grid = items.reshape(top, rows).T
    grid = grid[jax.random.permutation(jax.random.fold_in(own, 1), rows)]
    rotation = jax.random.randint(jax.random.fold_in(own, 2), (rows, 1), 0, top)
    return jnp.take_along_axis(grid, (jnp.arange(top)[None, :] + rotation) % top, axis=1)


def load_shares(number_of, total, limit, slope, full):
    loads = [(1 << 20) // math.isqrt(standing ** slope) + 1 for standing in range(1, number_of + 1)]
    largest = limit if full else min(limit, max(-(-total // number_of), total * loads[0] // sum(loads)))
    least = 1 if total - largest >= number_of - 1 else 0
    given, spare = [largest] + [least] * (number_of - 1), total - largest - least * (number_of - 1)
    while spare > 0:
        candidates = [i for i in range(1, number_of) if given[i] < largest] or [i for i in range(1, number_of) if given[i] < limit]
        mass, left = sum([loads[i] for i in candidates]), spare
        for i in candidates:
            extra = min(limit - given[i], max(1, left * loads[i] // mass), spare)
            given[i] = given[i] + extra
            spare = spare - extra
    return np.array(given)


def bell_draw(own_key, dims, scale, most, cuts=(), kind=jnp.bfloat16):
    values = scale * jax.random.normal(own_key, dims, jnp.float32)
    if cuts:
        values = values * levels(own_key, dims, cuts, -0.22, 0.18)
    return jnp.clip(values, -most, most).astype(kind)


def setup_inputs(seed: int = 0) -> dict:
    seeds = jax.random.split(jax.random.key(seed), 11)
    hidden_in = bell_draw(seeds[0], (SEQS, LENGTH, D), 0.5, 3.0, ((0, 32), (1, 8)))
    query = draw_query(jax.random.fold_in(seeds[10], 71), 0)
    keyval = draw_keyval(jax.random.fold_in(seeds[10], 71), 0)
    out_proj = bell_draw(seeds[3], (QH * HD, D), (QH * HD // 16) ** -0.5, 0.375, ((0, 32),))
    norm_gain = jnp.clip(1.0 + 0.18 * jax.random.normal(seeds[4], (D,), jnp.float32), 0.099609375, 1.8984375).astype(jnp.bfloat16)
    expert_ids_keys = jax.random.split(jax.random.fold_in(seeds[5], 1), SEQS * LENGTH // TOK_DEV)
    expert_ids_turns = jax.random.permutation(jax.random.fold_in(seeds[5], 3), SEQS * LENGTH // TOK_DEV)
    expert_ids = jax.vmap(lambda own, number: assign_block(jax.random.fold_in(seeds[5], 2), own, number, TOK_DEV, EXPERTS, TOP, CAP, 1))(expert_ids_keys, expert_ids_turns).reshape((SEQS, LENGTH, TOP))
    gate_weights = jnp.clip(0.1 + 0.3 * jax.random.uniform(seeds[6], (SEQS, LENGTH, TOP), jnp.float32) ** levels(seeds[6], (SEQS, LENGTH, TOP), ((0, 32), (1, 8)), -0.2, 0.2), 0.1, 0.4)
    w_gate = bell_draw(seeds[7], (EXPERTS, D, EF), D ** -0.5, 0.125, ((0, 32),))
    w_up = bell_draw(seeds[8], (EXPERTS, D, EF), D ** -0.5, 0.125, ((0, 32),))
    w_down = bell_draw(seeds[9], (EXPERTS, EF, D), EF ** -0.5, 0.21875, ((0, 32),))
    return {"hidden_in": hidden_in, "query": query, "keyval": keyval, "out_proj": out_proj, "norm_gain": norm_gain, "expert_ids": expert_ids, "gate_weights": gate_weights, "w_gate": w_gate, "w_up": w_up, "w_down": w_down}


def sequence_attention(query_seq, key_value):
    length = query_seq.shape[0]
    group_size = QH // KVH
    queries = query_seq.astype(jnp.float32).reshape(length, KVH, group_size, HD)
    key_rows = key_value[:, :KVH * HD].astype(jnp.float32).reshape(length, KVH, HD)
    values = key_value[:, KVH * HD:].astype(jnp.float32).reshape(length, KVH, HD)
    scores = jnp.einsum('qhgd,khd->hgqk', queries, key_rows, precision=lax.Precision.HIGHEST) * HD ** (-0.5)
    positions = jnp.arange(length, dtype=jnp.int32)
    visible = positions[:, None] >= positions[None, :]
    scores = jnp.where(visible, scores, -1e+30)
    row_max = lax.optimization_barrier(jnp.max(scores, axis=-1, keepdims=True))
    weights = jnp.where(visible, jnp.exp(scores - row_max), 0.0)
    row_sum = lax.optimization_barrier(jnp.sum(weights, axis=-1))
    weights_b = lax.optimization_barrier(weights.astype(jnp.bfloat16)).astype(jnp.float32)
    mixed = jnp.einsum('hgqk,khd->hgqd', weights_b, values, precision=lax.Precision.HIGHEST) / row_sum[..., None]
    return mixed.transpose(2, 0, 1, 3).reshape(length, QH * HD).astype(jnp.bfloat16)

def reference(hidden_in, query, keyval, out_proj, norm_gain, expert_ids, gate_weights, w_gate, w_up, w_down):
    attended = lax.map(lambda inputs: sequence_attention(inputs[0], inputs[1]), (query, keyval))
    tokens = SEQS * LENGTH
    flat_heads = attended.reshape(tokens, QH * HD)
    projected = jnp.dot(flat_heads, out_proj, preferred_element_type=jnp.float32)
    residual = hidden_in.reshape(tokens, D).astype(jnp.float32) + projected
    scale_inv = lax.rsqrt(lax.optimization_barrier(jnp.mean(residual * residual, axis=-1, keepdims=True)) + 1e-06)
    normed = (residual * scale_inv * norm_gain.astype(jnp.float32)).astype(jnp.bfloat16)
    blocks = tokens // TOK_DEV
    routes = expert_ids.reshape(blocks, TOK_DEV * TOP).astype(jnp.int32)
    onehot = (routes[:, :, None] == jnp.arange(EXPERTS, dtype=jnp.int32)[None, None, :]).astype(jnp.int32)
    slot_rank = lax.optimization_barrier(jnp.sum(onehot * (jnp.cumsum(onehot, axis=1) - 1), axis=2)).astype(jnp.int32)
    block_ids = jnp.broadcast_to(jnp.arange(blocks, dtype=jnp.int32)[:, None], routes.shape)
    pair_ids = jnp.broadcast_to(jnp.arange(TOK_DEV * TOP, dtype=jnp.int32)[None, :], routes.shape)
    slot_table = jnp.full((EXPERTS, blocks, CAP), -1, jnp.int32).at[routes, block_ids, slot_rank].set(pair_ids)
    gate_flat = gate_weights.reshape(tokens * TOP).astype(jnp.float32)

    def one_expert(running, inputs):
        slots, gate_mat, up_mat, down_mat = inputs
        filled = (slots >= 0).reshape(-1)
        pair_idx = jnp.where(slots >= 0, slots, 0).astype(jnp.int32)
        global_pair = (jnp.arange(blocks, dtype=jnp.int32)[:, None] * (TOK_DEV * TOP) + pair_idx).reshape(-1)
        token_idx = (global_pair // TOP).astype(jnp.int32)
        gathered = normed[token_idx]
        gate_pre = jnp.dot(gathered, gate_mat, preferred_element_type=jnp.float32)
        up_pre = jnp.dot(gathered, up_mat, preferred_element_type=jnp.float32)
        activated = (jax.nn.silu(gate_pre) * up_pre).astype(jnp.bfloat16)
        expert_out = jnp.dot(activated, down_mat, preferred_element_type=jnp.float32).astype(jnp.bfloat16)
        expert_out = lax.optimization_barrier(expert_out).astype(jnp.float32)
        weight = jnp.where(filled, gate_flat[global_pair], 0.0)
        return (running.at[token_idx].add(weight[:, None] * expert_out), None)
    expert_sum, _ = lax.scan(one_expert, jnp.zeros((tokens, D), jnp.float32), (slot_table, w_gate, w_up, w_down))
    result = (residual + expert_sum).astype(jnp.bfloat16)
    return result.reshape(SEQS, LENGTH, D)
```

```python
import math

import jax
import jax.numpy as jnp
from jax import lax
from jax.experimental import pallas as pl
from jax.experimental.pallas import tpu as pltpu
from jax.sharding import PartitionSpec as P

D = 2048
QH = 32
KVH = 2
HD = 128
EF = 768
TOP = 8
TOK = 128
EXPERTS = 32
CAP = 34
ROWS = 144
HALF = 64
NZ = 8
NCTX = 8
MESH = pl.DeviceIdType.MESH
BF = jnp.bfloat16
F32 = jnp.float32

A0, A1, B0 = 0, 1, 2
STREAM = ((0, 0), (1, 0), (0, 1))
HOPS = ((4, 3), (3, 4), (4, 3))


class Place:
    def __init__(self):
        ctx, exp = lax.axis_index("ctx"), lax.axis_index("exp")
        self.ctx, self.exp = ctx, exp
        self.xlo, self.y = ctx // 4, ctx % 4
        self.z, self.xhi, self.core = exp // 4, (exp // 2) % 2, exp % 2

    def device(self, xlo, z, xhi, core):
        return {"ctx": xlo * 4 + self.y, "exp": z * 4 + xhi * 2 + core}

    def up(self):
        return self.device(self.xlo, (self.z + 1) % NZ, self.xhi, self.core)

    def down(self):
        return self.device(self.xlo, (self.z + NZ - 1) % NZ, self.xhi, self.core)

    def cross(self):
        return self.device(1 - self.xlo, self.z, 1 - self.xhi, self.core)

    def peer(self):
        return self.device(self.xlo, self.z, self.xhi, 1 - self.core)

    def plane(self, rel):
        return (self.z + rel + NZ) % NZ

    def column(self, col):
        return self.xhi if col == 0 else 1 - self.xhi

    def slot(self, rel, col, core=None):
        core = self.core if core is None else core
        return self.plane(rel) * 4 + self.column(col) * 2 + core


def rels(k):
    return (0,) if k == 0 else ((4,) if k == 4 else (-k, k))


def remote(src, dst, send, recv, device):
    return pltpu.make_async_remote_copy(
        src_ref=src, dst_ref=dst, send_sem=send, recv_sem=recv, device_id=device, device_id_type=MESH
    )


class Gather:
    def __init__(self, at, buf, zs, zr, cs, cr, ps, pr):
        self.at, self.buf = at, buf
        self.zs, self.zr, self.cs, self.cr, self.ps, self.pr = zs, zr, cs, cr, ps, pr
        self.sent = {k: [] for k in range(5)}

    def rows(self, rel, col, half, core=None):
        start = self.at.slot(rel, col, core) * TOK + half * HALF
        return self.buf.at[pl.ds(pl.multiple_of(start, HALF), HALF)]

    def go(self, k, copy):
        copy.start()
        self.sent[k].append(copy)

    def hop(self, stream, direction, k):
        col, half = STREAM[stream]
        if k > HOPS[stream][direction]:
            return
        rel = -(k - 1) if direction == 0 else k - 1
        ref = self.rows(rel, col, half)
        to = self.at.up() if direction == 0 else self.at.down()
        self.go(abs(rel), remote(ref, ref, self.zs.at[stream, direction, k], self.zr.at[stream, direction, k], to))

    def crossing(self, rel, half):
        ref = self.rows(rel, 0, half)
        index = rel % NZ if half == 1 else NZ
        return remote(ref, ref, self.cs.at[index], self.cr.at[index], self.at.cross())

    def crossed(self, rel, half):
        ref = self.rows(rel, 1, half)
        index = rel % NZ if half == 1 else NZ
        remote(ref, ref, self.cs.at[index], self.cr.at[index], self.at.cross()).wait_recv()

    def share(self, rel, col, half):
        ref = self.rows(rel, col, half)
        index = (rel % NZ) * 4 + col * 2 + half
        self.go(abs(rel), remote(ref, ref, self.ps.at[index], self.pr.at[index], self.at.peer()))

    def begin(self):
        self.go(0, self.crossing(0, 0))
        for stream in (A0, B0):
            for direction in (0, 1):
                self.hop(stream, direction, 1)
        self.go(0, self.crossing(0, 1))
        self.share(0, 0, 0)
        self.share(0, 0, 1)

    def begin_column(self):
        self.crossed(0, 0)
        for direction in (0, 1):
            self.hop(A1, direction, 1)
        self.share(0, 1, 0)

    def ring(self, k):
        for stream in (A0, B0, A1):
            col, half = STREAM[stream]
            for direction in (0, 1):
                if k > HOPS[stream][direction]:
                    continue
                rel = -k if direction == 0 else k
                rel = 4 if k == 4 else rel
                ref = self.rows(rel, col, half)
                sem = self.zr.at[stream, direction, k]
                remote(ref, ref, self.zs.at[stream, direction, k], sem, self.at.up()).wait_recv()
                self.hop(stream, direction, k + 1)
                if stream == B0:
                    self.go(k, self.crossing(rel, 1))
                self.share(rel, col, half)

    def column(self, k):
        for rel in rels(k):
            self.crossed(rel, 1)
            self.share(rel, 1, 1)

    def shared(self, k):
        for rel in rels(k):
            for col in (0, 1):
                for half in (0, 1):
                    ref = self.rows(rel, col, half, 1 - self.at.core)
                    index = (rel % NZ) * 4 + col * 2 + half
                    remote(ref, ref, self.ps.at[index], self.pr.at[index], self.at.peer()).wait_recv()

    def settle(self, k):
        for copy in self.sent[k]:
            copy.wait_send()


GATHER_SEMS = [
    pltpu.SemaphoreType.DMA((3, 2, 5)),
    pltpu.SemaphoreType.DMA((3, 2, 5)),
    pltpu.SemaphoreType.DMA((9,)),
    pltpu.SemaphoreType.DMA((9,)),
    pltpu.SemaphoreType.DMA((32,)),
    pltpu.SemaphoreType.DMA((32,)),
]


def attention_kernel(
    hidden_ref, query_ref, kv_ref, proj_ref, gain_ref, gates_ref,
    residual_ref, normed_ref, gates_out,
    weights, heads, kvs, scores, mixed, total,
    zs, zr, cs, cr, ps, pr, ks, kr, gs, gr, own_sem,
):
    at = Place()
    position = at.ctx

    def gate_target(off):
        other = (at.exp + off) % EXPERTS
        other_hi = (other // 2) % 2
        return other, {"ctx": ((at.xlo + at.xhi + other_hi) % 2) * 4 + at.y, "exp": other}

    barrier = pltpu.get_barrier_semaphore()

    def greet(off, carry):
        _, device = gate_target(off)
        pl.semaphore_signal(barrier, inc=1, device_id=device, device_id_type=MESH)
        return carry

    lax.fori_loop(1, EXPERTS, greet, 0)
    for off in range(1, NCTX):
        device = {"ctx": (position + off) % NCTX, "exp": at.exp}
        pl.semaphore_signal(barrier, inc=1, device_id=device, device_id_type=MESH)

    own = pltpu.make_async_copy(proj_ref, weights.at[pl.ds(at.exp * TOK, TOK)], own_sem)
    own.start()
    kvs[pl.ds(pl.multiple_of(position * TOK, TOK), TOK), :] = kv_ref[...]
    for h in range(QH):
        heads[h * TOK : (h + 1) * TOK, :] = query_ref[:, h * HD : (h + 1) * HD]
    gates_out[pl.ds(at.exp, 1)] = gates_ref[pl.ds(at.exp, 1)]
    own.wait()
    pl.semaphore_wait(barrier, EXPERTS - 1 + NCTX - 1)

    gather = Gather(at, weights, zs, zr, cs, cr, ps, pr)
    gather.begin()

    kv_copies = []
    mine = kvs.at[pl.ds(pl.multiple_of(position * TOK, TOK), TOK)]
    for off in (1, 7, 4, 3, 5, 2, 6):
        device = {"ctx": (position + off) % NCTX, "exp": at.exp}
        copy = remote(mine, mine, ks.at[off], kr.at[off], device)
        copy.start()
        kv_copies.append((off, copy))

    def send_gates(off, carry):
        other, device = gate_target(off)
        remote(gates_ref.at[other], gates_out.at[at.exp], gs.at[off], gr.at[off], device).start()
        return carry

    lax.fori_loop(1, EXPERTS, send_gates, 0)
    gather.begin_column()

    for off, _ in kv_copies:
        origin = (position + NCTX - off) % NCTX
        ref = kvs.at[pl.ds(pl.multiple_of(origin * TOK, TOK), TOK)]
        device = {"ctx": origin, "exp": at.exp}
        remote(ref, ref, ks.at[off], kr.at[off], device).wait_recv()

    scale = HD ** (-0.5) * math.log2(math.e)
    last = position // 2
    row_pos = position * TOK + lax.broadcasted_iota(jnp.int32, (2 * TOK, 2 * TOK), 0) % TOK
    key_pos = last * 2 * TOK + lax.broadcasted_iota(jnp.int32, (2 * TOK, 2 * TOK), 1)
    visible = row_pos >= key_pos

    def attend(chunk, carry):
        lane = pl.multiple_of((chunk // 8) * HD, HD)
        q = heads[pl.ds(pl.multiple_of(chunk * 2 * TOK, 2 * TOK), 2 * TOK), :]

        def score(pair):
            keys = kvs[pl.ds(pl.multiple_of(pair * 2 * TOK, 2 * TOK), 2 * TOK), pl.ds(lane, HD)]
            return lax.dot_general(q, keys, (((1,), (1,)), ((), ())), preferred_element_type=F32)

        def first(pair, running):
            s = score(pair)
            scores[pair] = s
            return jnp.maximum(running, jnp.maximum(s[:, :TOK], s[:, TOK:]))

        running = lax.fori_loop(0, last, first, jnp.full((2 * TOK, TOK), -1e30, F32))
        s = jnp.where(visible, score(last), -1e30)
        scores[last] = s
        running = jnp.maximum(running, jnp.maximum(s[:, :TOK], s[:, TOK:]))
        row_max = jnp.max(running, axis=1, keepdims=True)

        def second(pair, state):
            row_sum, acc = state
            weight = jnp.exp2((scores[pair] - row_max) * scale)
            values = kvs[
                pl.ds(pl.multiple_of(pair * 2 * TOK, 2 * TOK), 2 * TOK),
                pl.ds(pl.multiple_of(lane + KVH * HD, HD), HD),
            ]
            acc = acc + jnp.dot(weight.astype(BF), values, preferred_element_type=F32)
            return row_sum + weight[:, :TOK] + weight[:, TOK:], acc

        zero = jnp.zeros((2 * TOK, TOK), F32)
        row_sum, acc = lax.fori_loop(0, last + 1, second, (zero, zero))
        out = (acc / jnp.sum(row_sum, axis=1, keepdims=True)).astype(BF)
        plane, side = chunk // 2, chunk % 2
        for i in range(2):
            columns = pl.ds(pl.multiple_of((side * 2 + i) * HD, HD), HD)
            mixed[plane, :, columns] = out[i * TOK : (i + 1) * TOK]
        return carry

    lax.fori_loop(0, 8, attend, 0)
    gather.column(0)
    gather.ring(1)
    lax.fori_loop(8, 16, attend, 0)

    total[...] = hidden_ref[...].astype(F32)

    def project(rel):
        plane = at.plane(rel)

        def tile(n, carry):
            columns = pl.ds(pl.multiple_of(n * 512, 512), 512)
            part = weights[pl.ds(pl.multiple_of(plane * 512, 512), 512), columns]
            total[:, columns] += jnp.dot(mixed[plane], part, preferred_element_type=F32)
            return carry

        lax.fori_loop(0, 4, tile, 0)

    for k in range(5):
        if k >= 1:
            gather.column(k)
        if k + 1 in (2, 3, 4):
            gather.ring(k + 1)
        gather.shared(k)
        for rel in rels(k):
            project(rel)

    def norm(i, carry):
        rows = pl.ds(pl.multiple_of(i * 16, 16), 16)
        r = total[rows, :]
        inverse = lax.rsqrt(jnp.mean(r * r, axis=-1, keepdims=True) + 1e-06)
        normed_ref[rows, :] = (r * inverse * gain_ref[...].astype(F32)).astype(BF)
        residual_ref[rows, :] = r
        return carry

    lax.fori_loop(0, TOK // 16, norm, 0)

    def take_gates(off, carry):
        other, device = gate_target(off)
        origin = (at.exp + EXPERTS - off) % EXPERTS
        copy = remote(gates_ref.at[other], gates_out.at[origin], gs.at[off], gr.at[off], device)
        copy.wait_send()
        copy.wait_recv()
        return carry

    lax.fori_loop(1, EXPERTS, take_gates, 0)
    for _, copy in kv_copies:
        copy.wait_send()
    for k in range(5):
        gather.settle(k)


def expert_kernel(
    normed_ref, residual_ref, gates_ref, gate_hbm, up_hbm, down_hbm,
    out_ref,
    buf, peer_part, ring_part, cross_part, wg, wu, wd, picked, act, outs,
    zs, zr, cs, cr, ps, pr, rzs, rzr, rcs, rcr, rps, rpr, wsem,
):
    at = Place()
    loads = [
        pltpu.make_async_copy(src, dst, wsem.at[i])
        for i, (src, dst) in enumerate(((gate_hbm, wg), (up_hbm, wu), (down_hbm, wd)))
    ]
    for load in loads:
        load.start()
    barrier = pltpu.get_barrier_semaphore()
    for device in (at.up(), at.down(), at.cross(), at.peer()):
        pl.semaphore_signal(barrier, inc=1, device_id=device, device_id_type=MESH)
    buf[pl.ds(pl.multiple_of(at.exp * TOK, TOK), TOK), :] = normed_ref[...]
    pl.semaphore_wait(barrier, 4)

    gather = Gather(at, buf, zs, zr, cs, cr, ps, pr)
    gather.begin()
    gather.begin_column()

    before = (
        lax.broadcasted_iota(jnp.int32, (TOK, TOK), 0) < lax.broadcasted_iota(jnp.int32, (TOK, TOK), 1)
    ).astype(BF)

    def selection(rel):
        places, gates = [], []
        for s in range(4):
            g = gates_ref[at.plane(rel) * 4 + s]
            named = g > 0.0
            rank = jnp.dot(named.astype(BF), before, preferred_element_type=F32)
            places.append(jnp.where(named, rank + s * CAP, -1.0))
            gates.append(g)
        place = jnp.concatenate(places, axis=1)[0:1]
        gate = jnp.concatenate(gates, axis=1)[0:1]
        number = lax.broadcasted_iota(jnp.int32, (ROWS, 4 * TOK), 0).astype(F32)
        hit = number == place
        gate_rows = jnp.sum(jnp.where(hit, gate, 0.0), axis=1, keepdims=True)
        return hit.astype(BF), gate_rows

    def plane_rows(rel):
        return pl.ds(pl.multiple_of(at.plane(rel) * 512, 512), 512)

    def process(k):
        these = rels(k)
        count = len(these) * ROWS
        chosen = [selection(rel) for rel in these]

        for i, rel in enumerate(these):
            def pick(n, carry):
                columns = pl.ds(pl.multiple_of(n * 512, 512), 512)
                picked[i * ROWS : (i + 1) * ROWS, columns] = jnp.dot(
                    chosen[i][0], buf[plane_rows(rel), columns], preferred_element_type=F32
                ).astype(BF)
                return carry

            lax.fori_loop(0, 4, pick, 0)

        def hidden(n, carry):
            columns = pl.ds(pl.multiple_of(n * 256, 256), 256)
            x = picked[:count, :]
            g = jnp.dot(x, wg[:, columns], preferred_element_type=F32)
            u = jnp.dot(x, wu[:, columns], preferred_element_type=F32)
            act[:count, columns] = (g / (1.0 + jnp.exp(-g)) * u).astype(BF)
            return carry

        lax.fori_loop(0, EF // 256, hidden, 0)
        gate_rows = [c[1] for c in chosen]
        gate_all = gate_rows[0] if len(these) == 1 else jnp.concatenate(gate_rows, axis=0)

        def spread(n, carry):
            columns = pl.ds(pl.multiple_of(n * 512, 512), 512)
            o = jnp.dot(act[:count, :], wd[:, columns], preferred_element_type=F32)
            o = (o * gate_all).astype(BF)
            for i, rel in enumerate(these):
                buf[plane_rows(rel), columns] = lax.dot_general(
                    chosen[i][0], o[i * ROWS : (i + 1) * ROWS], (((0,), (0,)), ((), ())),
                    preferred_element_type=F32,
                ).astype(BF)
            return carry

        lax.fori_loop(0, 4, spread, 0)
        for rel in these:
            for col in (0, 1):
                give_peer(rel, col)

    peer_sent = []

    def peer_copy(rel, col):
        src = buf.at[pl.ds(pl.multiple_of(at.slot(rel, col, 1 - at.core) * TOK, TOK), TOK)]
        dst = peer_part.at[pl.ds(pl.multiple_of((at.plane(rel) * 2 + at.column(col)) * TOK, TOK), TOK)]
        index = (rel % NZ) * 2 + col
        return remote(src, dst, rps.at[index], rpr.at[index], at.peer())

    def give_peer(rel, col):
        copy = peer_copy(rel, col)
        copy.start()
        peer_sent.append(copy)

    for k in range(5):
        if k >= 1:
            gather.column(k)
        else:
            gather.column(0)
        if k + 1 in (1, 2, 3, 4):
            gather.ring(k + 1)
        if k == 0:
            for load in loads:
                load.wait()
        gather.shared(k)
        gather.settle(k)
        process(k)

    back_sent = []

    def mine(rel, col, half):
        return buf.at[pl.ds(pl.multiple_of(at.slot(rel, col) * TOK + half * HALF, HALF), HALF)]

    def from_peer(rel, col, half):
        start = (at.plane(rel) * 2 + at.column(col)) * TOK + half * HALF
        return peer_part.at[pl.ds(pl.multiple_of(start, HALF), HALF)]

    def take_peer(rel):
        for col in (0, 1):
            peer_copy(rel, col).wait_recv()

    def add(target, others):
        def chunk(i, carry):
            rows = pl.ds(pl.multiple_of(i * 16, 16), 16)
            value = target[rows, :].astype(F32)
            for other in others:
                value = value + other[rows, :].astype(F32)
            target[rows, :] = value.astype(BF)
            return carry

        lax.fori_loop(0, HALF // 16, chunk, 0)

    def send_back(copy):
        copy.start()
        back_sent.append(copy)

    def give_cross(rel, half):
        index = rel % NZ if half == 1 else NZ
        send_back(remote(mine(rel, 1, half), cross_part.at[index], rcs.at[index], rcr.at[index], at.cross()))

    def take_cross(rel, half):
        index = rel % NZ if half == 1 else NZ
        part = cross_part.at[index]
        remote(part, part, rcs.at[index], rcr.at[index], at.cross()).wait_recv()
        return part

    def cross_half(rel):
        add(mine(rel, 1, 1), [from_peer(rel, 1, 1)])
        give_cross(rel, 1)

    def ring_slot(stream, direction, k):
        return ring_part.at[(stream * 2 + direction) * 4 + k]

    def take_ring(stream, direction, k):
        part = ring_slot(stream, direction, k)
        remote(
            part, part, rzs.at[stream, direction, k], rzr.at[stream, direction, k], at.up()
        ).wait_recv()
        return part

    def give_ring(stream, direction, k):
        col, half = STREAM[stream]
        if k > HOPS[stream][direction]:
            return
        rel = 4 if k == 4 else (-k if direction == 0 else k)
        others = [from_peer(rel, col, half)]
        if stream == B0:
            others.append(take_cross(rel, 1))
        if k + 1 <= HOPS[stream][direction]:
            others.append(take_ring(stream, direction, k))
        add(mine(rel, col, half), others)
        to = at.down() if direction == 0 else at.up()
        send_back(
            remote(
                mine(rel, col, half),
                ring_slot(stream, direction, k - 1),
                rzs.at[stream, direction, k - 1],
                rzr.at[stream, direction, k - 1],
                to,
            )
        )

    for rel in rels(4):
        take_peer(rel)
        cross_half(rel)
    for k in (4, 3, 2, 1):
        for direction in (0, 1):
            for stream in (A1, A0):
                give_ring(stream, direction, k)
        for rel in rels(k - 1):
            take_peer(rel)
            cross_half(rel)
        for direction in (0, 1):
            give_ring(B0, direction, k)
    add(
        mine(0, 1, 0),
        [from_peer(0, 1, 0), take_ring(A1, 0, 0), take_ring(A1, 1, 0)],
    )
    give_cross(0, 0)

    def finish(half, others):
        def chunk(i, carry):
            rows = pl.ds(pl.multiple_of(i * 16, 16), 16)
            value = mine(0, 0, half)[rows, :].astype(F32)
            for other in others:
                value = value + other[rows, :].astype(F32)
            place = pl.ds(pl.multiple_of(half * HALF + i * 16, 16), 16)
            out_ref[place, :] = (residual_ref[place, :] + value).astype(BF)
            return carry

        lax.fori_loop(0, HALF // 16, chunk, 0)

    finish(1, [from_peer(0, 0, 1), take_cross(0, 1), take_ring(B0, 0, 0), take_ring(B0, 1, 0)])
    finish(0, [from_peer(0, 0, 0), take_ring(A0, 0, 0), take_ring(A0, 1, 0), take_cross(0, 0)])
    for copy in peer_sent + back_sent:
        copy.wait_send()


VMEM = pl.BlockSpec(memory_space=pltpu.VMEM)
ANY = pl.BlockSpec(memory_space=pl.ANY)


def body(
    hidden_in, query, keyval, out_proj, norm_gain, expert_ids, gate_weights, w_gate, w_up, w_down
):
    names = jnp.arange(EXPERTS, dtype=jnp.int32)[:, None, None]
    gates = jnp.sum(
        jnp.where(expert_ids[0].T[None] == names, gate_weights[0].T[None], 0.0), axis=1
    )
    gates = jnp.broadcast_to(gates[:, None, :], (EXPERTS, 8, TOK))

    residual, normed, routed = pl.pallas_call(
        attention_kernel,
        out_shape=(
            jax.ShapeDtypeStruct((TOK, D), F32),
            jax.ShapeDtypeStruct((TOK, D), BF),
            jax.ShapeDtypeStruct((EXPERTS, 8, TOK), F32),
        ),
        in_specs=[VMEM, VMEM, VMEM, ANY, VMEM, VMEM],
        out_specs=(VMEM, VMEM, VMEM),
        scratch_shapes=[
            pltpu.VMEM((QH * HD, D), BF),
            pltpu.VMEM((QH * TOK, HD), BF),
            pltpu.VMEM((NCTX * TOK, 2 * KVH * HD), BF),
            pltpu.VMEM((4, 2 * TOK, 2 * TOK), F32),
            pltpu.VMEM((NZ, TOK, 4 * HD), BF),
            pltpu.VMEM((TOK, D), F32),
            *GATHER_SEMS,
            pltpu.SemaphoreType.DMA((NCTX,)),
            pltpu.SemaphoreType.DMA((NCTX,)),
            pltpu.SemaphoreType.DMA((EXPERTS,)),
            pltpu.SemaphoreType.DMA((EXPERTS,)),
            pltpu.SemaphoreType.DMA(()),
        ],
        compiler_params=pltpu.CompilerParams(
            collective_id=0, has_side_effects=True, vmem_limit_bytes=48 << 20
        ),
        name="attend_project",
    )(hidden_in[0], query[0], keyval[0], out_proj, norm_gain.reshape(1, D), gates)

    result = pl.pallas_call(
        expert_kernel,
        out_shape=jax.ShapeDtypeStruct((TOK, D), BF),
        in_specs=[VMEM, VMEM, VMEM, ANY, ANY, ANY],
        out_specs=VMEM,
        scratch_shapes=[
            pltpu.VMEM((EXPERTS * TOK, D), BF),
            pltpu.VMEM((EXPERTS * TOK // 2, D), BF),
            pltpu.VMEM((24, HALF, D), BF),
            pltpu.VMEM((9, HALF, D), BF),
            pltpu.VMEM((D, EF), BF),
            pltpu.VMEM((D, EF), BF),
            pltpu.VMEM((EF, D), BF),
            pltpu.VMEM((2 * ROWS, D), BF),
            pltpu.VMEM((2 * ROWS, EF), BF),
            pltpu.VMEM((8, 128), BF),
            *GATHER_SEMS,
            pltpu.SemaphoreType.DMA((3, 2, 4)),
            pltpu.SemaphoreType.DMA((3, 2, 4)),
            pltpu.SemaphoreType.DMA((9,)),
            pltpu.SemaphoreType.DMA((9,)),
            pltpu.SemaphoreType.DMA((16,)),
            pltpu.SemaphoreType.DMA((16,)),
            pltpu.SemaphoreType.DMA((3,)),
        ],
        compiler_params=pltpu.CompilerParams(
            collective_id=1, has_side_effects=True, vmem_limit_bytes=58 << 20
        ),
        name="experts",
    )(normed, residual, routed, w_gate[0], w_up[0], w_down[0])
    return result[None]


def solution(mesh):
    in_specs = (
        P("exp", "ctx", None),
        P("exp", "ctx", None),
        P("exp", "ctx", None),
        P("exp", None),
        P(),
        P("exp", "ctx", None),
        P("exp", "ctx", None),
        P("exp", None, None),
        P("exp", None, None),
        P("exp", None, None),
    )
    out_specs = P("exp", "ctx", None)
    return jax.shard_map(body, mesh=mesh, in_specs=in_specs, out_specs=out_specs, check_vma=False)
```

```python
import functools
import math

import jax
import jax.numpy as jnp
from jax import lax
from jax.experimental import pallas as pl
from jax.experimental.pallas import tpu as pltpu
from jax.sharding import PartitionSpec as P

D = 2048
QH = 32
KVH = 2
HD = 128
EF = 768
TOP = 8
TOK = 128
EXPERTS = 32
CAP = 34
ROWS = 144
HALF = 64
DIRECT = 1024
QUARTER = 256
NZ = 8
NCTX = 8
MESH = pl.DeviceIdType.MESH
BF = jnp.bfloat16
F32 = jnp.float32

A0, A1, B0 = 0, 1, 2
STREAM = ((0, 0), (1, 0), (0, 1))
HOPS = ((4, 3), (3, 4), (4, 3))


class Place:
    def __init__(self):
        ctx, exp = lax.axis_index("ctx"), lax.axis_index("exp")
        self.ctx, self.exp = ctx, exp
        self.xlo, self.y = ctx // 4, ctx % 4
        self.z, self.xhi, self.core = exp // 4, (exp // 2) % 2, exp % 2

    def device(self, xlo, z, xhi, core):
        return {"ctx": xlo * 4 + self.y, "exp": z * 4 + xhi * 2 + core}

    def up(self):
        return self.device(self.xlo, (self.z + 1) % NZ, self.xhi, self.core)

    def down(self):
        return self.device(self.xlo, (self.z + NZ - 1) % NZ, self.xhi, self.core)

    def cross(self):
        return self.device(1 - self.xlo, self.z, 1 - self.xhi, self.core)

    def peer(self):
        return self.device(self.xlo, self.z, self.xhi, 1 - self.core)

    def plane(self, rel):
        return (self.z + rel + NZ) % NZ

    def column(self, col):
        return self.xhi if col == 0 else 1 - self.xhi

    def slot(self, rel, col, core=None):
        core = self.core if core is None else core
        return self.plane(rel) * 4 + self.column(col) * 2 + core


def rels(k):
    return (0,) if k == 0 else ((4,) if k == 4 else (-k, k))


def remote(src, dst, send, recv, device):
    return pltpu.make_async_remote_copy(
        src_ref=src, dst_ref=dst, send_sem=send, recv_sem=recv, device_id=device, device_id_type=MESH
    )


class Gather:
    def __init__(self, at, buf, zs, zr, cs, cr, ps, pr):
        self.at, self.buf = at, buf
        self.zs, self.zr, self.cs, self.cr, self.ps, self.pr = zs, zr, cs, cr, ps, pr
        self.sent = {k: [] for k in range(5)}

    def rows(self, rel, col, half, core=None):
        start = self.at.slot(rel, col, core) * TOK + half * HALF
        return self.buf.at[pl.ds(pl.multiple_of(start, HALF), HALF)]

    def go(self, k, copy):
        copy.start()
        self.sent[k].append(copy)

    def hop(self, stream, direction, k):
        col, half = STREAM[stream]
        if k > HOPS[stream][direction]:
            return
        rel = -(k - 1) if direction == 0 else k - 1
        ref = self.rows(rel, col, half)
        to = self.at.up() if direction == 0 else self.at.down()
        self.go(abs(rel), remote(ref, ref, self.zs.at[stream, direction, k], self.zr.at[stream, direction, k], to))

    def crossing(self, rel, half):
        ref = self.rows(rel, 0, half)
        index = rel % NZ if half == 1 else NZ
        return remote(ref, ref, self.cs.at[index], self.cr.at[index], self.at.cross())

    def crossed(self, rel, half):
        ref = self.rows(rel, 1, half)
        index = rel % NZ if half == 1 else NZ
        remote(ref, ref, self.cs.at[index], self.cr.at[index], self.at.cross()).wait_recv()

    def block(self, rel, col, core=None):
        return self.buf.at[pl.ds(pl.multiple_of(self.at.slot(rel, col, core) * TOK, TOK), TOK)]

    def share(self, rel, col):
        ref = self.block(rel, col)
        index = (rel % NZ) * 2 + col
        self.go(abs(rel), remote(ref, ref, self.ps.at[index], self.pr.at[index], self.at.peer()))

    def begin(self):
        self.go(0, self.crossing(0, 0))
        for stream in (B0, A0):
            for direction in (0, 1):
                self.hop(stream, direction, 1)
        self.go(0, self.crossing(0, 1))
        self.share(0, 0)

    def begin_column(self):
        self.crossed(0, 0)
        for direction in (0, 1):
            self.hop(A1, direction, 1)

    def ring(self, k):
        for stream in (B0, A0, A1):
            col, half = STREAM[stream]
            for direction in (0, 1):
                if k > HOPS[stream][direction]:
                    continue
                rel = -k if direction == 0 else k
                rel = 4 if k == 4 else rel
                ref = self.rows(rel, col, half)
                sem = self.zr.at[stream, direction, k]
                remote(ref, ref, self.zs.at[stream, direction, k], sem, self.at.up()).wait_recv()
                self.hop(stream, direction, k + 1)
                if stream == B0:
                    self.go(k, self.crossing(rel, 1))
                if stream == A0:
                    self.share(rel, 0)

    def column(self, k):
        for rel in rels(k):
            self.crossed(rel, 1)
            self.share(rel, 1)

    def shared(self, k):
        for rel in rels(k):
            for col in (0, 1):
                ref = self.block(rel, col, 1 - self.at.core)
                index = (rel % NZ) * 2 + col
                remote(ref, ref, self.ps.at[index], self.pr.at[index], self.at.peer()).wait_recv()

    def settle(self, k):
        for copy in self.sent[k]:
            copy.wait_send()


GATHER_SEMS = [
    pltpu.SemaphoreType.DMA((3, 2, 5)),
    pltpu.SemaphoreType.DMA((3, 2, 5)),
    pltpu.SemaphoreType.DMA((9,)),
    pltpu.SemaphoreType.DMA((9,)),
    pltpu.SemaphoreType.DMA((16,)),
    pltpu.SemaphoreType.DMA((16,)),
]


class Around:
    def __init__(self, at, ring, rest, ys, yr, ps, pr):
        self.at, self.ring, self.rest = at, ring, rest
        self.ys, self.yr, self.ps, self.pr = ys, yr, ps, pr
        self.sent = []

    def device(self, off):
        return {"ctx": self.at.xlo * 4 + (self.at.y + off) % 4, "exp": self.at.exp}

    def rows(self, rel, col, core=None):
        return pl.ds(pl.multiple_of(self.at.slot(rel, col, core) * TOK, TOK), TOK)

    def copy(self, src, rel, col, off, to):
        index = (rel % NZ) * 2 + col
        dst = self.rest.at[off - 1, self.rows(rel, col)]
        return remote(src, dst, self.ys.at[index, off], self.yr.at[index, off], self.device(to))

    def go(self, copy):
        copy.start()
        self.sent.append(copy)

    def give(self, rel, col):
        src = self.ring.at[self.rows(rel, col), pl.ds(DIRECT, QUARTER)]
        self.go(self.copy(src, rel, col, 1, 3))
        self.go(self.copy(src, rel, col, 3, 1))

    def arrived(self, rel, col, off):
        here = self.rest.at[off - 1, self.rows(rel, col)]
        self.copy(here, rel, col, off, 1).wait_recv()

    def forward(self, rel, col):
        self.arrived(rel, col, 1)
        self.arrived(rel, col, 3)
        off, to = (3, 1) if col == 0 else (1, 3)
        self.go(self.copy(self.rest.at[off - 1, self.rows(rel, col)], rel, col, 2, to))

    def share(self, rel, col):
        if (rel, col) != (0, 0):
            self.arrived(rel, col, 2)
        ref = self.rest.at[:, self.rows(rel, col)]
        index = (rel % NZ) * 2 + col
        self.go(remote(ref, ref, self.ps.at[index], self.pr.at[index], self.at.peer()))

    def shared(self, k):
        for rel in rels(k):
            for col in (0, 1):
                ref = self.rest.at[:, self.rows(rel, col, 1 - self.at.core)]
                index = (rel % NZ) * 2 + col
                remote(ref, ref, self.ps.at[index], self.pr.at[index], self.at.peer()).wait_recv()

    def settle(self):
        for copy in self.sent:
            copy.wait_send()


def attention_kernel(
    hidden_hbm, query_hbm, kv_hbm, proj_hbm, gain_ref, gates_ref,
    residual_ref, normed_ref, gates_out,
    ring, rest, heads, kvs, visible, mixed, total, hidden,
    zs, zr, cs, cr, ps, pr, ks, kr, gs, gr, ys, yr, yps, ypr, own_sem,
):
    at = Place()
    position = at.ctx
    place = pl.ds(pl.multiple_of(at.exp * TOK, TOK), TOK)
    loads = [
        (kv_hbm, kvs.at[pl.ds(pl.multiple_of(position * TOK, TOK), TOK)]),
        (proj_hbm.at[:, pl.ds(0, DIRECT)], ring.at[place, pl.ds(0, DIRECT)]),
    ]
    for off in range(4):
        columns = pl.ds(pl.multiple_of(DIRECT + (at.y + off) % 4 * QUARTER, QUARTER), QUARTER)
        to = ring.at[place, pl.ds(DIRECT, QUARTER)] if off == 0 else rest.at[off - 1, place]
        loads.append((proj_hbm.at[:, columns], to))
    for h in range(QH):
        loads.append((query_hbm.at[:, pl.ds(h * HD, HD)], heads.at[pl.ds(h * TOK, TOK)]))
    loads.append((hidden_hbm, hidden))
    loads = [pltpu.make_async_copy(src, dst, own_sem.at[i]) for i, (src, dst) in enumerate(loads)]
    for load in loads:
        load.start()

    def gate_target(off):
        other = (at.exp + off) % EXPERTS
        other_hi = (other // 2) % 2
        return other, {"ctx": ((at.xlo + at.xhi + other_hi) % 2) * 4 + at.y, "exp": other}

    barrier = pltpu.get_barrier_semaphore()

    def greet(off, carry):
        _, device = gate_target(off)
        pl.semaphore_signal(barrier, inc=1, device_id=device, device_id_type=MESH)
        return carry

    lax.fori_loop(1, EXPERTS, greet, 0)
    for off in range(1, NCTX):
        device = {"ctx": (position + off) % NCTX, "exp": at.exp}
        pl.semaphore_signal(barrier, inc=1, device_id=device, device_id_type=MESH)

    gates_out[pl.ds(at.exp, 1)] = gates_ref[pl.ds(at.exp, 1)]

    @pl.when(position % 2 == 0)
    def _():
        kvs[pl.ds(pl.multiple_of((position + 1) * TOK, TOK), TOK), :] = jnp.zeros((TOK, 2 * KVH * HD), BF)

    for load in loads[:6]:
        load.wait()
    pl.semaphore_wait(barrier, EXPERTS - 1 + NCTX - 1)

    gather = Gather(at, ring, zs, zr, cs, cr, ps, pr)
    around = Around(at, ring, rest, ys, yr, yps, ypr)
    gather.begin()

    mine = kvs.at[pl.ds(pl.multiple_of(position * TOK, TOK), TOK)]

    def kv_copy(off):
        device = {"ctx": (position + off) % NCTX, "exp": at.exp}
        return remote(mine, mine, ks.at[off], kr.at[off], device)

    for off in range(1, NCTX):
        pl.when(position + off < NCTX)(lambda off=off: kv_copy(off).start())

    def send_gates(off, carry):
        other, device = gate_target(off)
        remote(gates_ref.at[other], gates_out.at[at.exp], gs.at[off], gr.at[off], device).start()
        return carry

    lax.fori_loop(1, EXPERTS, send_gates, 0)
    gather.begin_column()
    around.share(0, 0)
    for load in loads[6:]:
        load.wait()

    def kv_arrived(off):
        ref = kvs.at[pl.ds(pl.multiple_of((position + NCTX - off) % NCTX * TOK, TOK), TOK)]
        remote(ref, ref, ks.at[off], kr.at[off], {"ctx": (position + off) % NCTX, "exp": at.exp}).wait_recv()

    scale = HD ** (-0.5) * math.log2(math.e)
    last = position // 2
    row_pos = position * TOK + lax.broadcasted_iota(jnp.int32, (2 * TOK, 2 * TOK), 0) % TOK
    key_pos = last * 2 * TOK + lax.broadcasted_iota(jnp.int32, (2 * TOK, 2 * TOK), 1)
    visible[...] = jnp.where(row_pos >= key_pos, 0.0, 1.0)

    def attend(pairs, chunk, carry):
        lane = pl.multiple_of((chunk // 8) * HD, HD)
        q = heads[pl.ds(pl.multiple_of(chunk * 2 * TOK, 2 * TOK), 2 * TOK), :]
        parts, running = [], None
        for pair in range(pairs):
            keys = kvs[pair * 2 * TOK : (pair + 1) * 2 * TOK, pl.ds(lane, HD)]
            s = lax.dot_general(q, keys, (((1,), (1,)), ((), ())), preferred_element_type=F32)
            if pair == pairs - 1:
                s = jnp.where(visible[...] == 0.0, s, -1e30)
            parts.append(s)
            top = jnp.maximum(s[:, :TOK], s[:, TOK:])
            running = top if running is None else jnp.maximum(running, top)
        row_max = jnp.max(running, axis=1, keepdims=True)
        row_sum, acc = None, None
        for pair in range(pairs):
            weight = jnp.exp2((parts[pair] - row_max) * scale)
            values = kvs[pair * 2 * TOK : (pair + 1) * 2 * TOK, pl.ds(pl.multiple_of(lane + KVH * HD, HD), HD)]
            part = jnp.dot(weight.astype(BF), values, preferred_element_type=F32)
            both = weight[:, :TOK] + weight[:, TOK:]
            acc = part if acc is None else acc + part
            row_sum = both if row_sum is None else row_sum + both
        out = (acc / jnp.sum(row_sum, axis=1, keepdims=True)).astype(BF)
        plane, side = chunk // 2, chunk % 2
        for i in range(2):
            columns = pl.ds(pl.multiple_of((side * 2 + i) * HD, HD), HD)
            mixed[plane, :, columns] = out[i * TOK : (i + 1) * TOK]
        return carry

    def some(pairs, first, end):
        lax.fori_loop(first, end, functools.partial(attend, pairs), 0)

    def attend_some(first, end):
        for pairs in range(1, NCTX // 2 + 1):
            pl.when(last == pairs - 1)(
                lambda pairs=pairs: some(pairs, first, end)
            )

    def give(k, col):
        for rel in rels(k):
            around.give(rel, col)

    def forward(k, col):
        for rel in rels(k):
            around.forward(rel, col)

    def share(k):
        for rel in rels(k):
            for col in (0, 1):
                if (rel, col) != (0, 0):
                    around.share(rel, col)

    def project(k):
        gather.shared(k)
        around.shared(k)
        for rel in rels(k):
            plane = at.plane(rel)
            rows = pl.ds(pl.multiple_of(plane * 4 * TOK, 4 * TOK), 4 * TOK)

            def tile(n, carry):
                columns = pl.ds(pl.multiple_of(n * 512, 512), 512)
                total[:, columns] += jnp.dot(mixed[plane], ring[rows, columns], preferred_element_type=F32)
                return carry

            lax.fori_loop(0, DIRECT // 512, tile, 0)
            for off in range(4):
                part = ring[rows, DIRECT:] if off == 0 else rest[off - 1, rows, :]
                columns = pl.ds(pl.multiple_of(DIRECT + (at.y + off) % 4 * QUARTER, QUARTER), QUARTER)
                total[:, columns] += jnp.dot(mixed[plane], part, preferred_element_type=F32)

    gather.column(0)
    give(0, 1)
    gather.ring(1)
    give(1, 0)
    for off in range(1, NCTX):
        pl.when(position - off >= 0)(lambda off=off: kv_arrived(off))

    attend_some(0, 5)
    gather.column(1)
    give(1, 1)
    forward(0, 1)
    gather.ring(2)
    give(2, 0)
    forward(1, 0)
    attend_some(5, 10)
    gather.column(2)
    give(2, 1)
    forward(1, 1)
    share(0)
    gather.ring(3)
    give(3, 0)
    forward(2, 0)
    share(1)
    attend_some(10, 16)
    total[...] = hidden[...].astype(F32)
    project(0)
    gather.column(3)
    give(3, 1)
    forward(2, 1)
    project(1)
    gather.ring(4)
    give(4, 0)
    forward(3, 0)
    share(2)
    gather.column(4)
    give(4, 1)
    forward(3, 1)
    project(2)
    forward(4, 0)
    share(3)
    forward(4, 1)
    project(3)
    share(4)
    project(4)

    def norm(i, carry):
        rows = pl.ds(pl.multiple_of(i * 16, 16), 16)
        r = total[rows, :]
        inverse = lax.rsqrt(jnp.mean(r * r, axis=-1, keepdims=True) + 1e-06)
        normed_ref[rows, :] = (r * inverse * gain_ref[...].astype(F32)).astype(BF)
        residual_ref[rows, :] = r
        return carry

    lax.fori_loop(0, TOK // 16, norm, 0)

    def take_gates(off, carry):
        other, device = gate_target(off)
        origin = (at.exp + EXPERTS - off) % EXPERTS
        copy = remote(gates_ref.at[other], gates_out.at[origin], gs.at[off], gr.at[off], device)
        copy.wait_send()
        copy.wait_recv()
        return carry

    lax.fori_loop(1, EXPERTS, take_gates, 0)
    for off in range(1, NCTX):
        pl.when(position + off < NCTX)(lambda off=off: kv_copy(off).wait_send())
    around.settle()
    for k in range(5):
        gather.settle(k)


def expert_kernel(
    normed_hbm, residual_hbm, gates_ref, gate_hbm, up_hbm, down_hbm,
    out_ref,
    buf, peer_part, ring_part, cross_part, wg, wu, wd, picked, act, residual_ref,
    zs, zr, cs, cr, ps, pr, rzs, rzr, rcs, rcr, rps, rpr, wsem,
):
    at = Place()
    place = buf.at[pl.ds(pl.multiple_of(at.exp * TOK, TOK), TOK)]
    loads = (
        (normed_hbm, place), (gate_hbm, wg), (up_hbm, wu), (down_hbm, wd), (residual_hbm, residual_ref)
    )
    loads = [pltpu.make_async_copy(src, dst, wsem.at[i]) for i, (src, dst) in enumerate(loads)]
    for load in loads:
        load.start()
    barrier = pltpu.get_barrier_semaphore()
    for device in (at.up(), at.down(), at.cross(), at.peer()):
        pl.semaphore_signal(barrier, inc=1, device_id=device, device_id_type=MESH)
    loads[0].wait()
    pl.semaphore_wait(barrier, 4)

    gather = Gather(at, buf, zs, zr, cs, cr, ps, pr)
    gather.begin()
    gather.begin_column()

    before = (
        lax.broadcasted_iota(jnp.int32, (TOK, TOK), 0) < lax.broadcasted_iota(jnp.int32, (TOK, TOK), 1)
    ).astype(BF)

    def selection(rel):
        places, gates = [], []
        for s in range(4):
            g = gates_ref[at.plane(rel) * 4 + s]
            named = g > 0.0
            rank = jnp.dot(named.astype(BF), before, preferred_element_type=F32)
            places.append(jnp.where(named, rank + s * CAP, -1.0))
            gates.append(g)
        place = jnp.concatenate(places, axis=1)[0:1]
        gate = jnp.concatenate(gates, axis=1)[0:1]
        number = lax.broadcasted_iota(jnp.int32, (ROWS, 4 * TOK), 0).astype(F32)
        hit = number == place
        gate_rows = jnp.sum(jnp.where(hit, gate, 0.0), axis=1, keepdims=True)
        return hit.astype(BF), gate_rows

    def plane_rows(rel):
        return pl.ds(pl.multiple_of(at.plane(rel) * 512, 512), 512)

    def process(k):
        these = rels(k)
        count = len(these) * ROWS
        chosen = [selection(rel) for rel in these]

        for i, rel in enumerate(these):
            def pick(n, carry):
                columns = pl.ds(pl.multiple_of(n * 512, 512), 512)
                picked[i * ROWS : (i + 1) * ROWS, columns] = jnp.dot(
                    chosen[i][0], buf[plane_rows(rel), columns], preferred_element_type=F32
                ).astype(BF)
                return carry

            lax.fori_loop(0, 4, pick, 0)

        def hidden(n, carry):
            columns = pl.ds(pl.multiple_of(n * 256, 256), 256)
            x = picked[:count, :]
            g = jnp.dot(x, wg[:, columns], preferred_element_type=F32)
            u = jnp.dot(x, wu[:, columns], preferred_element_type=F32)
            act[:count, columns] = (g / (1.0 + jnp.exp(-g)) * u).astype(BF)
            return carry

        lax.fori_loop(0, EF // 256, hidden, 0)
        gate_rows = [c[1] for c in chosen]
        gate_all = gate_rows[0] if len(these) == 1 else jnp.concatenate(gate_rows, axis=0)

        def spread(n, carry):
            columns = pl.ds(pl.multiple_of(n * 512, 512), 512)
            o = jnp.dot(act[:count, :], wd[:, columns], preferred_element_type=F32)
            o = (o * gate_all).astype(BF)
            for i, rel in enumerate(these):
                buf[plane_rows(rel), columns] = lax.dot_general(
                    chosen[i][0], o[i * ROWS : (i + 1) * ROWS], (((0,), (0,)), ((), ())),
                    preferred_element_type=F32,
                ).astype(BF)
            return carry

        lax.fori_loop(0, 4, spread, 0)
        for rel in these:
            for col in (0, 1):
                give_peer(rel, col)

    peer_sent = []

    def peer_copy(rel, col):
        src = buf.at[pl.ds(pl.multiple_of(at.slot(rel, col, 1 - at.core) * TOK, TOK), TOK)]
        dst = peer_part.at[pl.ds(pl.multiple_of((at.plane(rel) * 2 + at.column(col)) * TOK, TOK), TOK)]
        index = (rel % NZ) * 2 + col
        return remote(src, dst, rps.at[index], rpr.at[index], at.peer())

    def give_peer(rel, col):
        copy = peer_copy(rel, col)
        copy.start()
        peer_sent.append(copy)

    for k in range(5):
        if k >= 1:
            gather.column(k)
        else:
            gather.column(0)
        if k + 1 in (1, 2, 3, 4):
            gather.ring(k + 1)
        if k == 0:
            for load in loads[1:]:
                load.wait()
        gather.shared(k)
        gather.settle(k)
        process(k)

    back_sent = []

    def mine(rel, col, half):
        return buf.at[pl.ds(pl.multiple_of(at.slot(rel, col) * TOK + half * HALF, HALF), HALF)]

    def from_peer(rel, col, half):
        start = (at.plane(rel) * 2 + at.column(col)) * TOK + half * HALF
        return peer_part.at[pl.ds(pl.multiple_of(start, HALF), HALF)]

    def take_peer(rel):
        for col in (0, 1):
            peer_copy(rel, col).wait_recv()

    def add(target, others):
        def chunk(i, carry):
            rows = pl.ds(pl.multiple_of(i * 16, 16), 16)
            value = target[rows, :].astype(F32)
            for other in others:
                value = value + other[rows, :].astype(F32)
            target[rows, :] = value.astype(BF)
            return carry

        lax.fori_loop(0, HALF // 16, chunk, 0)

    def send_back(copy):
        copy.start()
        back_sent.append(copy)

    def give_cross(rel, half):
        index = rel % NZ if half == 1 else NZ
        send_back(remote(mine(rel, 1, half), cross_part.at[index], rcs.at[index], rcr.at[index], at.cross()))

    def take_cross(rel, half):
        index = rel % NZ if half == 1 else NZ
        part = cross_part.at[index]
        remote(part, part, rcs.at[index], rcr.at[index], at.cross()).wait_recv()
        return part

    def cross_half(rel):
        add(mine(rel, 1, 1), [from_peer(rel, 1, 1)])
        give_cross(rel, 1)

    def ring_slot(stream, direction, k):
        return ring_part.at[(stream * 2 + direction) * 4 + k]

    def take_ring(stream, direction, k):
        part = ring_slot(stream, direction, k)
        remote(
            part, part, rzs.at[stream, direction, k], rzr.at[stream, direction, k], at.up()
        ).wait_recv()
        return part

    def give_ring(stream, direction, k):
        col, half = STREAM[stream]
        if k > HOPS[stream][direction]:
            return
        rel = 4 if k == 4 else (-k if direction == 0 else k)
        others = [from_peer(rel, col, half)]
        if stream == B0:
            others.append(take_cross(rel, 1))
        if k + 1 <= HOPS[stream][direction]:
            others.append(take_ring(stream, direction, k))
        add(mine(rel, col, half), others)
        to = at.down() if direction == 0 else at.up()
        send_back(
            remote(
                mine(rel, col, half),
                ring_slot(stream, direction, k - 1),
                rzs.at[stream, direction, k - 1],
                rzr.at[stream, direction, k - 1],
                to,
            )
        )

    for rel in rels(4):
        take_peer(rel)
        cross_half(rel)
    for k in (4, 3, 2, 1):
        for direction in (0, 1):
            for stream in (A1, A0):
                give_ring(stream, direction, k)
        for rel in rels(k - 1):
            take_peer(rel)
            cross_half(rel)
        for direction in (0, 1):
            give_ring(B0, direction, k)
    add(
        mine(0, 1, 0),
        [from_peer(0, 1, 0), take_ring(A1, 0, 0), take_ring(A1, 1, 0)],
    )
    give_cross(0, 0)

    def finish(half, others):
        def chunk(i, carry):
            rows = pl.ds(pl.multiple_of(i * 16, 16), 16)
            value = mine(0, 0, half)[rows, :].astype(F32)
            for other in others:
                value = value + other[rows, :].astype(F32)
            place = pl.ds(pl.multiple_of(half * HALF + i * 16, 16), 16)
            out_ref[place, :] = (residual_ref[place, :] + value).astype(BF)
            return carry

        lax.fori_loop(0, HALF // 16, chunk, 0)

    finish(1, [from_peer(0, 0, 1), take_cross(0, 1), take_ring(B0, 0, 0), take_ring(B0, 1, 0)])
    finish(0, [from_peer(0, 0, 0), take_ring(A0, 0, 0), take_ring(A0, 1, 0), take_cross(0, 0)])
    for copy in peer_sent + back_sent:
        copy.wait_send()


VMEM = pl.BlockSpec(memory_space=pltpu.VMEM)
ANY = pl.BlockSpec(memory_space=pl.ANY)


def body(
    hidden_in, query, keyval, out_proj, norm_gain, expert_ids, gate_weights, w_gate, w_up, w_down
):
    names = jnp.arange(EXPERTS, dtype=jnp.int32)[:, None, None]
    gates = jnp.sum(
        jnp.where(expert_ids[0].T[None] == names, gate_weights[0].T[None], 0.0), axis=1
    )
    gates = jnp.broadcast_to(gates[:, None, :], (EXPERTS, 8, TOK))

    residual, normed, routed = pl.pallas_call(
        attention_kernel,
        out_shape=(
            jax.ShapeDtypeStruct((TOK, D), F32),
            jax.ShapeDtypeStruct((TOK, D), BF),
            jax.ShapeDtypeStruct((EXPERTS, 8, TOK), F32),
        ),
        in_specs=[ANY, ANY, ANY, ANY, VMEM, VMEM],
        out_specs=(VMEM, VMEM, VMEM),
        scratch_shapes=[
            pltpu.VMEM((QH * HD, DIRECT + QUARTER), BF),
            pltpu.VMEM((3, QH * HD, QUARTER), BF),
            pltpu.VMEM((QH * TOK, HD), BF),
            pltpu.VMEM((NCTX * TOK, 2 * KVH * HD), BF),
            pltpu.VMEM((2 * TOK, 2 * TOK), F32),
            pltpu.VMEM((NZ, TOK, 4 * HD), BF),
            pltpu.VMEM((TOK, D), F32),
            pltpu.VMEM((TOK, D), BF),
            *GATHER_SEMS,
            pltpu.SemaphoreType.DMA((NCTX,)),
            pltpu.SemaphoreType.DMA((NCTX,)),
            pltpu.SemaphoreType.DMA((EXPERTS,)),
            pltpu.SemaphoreType.DMA((EXPERTS,)),
            pltpu.SemaphoreType.DMA((16, 4)),
            pltpu.SemaphoreType.DMA((16, 4)),
            pltpu.SemaphoreType.DMA((16,)),
            pltpu.SemaphoreType.DMA((16,)),
            pltpu.SemaphoreType.DMA((QH + 7,)),
        ],
        compiler_params=pltpu.CompilerParams(
            collective_id=0, has_side_effects=True, vmem_limit_bytes=48 << 20
        ),
        name="attend_project",
    )(hidden_in[0], query[0], keyval[0], out_proj, norm_gain.reshape(1, D), gates)

    result = pl.pallas_call(
        expert_kernel,
        out_shape=jax.ShapeDtypeStruct((TOK, D), BF),
        in_specs=[ANY, ANY, VMEM, ANY, ANY, ANY],
        out_specs=VMEM,
        scratch_shapes=[
            pltpu.VMEM((EXPERTS * TOK, D), BF),
            pltpu.VMEM((EXPERTS * TOK // 2, D), BF),
            pltpu.VMEM((24, HALF, D), BF),
            pltpu.VMEM((9, HALF, D), BF),
            pltpu.VMEM((D, EF), BF),
            pltpu.VMEM((D, EF), BF),
            pltpu.VMEM((EF, D), BF),
            pltpu.VMEM((2 * ROWS, D), BF),
            pltpu.VMEM((2 * ROWS, EF), BF),
            pltpu.VMEM((TOK, D), F32),
            *GATHER_SEMS,
            pltpu.SemaphoreType.DMA((3, 2, 4)),
            pltpu.SemaphoreType.DMA((3, 2, 4)),
            pltpu.SemaphoreType.DMA((9,)),
            pltpu.SemaphoreType.DMA((9,)),
            pltpu.SemaphoreType.DMA((16,)),
            pltpu.SemaphoreType.DMA((16,)),
            pltpu.SemaphoreType.DMA((5,)),
        ],
        compiler_params=pltpu.CompilerParams(
            collective_id=1, has_side_effects=True, vmem_limit_bytes=58 << 20
        ),
        name="experts",
    )(normed, residual, routed, w_gate[0], w_up[0], w_down[0])
    return result[None]


def solution(mesh):
    in_specs = (
        P("exp", "ctx", None),
        P("exp", "ctx", None),
        P("exp", "ctx", None),
        P("exp", None),
        P(),
        P("exp", "ctx", None),
        P("exp", "ctx", None),
        P("exp", None, None),
        P("exp", None, None),
        P("exp", None, None),
    )
    out_specs = P("exp", "ctx", None)
    return jax.shard_map(body, mesh=mesh, in_specs=in_specs, out_specs=out_specs, check_vma=False)
```

```python
import functools
import math

import jax
import jax.numpy as jnp
from jax import lax
from jax.experimental import pallas as pl
from jax.experimental.pallas import tpu as pltpu
from jax.sharding import PartitionSpec as P

D = 2048
QH = 32
KVH = 2
HD = 128
EF = 768
TOP = 8
TOK = 128
EXPERTS = 32
CAP = 34
ROWS = 144
HALF = 64
DIRECT = 1024
QUARTER = 256
NZ = 8
NCTX = 8
MESH = pl.DeviceIdType.MESH
BF = jnp.bfloat16
F32 = jnp.float32

A0, A1, B0 = 0, 1, 2
STREAM = ((0, 0), (1, 0), (0, 1))
HOPS = ((4, 3), (3, 4), (4, 3))


class Place:
    def __init__(self):
        ctx, exp = lax.axis_index("ctx"), lax.axis_index("exp")
        self.ctx, self.exp = ctx, exp
        self.xlo, self.y = ctx // 4, ctx % 4
        self.z, self.xhi, self.core = exp // 4, (exp // 2) % 2, exp % 2

    def device(self, xlo, z, xhi, core):
        return {"ctx": xlo * 4 + self.y, "exp": z * 4 + xhi * 2 + core}

    def up(self):
        return self.device(self.xlo, (self.z + 1) % NZ, self.xhi, self.core)

    def down(self):
        return self.device(self.xlo, (self.z + NZ - 1) % NZ, self.xhi, self.core)

    def cross(self):
        return self.device(1 - self.xlo, self.z, 1 - self.xhi, self.core)

    def peer(self):
        return self.device(self.xlo, self.z, self.xhi, 1 - self.core)

    def plane(self, rel):
        return (self.z + rel + NZ) % NZ

    def column(self, col):
        return self.xhi if col == 0 else 1 - self.xhi

    def slot(self, rel, col, core=None):
        core = self.core if core is None else core
        return self.plane(rel) * 4 + self.column(col) * 2 + core


def rels(k):
    return (0,) if k == 0 else ((4,) if k == 4 else (-k, k))


def remote(src, dst, send, recv, device):
    return pltpu.make_async_remote_copy(
        src_ref=src, dst_ref=dst, send_sem=send, recv_sem=recv, device_id=device, device_id_type=MESH
    )


class Gather:
    def __init__(self, at, buf, zs, zr, cs, cr, ps, pr):
        self.at, self.buf = at, buf
        self.zs, self.zr, self.cs, self.cr, self.ps, self.pr = zs, zr, cs, cr, ps, pr
        self.sent = {k: [] for k in range(5)}

    def rows(self, rel, col, half, core=None):
        start = self.at.slot(rel, col, core) * TOK + half * HALF
        return self.buf.at[pl.ds(pl.multiple_of(start, HALF), HALF)]

    def go(self, k, copy):
        copy.start()
        self.sent[k].append(copy)

    def hop(self, stream, direction, k):
        col, half = STREAM[stream]
        if k > HOPS[stream][direction]:
            return
        rel = -(k - 1) if direction == 0 else k - 1
        ref = self.rows(rel, col, half)
        to = self.at.up() if direction == 0 else self.at.down()
        self.go(abs(rel), remote(ref, ref, self.zs.at[stream, direction, k], self.zr.at[stream, direction, k], to))

    def crossing(self, rel, half):
        ref = self.rows(rel, 0, half)
        index = rel % NZ if half == 1 else NZ
        return remote(ref, ref, self.cs.at[index], self.cr.at[index], self.at.cross())

    def crossed(self, rel, half):
        ref = self.rows(rel, 1, half)
        index = rel % NZ if half == 1 else NZ
        remote(ref, ref, self.cs.at[index], self.cr.at[index], self.at.cross()).wait_recv()

    def block(self, rel, col, core=None):
        return self.buf.at[pl.ds(pl.multiple_of(self.at.slot(rel, col, core) * TOK, TOK), TOK)]

    def share(self, rel, col):
        ref = self.block(rel, col)
        index = (rel % NZ) * 2 + col
        self.go(abs(rel), remote(ref, ref, self.ps.at[index], self.pr.at[index], self.at.peer()))

    def begin(self):
        self.go(0, self.crossing(0, 0))
        for stream in (B0, A0):
            for direction in (0, 1):
                self.hop(stream, direction, 1)
        self.go(0, self.crossing(0, 1))
        self.share(0, 0)

    def begin_column(self):
        self.crossed(0, 0)
        for direction in (0, 1):
            self.hop(A1, direction, 1)

    def ring(self, k):
        for stream in (B0, A0, A1):
            col, half = STREAM[stream]
            for direction in (0, 1):
                if k > HOPS[stream][direction]:
                    continue
                rel = -k if direction == 0 else k
                rel = 4 if k == 4 else rel
                ref = self.rows(rel, col, half)
                sem = self.zr.at[stream, direction, k]
                remote(ref, ref, self.zs.at[stream, direction, k], sem, self.at.up()).wait_recv()
                self.hop(stream, direction, k + 1)
                if stream == B0:
                    self.go(k, self.crossing(rel, 1))
                if stream == A0:
                    self.share(rel, 0)

    def column(self, k):
        for rel in rels(k):
            self.crossed(rel, 1)
            self.share(rel, 1)

    def shared(self, k):
        for rel in rels(k):
            for col in (0, 1):
                ref = self.block(rel, col, 1 - self.at.core)
                index = (rel % NZ) * 2 + col
                remote(ref, ref, self.ps.at[index], self.pr.at[index], self.at.peer()).wait_recv()

    def settle(self, k):
        for copy in self.sent[k]:
            copy.wait_send()


GATHER_SEMS = [
    pltpu.SemaphoreType.DMA((3, 2, 5)),
    pltpu.SemaphoreType.DMA((3, 2, 5)),
    pltpu.SemaphoreType.DMA((9,)),
    pltpu.SemaphoreType.DMA((9,)),
    pltpu.SemaphoreType.DMA((16,)),
    pltpu.SemaphoreType.DMA((16,)),
]


class Around:
    def __init__(self, at, ring, rest, ys, yr, ps, pr):
        self.at, self.ring, self.rest = at, ring, rest
        self.ys, self.yr, self.ps, self.pr = ys, yr, ps, pr
        self.sent = []

    def device(self, off):
        return {"ctx": self.at.xlo * 4 + (self.at.y + off) % 4, "exp": self.at.exp}

    def rows(self, rel, col, core=None):
        return pl.ds(pl.multiple_of(self.at.slot(rel, col, core) * TOK, TOK), TOK)

    def copy(self, src, rel, col, off, to):
        index = (rel % NZ) * 2 + col
        dst = self.rest.at[off - 1, self.rows(rel, col)]
        return remote(src, dst, self.ys.at[index, off], self.yr.at[index, off], self.device(to))

    def go(self, copy):
        copy.start()
        self.sent.append(copy)

    def give(self, rel, col):
        src = self.ring.at[self.rows(rel, col), pl.ds(DIRECT, QUARTER)]
        self.go(self.copy(src, rel, col, 1, 3))
        self.go(self.copy(src, rel, col, 3, 1))

    def arrived(self, rel, col, off):
        here = self.rest.at[off - 1, self.rows(rel, col)]
        self.copy(here, rel, col, off, 1).wait_recv()

    def forward(self, rel, col):
        self.arrived(rel, col, 1)
        self.arrived(rel, col, 3)
        off, to = (3, 1) if col == 0 else (1, 3)
        self.go(self.copy(self.rest.at[off - 1, self.rows(rel, col)], rel, col, 2, to))

    def share(self, rel, col):
        if (rel, col) != (0, 0):
            self.arrived(rel, col, 2)
        ref = self.rest.at[:, self.rows(rel, col)]
        index = (rel % NZ) * 2 + col
        self.go(remote(ref, ref, self.ps.at[index], self.pr.at[index], self.at.peer()))

    def shared(self, k):
        for rel in rels(k):
            for col in (0, 1):
                ref = self.rest.at[:, self.rows(rel, col, 1 - self.at.core)]
                index = (rel % NZ) * 2 + col
                remote(ref, ref, self.ps.at[index], self.pr.at[index], self.at.peer()).wait_recv()

    def settle(self):
        for copy in self.sent:
            copy.wait_send()


def attention_kernel(
    hidden_hbm, query_hbm, kv_hbm, proj_hbm, gain_ref, gates_ref,
    residual_ref, normed_ref, gates_out, cross_gates_out,
    ring, rest, heads, kvs, visible, mixed, total, hidden,
    zs, zr, cs, cr, ps, pr, ks, kr, gs, gr, ys, yr, yps, ypr, g2s, g2r, own_sem,
):
    at = Place()
    position = at.ctx
    place = pl.ds(pl.multiple_of(at.exp * TOK, TOK), TOK)
    loads = [
        (kv_hbm, kvs.at[pl.ds(pl.multiple_of(position * TOK, TOK), TOK)]),
        (proj_hbm.at[:, pl.ds(0, DIRECT)], ring.at[place, pl.ds(0, DIRECT)]),
    ]
    for off in range(4):
        columns = pl.ds(pl.multiple_of(DIRECT + (at.y + off) % 4 * QUARTER, QUARTER), QUARTER)
        to = ring.at[place, pl.ds(DIRECT, QUARTER)] if off == 0 else rest.at[off - 1, place]
        loads.append((proj_hbm.at[:, columns], to))
    for h in range(QH):
        loads.append((query_hbm.at[:, pl.ds(h * HD, HD)], heads.at[pl.ds(h * TOK, TOK)]))
    loads.append((hidden_hbm, hidden))
    loads = [pltpu.make_async_copy(src, dst, own_sem.at[i]) for i, (src, dst) in enumerate(loads)]
    for load in loads:
        load.start()

    def gate_target(off):
        other = (at.exp + off) % EXPERTS
        other_hi = (other // 2) % 2
        return other, {"ctx": ((at.xlo + at.xhi + other_hi) % 2) * 4 + at.y, "exp": other}

    barrier = pltpu.get_barrier_semaphore()

    def greet(off, carry):
        _, device = gate_target(off)
        pl.semaphore_signal(barrier, inc=1, device_id=device, device_id_type=MESH)
        return carry

    lax.fori_loop(1, EXPERTS, greet, 0)
    for off in range(1, NCTX):
        device = {"ctx": (position + off) % NCTX, "exp": at.exp}
        pl.semaphore_signal(barrier, inc=1, device_id=device, device_id_type=MESH)

    gates_out[pl.ds(at.exp, 1)] = gates_ref[pl.ds(at.exp, 1)]

    def partner_gates(off):
        plane = (at.z + off) % NZ
        src = gates_ref.at[pl.ds(plane * 4 + (1 - at.xhi) * 2, 2)]
        to = at.device(at.xlo, plane, at.xhi, at.core)
        return remote(src, cross_gates_out.at[at.z], g2s.at[off], g2r.at[off], to)

    cross_gates_out[pl.ds(at.z, 1)] = gates_ref[pl.ds(at.z * 4 + (1 - at.xhi) * 2, 2)][None]

    @pl.when(position % 2 == 0)
    def _():
        kvs[pl.ds(pl.multiple_of((position + 1) * TOK, TOK), TOK), :] = jnp.zeros((TOK, 2 * KVH * HD), BF)

    for load in loads[:6]:
        load.wait()
    pl.semaphore_wait(barrier, EXPERTS - 1 + NCTX - 1)

    gather = Gather(at, ring, zs, zr, cs, cr, ps, pr)
    around = Around(at, ring, rest, ys, yr, yps, ypr)
    gather.begin()

    mine = kvs.at[pl.ds(pl.multiple_of(position * TOK, TOK), TOK)]

    def kv_copy(off):
        device = {"ctx": (position + off) % NCTX, "exp": at.exp}
        return remote(mine, mine, ks.at[off], kr.at[off], device)

    for off in range(1, NCTX):
        pl.when(position + off < NCTX)(lambda off=off: kv_copy(off).start())

    def send_gates(off, carry):
        other, device = gate_target(off)
        remote(gates_ref.at[other], gates_out.at[at.exp], gs.at[off], gr.at[off], device).start()
        return carry

    lax.fori_loop(1, EXPERTS, send_gates, 0)
    for off in range(1, NZ):
        partner_gates(off).start()
    gather.begin_column()
    around.share(0, 0)
    for load in loads[6:]:
        load.wait()

    def kv_arrived(off):
        ref = kvs.at[pl.ds(pl.multiple_of((position + NCTX - off) % NCTX * TOK, TOK), TOK)]
        remote(ref, ref, ks.at[off], kr.at[off], {"ctx": (position + off) % NCTX, "exp": at.exp}).wait_recv()

    scale = HD ** (-0.5) * math.log2(math.e)
    last = position // 2
    row_pos = position * TOK + lax.broadcasted_iota(jnp.int32, (2 * TOK, 2 * TOK), 0) % TOK
    key_pos = last * 2 * TOK + lax.broadcasted_iota(jnp.int32, (2 * TOK, 2 * TOK), 1)
    visible[...] = jnp.where(row_pos >= key_pos, 0.0, 1.0)

    def attend(pairs, chunk, carry):
        lane = pl.multiple_of((chunk // 8) * HD, HD)
        q = heads[pl.ds(pl.multiple_of(chunk * 2 * TOK, 2 * TOK), 2 * TOK), :]
        parts, running = [], None
        for pair in range(pairs):
            keys = kvs[pair * 2 * TOK : (pair + 1) * 2 * TOK, pl.ds(lane, HD)]
            s = lax.dot_general(q, keys, (((1,), (1,)), ((), ())), preferred_element_type=F32)
            if pair == pairs - 1:
                s = jnp.where(visible[...] == 0.0, s, -1e30)
            parts.append(s)
            top = jnp.maximum(s[:, :TOK], s[:, TOK:])
            running = top if running is None else jnp.maximum(running, top)
        row_max = jnp.max(running, axis=1, keepdims=True)
        row_sum, acc = None, None
        for pair in range(pairs):
            weight = jnp.exp2((parts[pair] - row_max) * scale)
            values = kvs[pair * 2 * TOK : (pair + 1) * 2 * TOK, pl.ds(pl.multiple_of(lane + KVH * HD, HD), HD)]
            part = jnp.dot(weight.astype(BF), values, preferred_element_type=F32)
            both = weight[:, :TOK] + weight[:, TOK:]
            acc = part if acc is None else acc + part
            row_sum = both if row_sum is None else row_sum + both
        out = (acc / jnp.sum(row_sum, axis=1, keepdims=True)).astype(BF)
        plane, side = chunk // 2, chunk % 2
        for i in range(2):
            columns = pl.ds(pl.multiple_of((side * 2 + i) * HD, HD), HD)
            mixed[plane, :, columns] = out[i * TOK : (i + 1) * TOK]
        return carry

    def some(pairs, first, end):
        lax.fori_loop(first, end, functools.partial(attend, pairs), 0)

    def attend_some(first, end):
        for pairs in range(1, NCTX // 2 + 1):
            pl.when(last == pairs - 1)(
                lambda pairs=pairs: some(pairs, first, end)
            )

    def give(k, col):
        for rel in rels(k):
            around.give(rel, col)

    def forward(k, col):
        for rel in rels(k):
            around.forward(rel, col)

    def share(k):
        for rel in rels(k):
            for col in (0, 1):
                if (rel, col) != (0, 0):
                    around.share(rel, col)

    def project(k):
        gather.shared(k)
        around.shared(k)
        for rel in rels(k):
            plane = at.plane(rel)
            rows = pl.ds(pl.multiple_of(plane * 4 * TOK, 4 * TOK), 4 * TOK)

            def tile(n, carry):
                columns = pl.ds(pl.multiple_of(n * 512, 512), 512)
                total[:, columns] += jnp.dot(mixed[plane], ring[rows, columns], preferred_element_type=F32)
                return carry

            lax.fori_loop(0, DIRECT // 512, tile, 0, unroll=True)
            for off in range(4):
                part = ring[rows, DIRECT:] if off == 0 else rest[off - 1, rows, :]
                columns = pl.ds(pl.multiple_of(DIRECT + (at.y + off) % 4 * QUARTER, QUARTER), QUARTER)
                total[:, columns] += jnp.dot(mixed[plane], part, preferred_element_type=F32)

    gather.column(0)
    give(0, 1)
    gather.ring(1)
    give(1, 0)
    for off in range(1, NCTX):
        pl.when(position - off >= 0)(lambda off=off: kv_arrived(off))

    attend_some(0, 5)
    gather.column(1)
    give(1, 1)
    forward(0, 1)
    gather.ring(2)
    give(2, 0)
    forward(1, 0)
    attend_some(5, 10)
    gather.column(2)
    give(2, 1)
    forward(1, 1)
    share(0)
    gather.ring(3)
    give(3, 0)
    forward(2, 0)
    share(1)
    attend_some(10, 16)
    total[...] = hidden[...].astype(F32)
    project(0)
    gather.column(3)
    give(3, 1)
    forward(2, 1)
    project(1)
    gather.ring(4)
    give(4, 0)
    forward(3, 0)
    share(2)
    gather.column(4)
    give(4, 1)
    forward(3, 1)
    project(2)
    forward(4, 0)
    share(3)
    forward(4, 1)
    project(3)
    share(4)
    project(4)

    def norm(i, carry):
        rows = pl.ds(pl.multiple_of(i * 16, 16), 16)
        r = total[rows, :]
        inverse = lax.rsqrt(jnp.mean(r * r, axis=-1, keepdims=True) + 1e-06)
        normed_ref[rows, :] = (r * inverse * gain_ref[...].astype(F32)).astype(BF)
        residual_ref[rows, :] = r
        return carry

    lax.fori_loop(0, TOK // 16, norm, 0, unroll=4)

    def take_gates(off, carry):
        other, device = gate_target(off)
        origin = (at.exp + EXPERTS - off) % EXPERTS
        copy = remote(gates_ref.at[other], gates_out.at[origin], gs.at[off], gr.at[off], device)
        copy.wait_send()
        copy.wait_recv()
        return carry

    lax.fori_loop(1, EXPERTS, take_gates, 0)
    for off in range(1, NZ):
        ref = cross_gates_out.at[(at.z + NZ - off) % NZ]
        remote(ref, ref, g2s.at[off], g2r.at[off], at.up()).wait_recv()
        partner_gates(off).wait_send()
    for off in range(1, NCTX):
        pl.when(position + off < NCTX)(lambda off=off: kv_copy(off).wait_send())
    around.settle()
    for k in range(5):
        gather.settle(k)


class Cols:
    LEAD = (0, 256)
    LOW = (0, 1024)
    HIGH = (1024, 1024)
    LOW_REST = (256, 768)


WIDE = (Cols.LOW, Cols.HIGH)
COMPACT = (Cols.LOW_REST, Cols.HIGH)
WINDOW = 80


def block_rows(k):
    return WINDOW if k in (0, 4) else ROWS


def expert_kernel(
    normed_hbm, residual_hbm, gates_ref, cross_gates_ref, gate_hbm, up_hbm, down_hbm,
    out_ref,
    own, lead, own_peer, lead_peer, own_ring, lead_ring, lead_last,
    cross_out, cross_in, window_in, result_own, result_peer, result_in, back_in, picks, spreads,
    wg, wu, wd, picked, act, residual_ref,
    zs, zr, rzs, rzr, cs, cr, rcs, rcr, ls, lr, ps, pr, wsem,
):
    at = Place()
    core, other = at.core, 1 - at.core

    def rows(rel, which=None):
        which = core if which is None else which
        return pl.ds(pl.multiple_of(at.plane(rel) * 2 * TOK + which * TOK, TOK), TOK)

    def both(rel):
        return pl.ds(pl.multiple_of(at.plane(rel) * 2 * TOK, 2 * TOK), 2 * TOK)

    def kept(rel):
        return pl.ds(pl.multiple_of(at.plane(rel) * TOK, TOK), TOK)

    def cols(part):
        return pl.ds(part[0], part[1])

    loads = (
        (normed_hbm, own.at[rows(0)]), (gate_hbm, wg), (up_hbm, wu), (down_hbm, wd),
        (residual_hbm, residual_ref),
    )
    loads = [pltpu.make_async_copy(src, dst, wsem.at[i]) for i, (src, dst) in enumerate(loads)]
    for load in loads:
        load.start()
    barrier = pltpu.get_barrier_semaphore()
    for device in (at.up(), at.down(), at.cross(), at.peer()):
        pl.semaphore_signal(barrier, inc=1, device_id=device, device_id_type=MESH)

    before = (
        lax.broadcasted_iota(jnp.int32, (TOK, TOK), 0) < lax.broadcasted_iota(jnp.int32, (TOK, TOK), 1)
    ).astype(BF)

    def place(gate, offset):
        named = gate > 0.0
        rank = jnp.dot(named.astype(BF), before, preferred_element_type=F32)
        where = jnp.where(named, rank + jnp.asarray(offset).astype(F32), -1.0)
        return where[0:1], where.T[:, 0:1]

    def numbers(count):
        return lax.broadcasted_iota(jnp.int32, (count, TOK), 0).astype(F32)

    def numbers_across(count):
        return lax.broadcasted_iota(jnp.int32, (TOK, count), 1).astype(F32)

    def one_hot(hit):
        return jnp.where(hit, 1.0, 0.0).astype(BF)

    for k in range(5):
        for i, rel in enumerate(rels(k)):
            first, first_across = place(cross_gates_ref[at.plane(rel), 0], CAP * i)
            second, second_across = place(cross_gates_ref[at.plane(rel), 1], CAP * i + CAP * len(rels(k)))
            row = numbers(block_rows(k))
            picks[rel % NZ, : block_rows(k), :] = one_hot((row == first) | (row == second))
            row = numbers_across(block_rows(k))
            spreads[rel % NZ, :, : block_rows(k)] = one_hot((row == first_across) | (row == second_across))

    sent = {k: [] for k in range(5)}
    crossing_sent = {k: [] for k in range(5)}
    returned = []

    def go(log, copy):
        copy.start()
        log.append(copy)

    def stream_ref(stream, rel):
        return lead.at[rows(rel)] if stream == 2 else own.at[rows(rel), cols(WIDE[stream])]

    def hop(stream, direction, k):
        if k > HOPS[stream][direction]:
            return
        rel = -(k - 1) if direction == 0 else k - 1
        ref = stream_ref(stream, rel)
        to = at.up() if direction == 0 else at.down()
        go(sent[abs(rel)], remote(ref, ref, zs.at[stream, direction, k], zr.at[stream, direction, k], to))

    def share(index, src, dst, log):
        go(log, remote(src, dst, ps.at[index], pr.at[index], at.peer()))

    def shared(index, ref):
        remote(ref, ref, ps.at[index], pr.at[index], at.peer()).wait_recv()

    def cross_copy(src, dst, k, part, send, recv):
        these = (pl.ds(0, block_rows(k)), cols(COMPACT[part]))
        return remote(src.at[(k, *these)], dst.at[(k, *these)], send.at[k, part], recv.at[k, part], at.cross())

    def cross(k, part):
        start, width = COMPACT[part]

        def tile(n, carry):
            columns = pl.ds(pl.multiple_of(start + n * 256, 256), 256)
            total = None
            for rel in rels(k):
                one = jnp.dot(
                    picks[rel % NZ, : block_rows(k), :], own[rows(rel), columns], preferred_element_type=F32
                )
                total = one if total is None else total + one
            cross_out[k, : block_rows(k), columns] = total.astype(BF)
            return carry

        lax.fori_loop(0, width // 256, tile, 0, unroll=True)
        go(crossing_sent[k], cross_copy(cross_out, cross_in, k, part, cs, cr))

    def ring(k):
        for stream in (0, 1, 2):
            for direction in (0, 1):
                if k > HOPS[stream][direction]:
                    continue
                rel = 4 if k == 4 else (-k if direction == 0 else k)
                ref = stream_ref(stream, rel)
                remote(
                    ref, ref, zs.at[stream, direction, k], zr.at[stream, direction, k], at.up()
                ).wait_recv()
                hop(stream, direction, k + 1)
                if stream == 2:
                    share(8 + rel % NZ, lead.at[rows(rel)], lead.at[rows(rel)], sent[k])
            if stream < 2:
                cross(k, stream)
        for rel in rels(k):
            share(rel % NZ, own.at[rows(rel)], own.at[rows(rel)], sent[k])

    def window(k, which):
        start = which * 64 if block_rows(k) == ROWS else which * 0
        return pl.ds(pl.multiple_of(start, 16), WINDOW)

    def rest():
        return pl.ds(256, D - 256)

    def column(k):
        for part in (0, 1):
            cross_copy(cross_out, cross_in, k, part, cs, cr).wait_recv()
        share(16 + k, cross_in.at[k, window(k, other), rest()], window_in.at[k, :, rest()], returned)

    def gather_done(k):
        for rel in rels(k):
            shared(rel % NZ, own.at[rows(rel, other)])
            shared(8 + rel % NZ, lead.at[rows(rel, other)])
        shared(16 + k, window_in.at[k, :, rest()])
        for copy in sent[k]:
            copy.wait_send()

    def process(k):
        these = rels(k)
        pair = len(these) == 2
        mine = ROWS if pair else WINDOW
        count = mine + 2 * WINDOW
        first, second = slice(mine, mine + WINDOW), slice(mine + WINDOW, count)

        def gate(rel, col, which):
            return gates_ref[at.slot(rel, col, which)]

        own_hits, own_across, gate_mine = [], [], 0.0
        for i, rel in enumerate(these):
            hits, across = [], []
            for which in (0, 1):
                g = gate(rel, 0, which)
                line, standing = place(g, CAP * (2 * i + which))
                hit = numbers(mine) == line
                gate_mine = gate_mine + jnp.sum(jnp.where(hit, g[0:1], 0.0), axis=1, keepdims=True)
                hits.append(one_hot(hit))
                across.append(one_hot(numbers_across(mine) == standing))
            own_hits.append(jnp.concatenate(hits, axis=1))
            own_across.append(jnp.concatenate(across, axis=0))
        window_hits, window_across, gate_windows = [], [], []
        offset = 4 * core if pair else CAP * core
        for which in (core, other):
            hits, across, total = [], [], 0.0
            for i, rel in enumerate(these):
                g = gate(rel, 1, which)
                line, standing = place(g, offset + CAP * i)
                hit = numbers(WINDOW) == line
                total = total + jnp.sum(jnp.where(hit, g[0:1], 0.0), axis=1, keepdims=True)
                hits.append(one_hot(hit))
                across.append(one_hot(numbers_across(WINDOW) == standing))
            window_hits.append(hits)
            window_across.append(across)
            gate_windows.append(total)
        gate_all = jnp.concatenate([gate_mine, *gate_windows], axis=0)

        def pick(n, carry):
            columns = pl.ds(pl.multiple_of(n * 256, 256), 256)
            total = None
            for hits, rel in zip(own_hits, these):
                one = jnp.dot(hits, own[both(rel), columns], preferred_element_type=F32)
                total = one if total is None else total + one
            picked[:mine, columns] = total.astype(BF)
            return carry

        lax.fori_loop(0, D // 256, pick, 0, unroll=True)
        for side, which, target in ((0, core, first), (1, other, second)):
            total = None
            for hits, rel in zip(window_hits[side], these):
                one = jnp.dot(hits, lead[rows(rel, which), :], preferred_element_type=F32)
                total = one if total is None else total + one
            picked[target, :256] = total.astype(BF)
        picked[first, 256:] = cross_in[k, window(k, core), 256:]
        picked[second, 256:] = window_in[k, :, 256:]

        def hidden(n, carry):
            columns = pl.ds(pl.multiple_of(n * 256, 256), 256)
            x = picked[:count, :]
            g = jnp.dot(x, wg[:, columns], preferred_element_type=F32)
            u = jnp.dot(x, wu[:, columns], preferred_element_type=F32)
            act[:count, columns] = (g / (1.0 + jnp.exp(-g)) * u).astype(BF)
            return carry

        lax.fori_loop(0, EF // 256, hidden, 0, unroll=True)

        def scatter(hits, o):
            return jnp.dot(hits, o, preferred_element_type=F32).astype(BF)

        def outputs(columns):
            o = jnp.dot(act[:count, :], wd[:, columns], preferred_element_type=F32)
            o = (o * gate_all).astype(BF)
            for hits, rel in zip(own_across, these):
                own[both(rel), columns] = scatter(hits, o[:mine])
            return o

        o = outputs(slice(0, 256))
        for side, which, target in ((0, core, first), (1, other, second)):
            for hits, rel in zip(window_across[side], these):
                lead[rows(rel, which), :] = scatter(hits, o[target])

        def spread(n, carry):
            columns = pl.ds(pl.multiple_of(n * 256, 256), 256)
            o = outputs(columns)
            result_own[k, :, columns] = o[first]
            result_peer[k, :, columns] = o[second]
            return carry

        lax.fori_loop(1, D // 256, spread, 0, unroll=True)
        for rel in these:
            share(21 + rel % NZ, own.at[rows(rel, other)], own_peer.at[kept(rel)], returned)
            share(29 + rel % NZ, lead.at[rows(rel, other)], lead_peer.at[kept(rel)], returned)
        share(37 + k, result_peer.at[k, :, rest()], result_in.at[k, :, rest()], returned)

    def cross_back(k):
        for copy in crossing_sent[k]:
            copy.wait_send()
        shared(37 + k, result_in.at[k, :, rest()])

        def tile(n, carry):
            columns = pl.ds(pl.multiple_of(n * 256, 256), 256)
            if block_rows(k) == WINDOW:
                value = result_own[k, :, columns].astype(F32) + result_in[k, :, columns].astype(F32)
                cross_out[k, :WINDOW, columns] = value.astype(BF)
                return carry
            cross_out[k, window(k, core), columns] = result_own[k, :, columns]
            target = pl.ds(pl.multiple_of(80 * other, 16), 64)
            cross_out[k, target, columns] = result_in[k, pl.ds(pl.multiple_of(16 * other, 16), 64), columns]
            a = result_own[k, pl.ds(pl.multiple_of(64 * other, 16), 16), columns]
            b = result_in[k, pl.ds(pl.multiple_of(64 * core, 16), 16), columns]
            cross_out[k, 64:80, columns] = (a.astype(F32) + b.astype(F32)).astype(BF)
            return carry

        for part in (0, 1):
            start, width = COMPACT[part]
            lax.fori_loop(start // 256, (start + width) // 256, tile, 0, unroll=True)
            go(returned, cross_copy(cross_out, back_in, k, part, rcs, rcr))

    def ring_ref(stream, direction, k):
        if stream == 2:
            return lead_ring.at[direction * 4 + k]
        return own_ring.at[direction * 4 + k, :, cols(WIDE[stream])]

    def ring_take(stream, direction, k):
        ref = ring_ref(stream, direction, k)
        remote(
            ref, ref, rzs.at[stream, direction, k], rzr.at[stream, direction, k], at.up()
        ).wait_recv()
        return ref

    def gathered(rel, columns, with_cross, ring_parts):
        value = own[rows(rel), columns].astype(F32) + own_peer[kept(rel), columns].astype(F32)
        if with_cross:
            k = abs(rel)
            value = value + jnp.dot(
                spreads[rel % NZ, :, : block_rows(k)], back_in[k, : block_rows(k), columns],
                preferred_element_type=F32,
            )
        for slot in ring_parts:
            value = value + own_ring[slot, :, columns].astype(F32)
        return value

    def ring_give(stream, direction, k):
        if k > HOPS[stream][direction]:
            return
        rel = 4 if k == 4 else (-k if direction == 0 else k)
        chained = k + 1 <= HOPS[stream][direction]
        if chained:
            ring_take(stream, direction, k)
        slots = [direction * 4 + k] if chained else []
        if stream == 2:
            value = lead[rows(rel), :].astype(F32) + lead_peer[kept(rel), :].astype(F32)
            for slot in slots:
                value = value + lead_ring[slot].astype(F32)
            lead[rows(rel), :] = value.astype(BF)
        else:
            def tile(n, carry, with_cross=True):
                columns = pl.ds(pl.multiple_of(n * 256, 256), 256)
                own[rows(rel), columns] = gathered(rel, columns, with_cross, slots).astype(BF)
                return carry

            if stream == 0:
                tile(0, 0, False)
            lax.fori_loop(stream * 4 + (stream == 0), stream * 4 + 4, tile, 0, unroll=True)
        to = at.down() if direction == 0 else at.up()
        go(returned, remote(
            stream_ref(stream, rel), ring_ref(stream, direction, k - 1),
            rzs.at[stream, direction, k - 1], rzr.at[stream, direction, k - 1], to,
        ))

    def from_peer(k):
        for rel in rels(k):
            shared(21 + rel % NZ, own_peer.at[kept(rel)])
            shared(29 + rel % NZ, lead_peer.at[kept(rel)])

    loads[0].wait()
    pl.semaphore_wait(barrier, 4)
    lead_first = remote(own.at[rows(0), cols(Cols.LEAD)], lead.at[rows(0)], ls.at[0], lr.at[0], at.cross())
    go(sent[0], lead_first)
    for stream in (0, 1):
        for direction in (0, 1):
            hop(stream, direction, 1)
    share(0, own.at[rows(0)], own.at[rows(0)], sent[0])
    cross(0, 0)
    cross(0, 1)
    lead_first.wait_recv()
    for direction in (0, 1):
        hop(2, direction, 1)
    share(8, lead.at[rows(0)], lead.at[rows(0)], sent[0])

    for k in range(5):
        if k < 4:
            ring(k + 1)
        if k == 0:
            for load in loads[1:]:
                load.wait()
        column(k)
        gather_done(k)
        process(k)
        if k == 3:
            cross_back(3)

    cross_back(4)
    for k in (4, 3, 2, 1):
        from_peer(k)
        for direction in (0, 1):
            ring_give(2, direction, k)
        if k <= 3:
            cross_back(k - 1)
        for part in (0, 1):
            cross_copy(cross_out, back_in, k, part, rcs, rcr).wait_recv()
            for direction in (0, 1):
                ring_give(part, direction, k)
    from_peer(0)
    for direction in (0, 1):
        ring_take(2, direction, 0)
    value = lead[rows(0), :].astype(F32) + lead_peer[kept(0), :].astype(F32)
    lead[rows(0), :] = (value + lead_ring[0].astype(F32) + lead_ring[4].astype(F32)).astype(BF)
    last = remote(lead.at[rows(0)], lead_last, ls.at[1], lr.at[1], at.cross())
    last.start()
    for part in (0, 1):
        cross_copy(cross_out, back_in, 0, part, rcs, rcr).wait_recv()
        for direction in (0, 1):
            ring_take(part, direction, 0)

        def tile(n, carry):
            columns = pl.ds(pl.multiple_of(n * 256, 256), 256)
            value = gathered(0, columns, True, (0, 4))
            out_ref[:, columns] = (residual_ref[:, columns] + value).astype(BF)
            return carry

        lax.fori_loop(1 if part == 0 else 4, part * 4 + 4, tile, 0, unroll=True)
    last.wait()
    value = gathered(0, slice(0, 256), False, (0, 4)) + lead_last[...].astype(F32)
    out_ref[:, :256] = (residual_ref[:, :256] + value).astype(BF)
    for copy in returned:
        copy.wait_send()


VMEM = pl.BlockSpec(memory_space=pltpu.VMEM)
ANY = pl.BlockSpec(memory_space=pl.ANY)


def body(
    hidden_in, query, keyval, out_proj, norm_gain, expert_ids, gate_weights, w_gate, w_up, w_down
):
    names = jnp.arange(EXPERTS, dtype=jnp.int32)[:, None, None]
    gates = jnp.sum(
        jnp.where(expert_ids[0].T[None] == names, gate_weights[0].T[None], 0.0), axis=1
    )
    gates = jnp.broadcast_to(gates[:, None, :], (EXPERTS, 8, TOK))

    residual, normed, routed, cross_routed = pl.pallas_call(
        attention_kernel,
        out_shape=(
            jax.ShapeDtypeStruct((TOK, D), F32),
            jax.ShapeDtypeStruct((TOK, D), BF),
            jax.ShapeDtypeStruct((EXPERTS, 8, TOK), F32),
            jax.ShapeDtypeStruct((NZ, 2, 8, TOK), F32),
        ),
        in_specs=[ANY, ANY, ANY, ANY, VMEM, VMEM],
        out_specs=(VMEM, VMEM, VMEM, VMEM),
        scratch_shapes=[
            pltpu.VMEM((QH * HD, DIRECT + QUARTER), BF),
            pltpu.VMEM((3, QH * HD, QUARTER), BF),
            pltpu.VMEM((QH * TOK, HD), BF),
            pltpu.VMEM((NCTX * TOK, 2 * KVH * HD), BF),
            pltpu.VMEM((2 * TOK, 2 * TOK), F32),
            pltpu.VMEM((NZ, TOK, 4 * HD), BF),
            pltpu.VMEM((TOK, D), F32),
            pltpu.VMEM((TOK, D), BF),
            *GATHER_SEMS,
            pltpu.SemaphoreType.DMA((NCTX,)),
            pltpu.SemaphoreType.DMA((NCTX,)),
            pltpu.SemaphoreType.DMA((EXPERTS,)),
            pltpu.SemaphoreType.DMA((EXPERTS,)),
            pltpu.SemaphoreType.DMA((16, 4)),
            pltpu.SemaphoreType.DMA((16, 4)),
            pltpu.SemaphoreType.DMA((16,)),
            pltpu.SemaphoreType.DMA((16,)),
            pltpu.SemaphoreType.DMA((NZ,)),
            pltpu.SemaphoreType.DMA((NZ,)),
            pltpu.SemaphoreType.DMA((QH + 7,)),
        ],
        compiler_params=pltpu.CompilerParams(
            collective_id=0, has_side_effects=True, vmem_limit_bytes=48 << 20
        ),
        name="attend_project",
    )(hidden_in[0], query[0], keyval[0], out_proj, norm_gain.reshape(1, D), gates)

    result = pl.pallas_call(
        expert_kernel,
        out_shape=jax.ShapeDtypeStruct((TOK, D), BF),
        in_specs=[ANY, ANY, VMEM, VMEM, ANY, ANY, ANY],
        out_specs=VMEM,
        scratch_shapes=[
            pltpu.VMEM((NZ * 2 * TOK, D), BF),
            pltpu.VMEM((NZ * 2 * TOK, 256), BF),
            pltpu.VMEM((NZ * TOK, D), BF),
            pltpu.VMEM((NZ * TOK, 256), BF),
            pltpu.VMEM((8, TOK, D), BF),
            pltpu.VMEM((8, TOK, 256), BF),
            pltpu.VMEM((TOK, 256), BF),
            pltpu.VMEM((5, ROWS, D), BF),
            pltpu.VMEM((5, ROWS, D), BF),
            pltpu.VMEM((5, WINDOW, D), BF),
            pltpu.VMEM((5, WINDOW, D), BF),
            pltpu.VMEM((5, WINDOW, D), BF),
            pltpu.VMEM((5, WINDOW, D), BF),
            pltpu.VMEM((5, ROWS, D), BF),
            pltpu.VMEM((NZ, ROWS, TOK), BF),
            pltpu.VMEM((NZ, TOK, ROWS), BF),
            pltpu.VMEM((D, EF), BF),
            pltpu.VMEM((D, EF), BF),
            pltpu.VMEM((EF, D), BF),
            pltpu.VMEM((ROWS + 2 * WINDOW, D), BF),
            pltpu.VMEM((ROWS + 2 * WINDOW, EF), BF),
            pltpu.VMEM((TOK, D), F32),
            pltpu.SemaphoreType.DMA((3, 2, 5)),
            pltpu.SemaphoreType.DMA((3, 2, 5)),
            pltpu.SemaphoreType.DMA((3, 2, 4)),
            pltpu.SemaphoreType.DMA((3, 2, 4)),
            pltpu.SemaphoreType.DMA((5, 2)),
            pltpu.SemaphoreType.DMA((5, 2)),
            pltpu.SemaphoreType.DMA((5, 2)),
            pltpu.SemaphoreType.DMA((5, 2)),
            pltpu.SemaphoreType.DMA((2,)),
            pltpu.SemaphoreType.DMA((2,)),
            pltpu.SemaphoreType.DMA((42,)),
            pltpu.SemaphoreType.DMA((42,)),
            pltpu.SemaphoreType.DMA((5,)),
        ],
        compiler_params=pltpu.CompilerParams(
            collective_id=1, has_side_effects=True, vmem_limit_bytes=58 << 20
        ),
        name="experts",
    )(normed, residual, routed, cross_routed, w_gate[0], w_up[0], w_down[0])
    return result[None]


def solution(mesh):
    in_specs = (
        P("exp", "ctx", None),
        P("exp", "ctx", None),
        P("exp", "ctx", None),
        P("exp", None),
        P(),
        P("exp", "ctx", None),
        P("exp", "ctx", None),
        P("exp", None, None),
        P("exp", None, None),
        P("exp", None, None),
    )
    out_specs = P("exp", "ctx", None)
    return jax.shard_map(body, mesh=mesh, in_specs=in_specs, out_specs=out_specs, check_vma=False)
```

```python
import functools
import math

import jax
import jax.numpy as jnp
from jax import lax
from jax.experimental import pallas as pl
from jax.experimental.pallas import tpu as pltpu
from jax.sharding import PartitionSpec as P

D = 2048
QH = 32
KVH = 2
HD = 128
EF = 768
TOP = 8
TOK = 128
EXPERTS = 32
CAP = 34
ROWS = 144
HALF = 64
DIRECT = 512
QUARTER = 256
RING = DIRECT + 2 * QUARTER
SIDE = 4
NZ = 8
NCTX = 8
MESH = pl.DeviceIdType.MESH
BF = jnp.bfloat16
F32 = jnp.float32

A0, A1, B0 = 0, 1, 2
STREAM = ((0, 0), (1, 0), (0, 1))
HOPS = ((4, 3), (3, 4), (4, 3))


class Place:
    def __init__(self):
        ctx, exp = lax.axis_index("ctx"), lax.axis_index("exp")
        self.ctx, self.exp = ctx, exp
        self.xlo, self.y = ctx // 4, ctx % 4
        self.z, self.xhi, self.core = exp // 4, (exp // 2) % 2, exp % 2

    def device(self, xlo, z, xhi, core):
        return {"ctx": xlo * 4 + self.y, "exp": z * 4 + xhi * 2 + core}

    def up(self):
        return self.device(self.xlo, (self.z + 1) % NZ, self.xhi, self.core)

    def down(self):
        return self.device(self.xlo, (self.z + NZ - 1) % NZ, self.xhi, self.core)

    def cross(self):
        return self.device(1 - self.xlo, self.z, 1 - self.xhi, self.core)

    def peer(self):
        return self.device(self.xlo, self.z, self.xhi, 1 - self.core)

    def plane(self, rel):
        return (self.z + rel + NZ) % NZ

    def column(self, col):
        return self.xhi if col == 0 else 1 - self.xhi

    def slot(self, rel, col, core=None):
        core = self.core if core is None else core
        return self.plane(rel) * 4 + self.column(col) * 2 + core


def rels(k):
    return (0,) if k == 0 else ((4,) if k == 4 else (-k, k))


def remote(src, dst, send, recv, device):
    return pltpu.make_async_remote_copy(
        src_ref=src, dst_ref=dst, send_sem=send, recv_sem=recv, device_id=device, device_id_type=MESH
    )


class Gather:
    def __init__(self, at, buf, zs, zr, cs, cr, ps, pr):
        self.at, self.buf = at, buf
        self.zs, self.zr, self.cs, self.cr, self.ps, self.pr = zs, zr, cs, cr, ps, pr
        self.sent = {k: [] for k in range(5)}

    def rows(self, rel, col, half, core=None):
        start = self.at.slot(rel, col, core) * TOK + half * HALF
        return self.buf.at[pl.ds(pl.multiple_of(start, HALF), HALF)]

    def go(self, k, copy):
        copy.start()
        self.sent[k].append(copy)

    def hop(self, stream, direction, k):
        col, half = STREAM[stream]
        if k > HOPS[stream][direction]:
            return
        rel = -(k - 1) if direction == 0 else k - 1
        ref = self.rows(rel, col, half)
        to = self.at.up() if direction == 0 else self.at.down()
        self.go(abs(rel), remote(ref, ref, self.zs.at[stream, direction, k], self.zr.at[stream, direction, k], to))

    def crossing(self, rel, half):
        ref = self.rows(rel, 0, half)
        index = rel % NZ if half == 1 else NZ
        return remote(ref, ref, self.cs.at[index], self.cr.at[index], self.at.cross())

    def crossed(self, rel, half):
        ref = self.rows(rel, 1, half)
        index = rel % NZ if half == 1 else NZ
        remote(ref, ref, self.cs.at[index], self.cr.at[index], self.at.cross()).wait_recv()

    def block(self, rel, col, core=None):
        return self.buf.at[pl.ds(pl.multiple_of(self.at.slot(rel, col, core) * TOK, TOK), TOK)]

    def share(self, rel, col):
        ref = self.block(rel, col)
        index = (rel % NZ) * 2 + col
        self.go(abs(rel), remote(ref, ref, self.ps.at[index], self.pr.at[index], self.at.peer()))

    def begin(self):
        self.go(0, self.crossing(0, 0))
        for stream in (B0, A0):
            for direction in (0, 1):
                self.hop(stream, direction, 1)
        self.go(0, self.crossing(0, 1))
        self.share(0, 0)

    def begin_column(self):
        self.crossed(0, 0)
        for direction in (0, 1):
            self.hop(A1, direction, 1)

    def ring(self, k):
        for stream in (B0, A0, A1):
            col, half = STREAM[stream]
            for direction in (0, 1):
                if k > HOPS[stream][direction]:
                    continue
                rel = -k if direction == 0 else k
                rel = 4 if k == 4 else rel
                ref = self.rows(rel, col, half)
                sem = self.zr.at[stream, direction, k]
                remote(ref, ref, self.zs.at[stream, direction, k], sem, self.at.up()).wait_recv()
                self.hop(stream, direction, k + 1)
                if stream == B0:
                    self.go(k, self.crossing(rel, 1))
                if stream == A0:
                    self.share(rel, 0)

    def column(self, k):
        for rel in rels(k):
            self.crossed(rel, 1)
            self.share(rel, 1)

    def shared(self, k):
        for rel in rels(k):
            for col in (0, 1):
                ref = self.block(rel, col, 1 - self.at.core)
                index = (rel % NZ) * 2 + col
                remote(ref, ref, self.ps.at[index], self.pr.at[index], self.at.peer()).wait_recv()

    def settle(self, k):
        for copy in self.sent[k]:
            copy.wait_send()


GATHER_SEMS = [
    pltpu.SemaphoreType.DMA((3, 2, 5)),
    pltpu.SemaphoreType.DMA((3, 2, 5)),
    pltpu.SemaphoreType.DMA((9,)),
    pltpu.SemaphoreType.DMA((9,)),
    pltpu.SemaphoreType.DMA((16,)),
    pltpu.SemaphoreType.DMA((16,)),
]


class Around:
    def __init__(self, at, ring, rest, ys, yr, ps, pr):
        self.at, self.ring, self.rest = at, ring, rest
        self.ys, self.yr, self.ps, self.pr = ys, yr, ps, pr
        self.sent = []

    def device(self, off):
        if off == SIDE:
            return {"ctx": (1 - self.at.xlo) * 4 + self.at.y, "exp": self.at.exp}
        return {"ctx": self.at.xlo * 4 + (self.at.y + off) % 4, "exp": self.at.exp}

    def columns(self, off):
        if off >= SIDE:
            side = (self.at.xlo + self.at.xhi + off - SIDE) % 2
            return pl.ds(pl.multiple_of(DIRECT + side * QUARTER, QUARTER), QUARTER)
        start = DIRECT + 2 * QUARTER + (self.at.y + off) % 4 * QUARTER
        return pl.ds(pl.multiple_of(start, QUARTER), QUARTER)

    def rows(self, rel, col, core=None):
        return pl.ds(pl.multiple_of(self.at.slot(rel, col, core) * TOK, TOK), TOK)

    def copy(self, src, rel, col, off, to):
        index = (rel % NZ) * 2 + col
        dst = self.rest.at[off - 1, self.rows(rel, col)]
        return remote(src, dst, self.ys.at[index, off], self.yr.at[index, off], self.device(to))

    def go(self, copy):
        copy.start()
        self.sent.append(copy)

    def give(self, rel, col):
        src = self.ring.at[self.rows(rel, col), pl.ds(DIRECT + QUARTER, QUARTER)]
        self.go(self.copy(src, rel, col, 1, 3))
        self.go(self.copy(src, rel, col, 3, 1))
        if rel == 4:
            self.go(self.copy(src, rel, col, 2, 2))
        side = self.ring.at[self.rows(rel, col), pl.ds(DIRECT, QUARTER)]
        self.go(self.copy(side, rel, col, SIDE, SIDE))

    def arrived(self, rel, col, off):
        here = self.rest.at[off - 1, self.rows(rel, col)]
        self.copy(here, rel, col, off, 1).wait_recv()

    def forward(self, rel, col):
        self.arrived(rel, col, 1)
        self.arrived(rel, col, 3)
        if rel == 4:
            return
        off, to = (3, 1) if col == 0 else (1, 3)
        self.go(self.copy(self.rest.at[off - 1, self.rows(rel, col)], rel, col, 2, to))

    def share(self, rel, col):
        if (rel, col) != (0, 0):
            self.arrived(rel, col, 2)
            self.arrived(rel, col, SIDE)
        ref = self.rest.at[:, self.rows(rel, col)]
        index = (rel % NZ) * 2 + col
        self.go(remote(ref, ref, self.ps.at[index], self.pr.at[index], self.at.peer()))

    def shared(self, k):
        for rel in rels(k):
            for col in (0, 1):
                ref = self.rest.at[:, self.rows(rel, col, 1 - self.at.core)]
                index = (rel % NZ) * 2 + col
                remote(ref, ref, self.ps.at[index], self.pr.at[index], self.at.peer()).wait_recv()

    def settle(self):
        for copy in self.sent:
            copy.wait_send()


def attention_kernel(
    hidden_hbm, query_hbm, kv_hbm, proj_hbm, gain_ref, gates_ref,
    residual_ref, normed_ref, gates_out, cross_gates_out,
    ring, rest, heads, kvs, visible, mixed, total, hidden,
    zs, zr, cs, cr, ps, pr, ks, kr, gs, gr, ys, yr, yps, ypr, g2s, g2r, own_sem,
):
    at = Place()
    position = at.ctx
    place = pl.ds(pl.multiple_of(at.exp * TOK, TOK), TOK)
    loads = [
        (kv_hbm, kvs.at[pl.ds(pl.multiple_of(position * TOK, TOK), TOK)]),
        (proj_hbm.at[:, pl.ds(0, DIRECT)], ring.at[place, pl.ds(0, DIRECT)]),
    ]
    around = Around(at, ring, rest, ys, yr, yps, ypr)
    for off in range(6):
        if off == 0:
            to = ring.at[place, pl.ds(DIRECT + QUARTER, QUARTER)]
        elif off == SIDE:
            to = ring.at[place, pl.ds(DIRECT, QUARTER)]
        else:
            to = rest.at[off - 1 if off < SIDE else SIDE - 1, place]
        loads.append((proj_hbm.at[:, around.columns(off)], to))
    for h in range(QH):
        loads.append((query_hbm.at[:, pl.ds(h * HD, HD)], heads.at[pl.ds(h * TOK, TOK)]))
    loads.append((hidden_hbm, hidden))
    loads = [pltpu.make_async_copy(src, dst, own_sem.at[i]) for i, (src, dst) in enumerate(loads)]
    for load in loads:
        load.start()

    def gate_target(off):
        other = (at.exp + off) % EXPERTS
        other_hi = (other // 2) % 2
        return other, {"ctx": ((at.xlo + at.xhi + other_hi) % 2) * 4 + at.y, "exp": other}

    barrier = pltpu.get_barrier_semaphore()

    def greet(off, carry):
        _, device = gate_target(off)
        pl.semaphore_signal(barrier, inc=1, device_id=device, device_id_type=MESH)
        return carry

    lax.fori_loop(1, EXPERTS, greet, 0)
    for off in range(1, NCTX):
        device = {"ctx": (position + off) % NCTX, "exp": at.exp}
        pl.semaphore_signal(barrier, inc=1, device_id=device, device_id_type=MESH)

    gates_out[pl.ds(at.exp, 1)] = gates_ref[pl.ds(at.exp, 1)]

    def partner_gates(off):
        plane = (at.z + off) % NZ
        src = gates_ref.at[pl.ds(plane * 4 + (1 - at.xhi) * 2, 2)]
        to = at.device(at.xlo, plane, at.xhi, at.core)
        return remote(src, cross_gates_out.at[at.z], g2s.at[off], g2r.at[off], to)

    cross_gates_out[pl.ds(at.z, 1)] = gates_ref[pl.ds(at.z * 4 + (1 - at.xhi) * 2, 2)][None]

    @pl.when(position % 2 == 0)
    def _():
        kvs[pl.ds(pl.multiple_of((position + 1) * TOK, TOK), TOK), :] = jnp.zeros((TOK, 2 * KVH * HD), BF)

    for load in loads[:8]:
        load.wait()
    pl.semaphore_wait(barrier, EXPERTS - 1 + NCTX - 1)

    gather = Gather(at, ring, zs, zr, cs, cr, ps, pr)
    gather.begin()

    mine = kvs.at[pl.ds(pl.multiple_of(position * TOK, TOK), TOK)]

    def kv_copy(off):
        device = {"ctx": (position + off) % NCTX, "exp": at.exp}
        return remote(mine, mine, ks.at[off], kr.at[off], device)

    for off in range(1, NCTX):
        pl.when(position + off < NCTX)(lambda off=off: kv_copy(off).start())

    def send_gates(off, carry):
        other, device = gate_target(off)
        remote(gates_ref.at[other], gates_out.at[at.exp], gs.at[off], gr.at[off], device).start()
        return carry

    lax.fori_loop(1, EXPERTS, send_gates, 0)
    for off in range(1, NZ):
        partner_gates(off).start()
    gather.begin_column()
    around.share(0, 0)
    for load in loads[8:]:
        load.wait()

    def kv_arrived(off):
        ref = kvs.at[pl.ds(pl.multiple_of((position + NCTX - off) % NCTX * TOK, TOK), TOK)]
        remote(ref, ref, ks.at[off], kr.at[off], {"ctx": (position + off) % NCTX, "exp": at.exp}).wait_recv()

    scale = HD ** (-0.5) * math.log2(math.e)
    last = position // 2
    row_pos = position * TOK + lax.broadcasted_iota(jnp.int32, (2 * TOK, 2 * TOK), 0) % TOK
    key_pos = last * 2 * TOK + lax.broadcasted_iota(jnp.int32, (2 * TOK, 2 * TOK), 1)
    visible[...] = jnp.where(row_pos >= key_pos, 0.0, 1.0)

    def attend(pairs, chunk, carry):
        lane = pl.multiple_of((chunk // 8) * HD, HD)
        q = heads[pl.ds(pl.multiple_of(chunk * 2 * TOK, 2 * TOK), 2 * TOK), :]
        parts, running = [], None
        for pair in range(pairs):
            keys = kvs[pair * 2 * TOK : (pair + 1) * 2 * TOK, pl.ds(lane, HD)]
            s = lax.dot_general(q, keys, (((1,), (1,)), ((), ())), preferred_element_type=F32)
            if pair == pairs - 1:
                s = jnp.where(visible[...] == 0.0, s, -1e30)
            parts.append(s)
            top = jnp.maximum(s[:, :TOK], s[:, TOK:])
            running = top if running is None else jnp.maximum(running, top)
        row_max = jnp.max(running, axis=1, keepdims=True)
        row_sum, acc = None, None
        for pair in range(pairs):
            weight = jnp.exp2((parts[pair] - row_max) * scale)
            values = kvs[pair * 2 * TOK : (pair + 1) * 2 * TOK, pl.ds(pl.multiple_of(lane + KVH * HD, HD), HD)]
            part = jnp.dot(weight.astype(BF), values, preferred_element_type=F32)
            both = weight[:, :TOK] + weight[:, TOK:]
            acc = part if acc is None else acc + part
            row_sum = both if row_sum is None else row_sum + both
        out = (acc / jnp.sum(row_sum, axis=1, keepdims=True)).astype(BF)
        plane, side = chunk // 2, chunk % 2
        for i in range(2):
            columns = pl.ds(pl.multiple_of((side * 2 + i) * HD, HD), HD)
            mixed[plane, :, columns] = out[i * TOK : (i + 1) * TOK]
        return carry

    def some(pairs, first, end):
        lax.fori_loop(first, end, functools.partial(attend, pairs), 0)

    def attend_some(first, end):
        for pairs in range(1, NCTX // 2 + 1):
            pl.when(last == pairs - 1)(
                lambda pairs=pairs: some(pairs, first, end)
            )

    def give(k, col):
        for rel in rels(k):
            around.give(rel, col)

    def forward(k, col):
        for rel in rels(k):
            around.forward(rel, col)

    def share(k):
        for rel in rels(k):
            for col in (0, 1):
                if (rel, col) != (0, 0):
                    around.share(rel, col)

    def project(k):
        gather.shared(k)
        around.shared(k)
        for rel in rels(k):
            plane = at.plane(rel)
            rows = pl.ds(pl.multiple_of(plane * 4 * TOK, 4 * TOK), 4 * TOK)

            def tile(n, carry):
                columns = pl.ds(pl.multiple_of(n * 512, 512), 512)
                total[:, columns] += jnp.dot(mixed[plane], ring[rows, columns], preferred_element_type=F32)
                return carry

            lax.fori_loop(0, DIRECT // 512, tile, 0, unroll=True)
            for off in range(6):
                if off in (0, SIDE):
                    start = DIRECT + QUARTER if off == 0 else DIRECT
                    part = ring[rows, start : start + QUARTER]
                else:
                    part = rest[off - 1 if off < SIDE else SIDE - 1, rows, :]
                columns = around.columns(off)
                total[:, columns] += jnp.dot(mixed[plane], part, preferred_element_type=F32)

    gather.column(0)
    give(0, 1)
    gather.ring(1)
    give(1, 0)
    for off in range(1, NCTX):
        pl.when(position - off >= 0)(lambda off=off: kv_arrived(off))

    attend_some(0, 5)
    gather.column(1)
    give(1, 1)
    forward(0, 1)
    gather.ring(2)
    give(2, 0)
    forward(1, 0)
    attend_some(5, 10)
    gather.column(2)
    give(2, 1)
    forward(1, 1)
    share(0)
    gather.ring(3)
    give(3, 0)
    forward(2, 0)
    share(1)
    attend_some(10, 16)
    total[...] = hidden[...].astype(F32)
    project(0)
    gather.column(3)
    give(3, 1)
    forward(2, 1)
    project(1)
    gather.ring(4)
    give(4, 0)
    forward(3, 0)
    share(2)
    gather.column(4)
    give(4, 1)
    forward(3, 1)
    project(2)
    forward(4, 0)
    share(3)
    forward(4, 1)
    project(3)
    share(4)
    project(4)

    def norm(i, carry):
        rows = pl.ds(pl.multiple_of(i * 16, 16), 16)
        r = total[rows, :]
        inverse = lax.rsqrt(jnp.mean(r * r, axis=-1, keepdims=True) + 1e-06)
        normed_ref[rows, :] = (r * inverse * gain_ref[...].astype(F32)).astype(BF)
        residual_ref[rows, :] = r
        return carry

    lax.fori_loop(0, TOK // 16, norm, 0, unroll=4)

    def take_gates(off, carry):
        other, device = gate_target(off)
        origin = (at.exp + EXPERTS - off) % EXPERTS
        copy = remote(gates_ref.at[other], gates_out.at[origin], gs.at[off], gr.at[off], device)
        copy.wait_send()
        copy.wait_recv()
        return carry

    lax.fori_loop(1, EXPERTS, take_gates, 0)
    for off in range(1, NZ):
        ref = cross_gates_out.at[(at.z + NZ - off) % NZ]
        remote(ref, ref, g2s.at[off], g2r.at[off], at.up()).wait_recv()
        partner_gates(off).wait_send()
    for off in range(1, NCTX):
        pl.when(position + off < NCTX)(lambda off=off: kv_copy(off).wait_send())
    around.settle()
    for k in range(5):
        gather.settle(k)


class Cols:
    LEAD = (0, 256)
    LOW = (0, 1024)
    HIGH = (1024, 1024)
    LOW_REST = (256, 768)


WIDE = (Cols.LOW, Cols.HIGH)
COMPACT = (Cols.LOW_REST, Cols.HIGH)
WINDOW = 80


def block_rows(k):
    return WINDOW if k in (0, 4) else ROWS


def expert_kernel(
    normed_hbm, residual_hbm, gates_ref, cross_gates_ref, gate_hbm, up_hbm, down_hbm,
    out_ref,
    own, lead, own_peer, lead_peer, own_ring, lead_ring, lead_last,
    cross_out, cross_in, window_in, result_own, result_peer, result_in, back_in, picks, spreads,
    wg, wu, wd, picked, act, residual_ref,
    zs, zr, rzs, rzr, cs, cr, rcs, rcr, ls, lr, ps, pr, wsem,
):
    at = Place()
    core, other = at.core, 1 - at.core

    def rows(rel, which=None):
        which = core if which is None else which
        return pl.ds(pl.multiple_of(at.plane(rel) * 2 * TOK + which * TOK, TOK), TOK)

    def both(rel):
        return pl.ds(pl.multiple_of(at.plane(rel) * 2 * TOK, 2 * TOK), 2 * TOK)

    def kept(rel):
        return pl.ds(pl.multiple_of(at.plane(rel) * TOK, TOK), TOK)

    def cols(part):
        return pl.ds(part[0], part[1])

    loads = (
        (normed_hbm, own.at[rows(0)]), (gate_hbm, wg), (up_hbm, wu), (down_hbm, wd),
        (residual_hbm, residual_ref),
    )
    loads = [pltpu.make_async_copy(src, dst, wsem.at[i]) for i, (src, dst) in enumerate(loads)]
    for load in loads:
        load.start()
    barrier = pltpu.get_barrier_semaphore()
    for device in (at.up(), at.down(), at.cross(), at.peer()):
        pl.semaphore_signal(barrier, inc=1, device_id=device, device_id_type=MESH)

    before = (
        lax.broadcasted_iota(jnp.int32, (TOK, TOK), 0) < lax.broadcasted_iota(jnp.int32, (TOK, TOK), 1)
    ).astype(BF)

    def place(gate, offset):
        named = gate > 0.0
        rank = jnp.dot(named.astype(BF), before, preferred_element_type=F32)
        where = jnp.where(named, rank + jnp.asarray(offset).astype(F32), -1.0)
        return where[0:1], where.T[:, 0:1]

    def numbers(count):
        return lax.broadcasted_iota(jnp.int32, (count, TOK), 0).astype(F32)

    def numbers_across(count):
        return lax.broadcasted_iota(jnp.int32, (TOK, count), 1).astype(F32)

    def one_hot(hit):
        return jnp.where(hit, 1.0, 0.0).astype(BF)

    for k in range(5):
        for i, rel in enumerate(rels(k)):
            first, first_across = place(cross_gates_ref[at.plane(rel), 0], CAP * i)
            second, second_across = place(cross_gates_ref[at.plane(rel), 1], CAP * i + CAP * len(rels(k)))
            row = numbers(block_rows(k))
            picks[rel % NZ, : block_rows(k), :] = one_hot((row == first) | (row == second))
            row = numbers_across(block_rows(k))
            spreads[rel % NZ, :, : block_rows(k)] = one_hot((row == first_across) | (row == second_across))

    sent = {k: [] for k in range(5)}
    crossing_sent = {k: [] for k in range(5)}
    returned = []

    def go(log, copy):
        copy.start()
        log.append(copy)

    def stream_ref(stream, rel):
        return lead.at[rows(rel)] if stream == 2 else own.at[rows(rel), cols(WIDE[stream])]

    def hop(stream, direction, k):
        if k > HOPS[stream][direction]:
            return
        rel = -(k - 1) if direction == 0 else k - 1
        ref = stream_ref(stream, rel)
        to = at.up() if direction == 0 else at.down()
        go(sent[abs(rel)], remote(ref, ref, zs.at[stream, direction, k], zr.at[stream, direction, k], to))

    def share(index, src, dst, log):
        go(log, remote(src, dst, ps.at[index], pr.at[index], at.peer()))

    def shared(index, ref):
        remote(ref, ref, ps.at[index], pr.at[index], at.peer()).wait_recv()

    def cross_copy(src, dst, k, part, send, recv):
        these = (pl.ds(0, block_rows(k)), cols(COMPACT[part]))
        return remote(src.at[(k, *these)], dst.at[(k, *these)], send.at[k, part], recv.at[k, part], at.cross())

    def cross(k, part):
        start, width = COMPACT[part]

        def tile(n, carry):
            columns = pl.ds(pl.multiple_of(start + n * 256, 256), 256)
            total = None
            for rel in rels(k):
                one = jnp.dot(
                    picks[rel % NZ, : block_rows(k), :], own[rows(rel), columns], preferred_element_type=F32
                )
                total = one if total is None else total + one
            cross_out[k, : block_rows(k), columns] = total.astype(BF)
            return carry

        lax.fori_loop(0, width // 256, tile, 0)
        go(crossing_sent[k], cross_copy(cross_out, cross_in, k, part, cs, cr))

    def ring(k):
        for stream in (0, 1, 2):
            for direction in (0, 1):
                if k > HOPS[stream][direction]:
                    continue
                rel = 4 if k == 4 else (-k if direction == 0 else k)
                ref = stream_ref(stream, rel)
                remote(
                    ref, ref, zs.at[stream, direction, k], zr.at[stream, direction, k], at.up()
                ).wait_recv()
                hop(stream, direction, k + 1)
                if stream == 2:
                    share(8 + rel % NZ, lead.at[rows(rel)], lead.at[rows(rel)], sent[k])
            if stream < 2:
                cross(k, stream)
        for rel in rels(k):
            share(rel % NZ, own.at[rows(rel)], own.at[rows(rel)], sent[k])

    def window(k, which):
        start = which * 64 if block_rows(k) == ROWS else which * 0
        return pl.ds(pl.multiple_of(start, 16), WINDOW)

    def rest():
        return pl.ds(256, D - 256)

    def column(k):
        for part in (0, 1):
            cross_copy(cross_out, cross_in, k, part, cs, cr).wait_recv()
        share(16 + k, cross_in.at[k, window(k, other), rest()], window_in.at[k, :, rest()], returned)

    def gather_done(k):
        for rel in rels(k):
            shared(rel % NZ, own.at[rows(rel, other)])
            shared(8 + rel % NZ, lead.at[rows(rel, other)])
        shared(16 + k, window_in.at[k, :, rest()])
        for copy in sent[k]:
            copy.wait_send()

    def process(k):
        these = rels(k)
        pair = len(these) == 2
        mine = ROWS if pair else WINDOW
        count = mine + 2 * WINDOW
        first, second = slice(mine, mine + WINDOW), slice(mine + WINDOW, count)

        def gate(rel, col, which):
            return gates_ref[at.slot(rel, col, which)]

        own_hits, own_across, gate_mine = [], [], 0.0
        for i, rel in enumerate(these):
            hits, across = [], []
            for which in (0, 1):
                g = gate(rel, 0, which)
                line, standing = place(g, CAP * (2 * i + which))
                hit = numbers(mine) == line
                gate_mine = gate_mine + jnp.sum(jnp.where(hit, g[0:1], 0.0), axis=1, keepdims=True)
                hits.append(one_hot(hit))
                across.append(one_hot(numbers_across(mine) == standing))
            own_hits.append(jnp.concatenate(hits, axis=1))
            own_across.append(jnp.concatenate(across, axis=0))
        window_hits, window_across, gate_windows = [], [], []
        offset = 4 * core if pair else CAP * core
        for which in (core, other):
            hits, across, total = [], [], 0.0
            for i, rel in enumerate(these):
                g = gate(rel, 1, which)
                line, standing = place(g, offset + CAP * i)
                hit = numbers(WINDOW) == line
                total = total + jnp.sum(jnp.where(hit, g[0:1], 0.0), axis=1, keepdims=True)
                hits.append(one_hot(hit))
                across.append(one_hot(numbers_across(WINDOW) == standing))
            window_hits.append(hits)
            window_across.append(across)
            gate_windows.append(total)
        gate_all = jnp.concatenate([gate_mine, *gate_windows], axis=0)

        def pick(n, carry):
            columns = pl.ds(pl.multiple_of(n * 256, 256), 256)
            total = None
            for hits, rel in zip(own_hits, these):
                one = jnp.dot(hits, own[both(rel), columns], preferred_element_type=F32)
                total = one if total is None else total + one
            picked[:mine, columns] = total.astype(BF)
            return carry

        lax.fori_loop(0, D // 256, pick, 0, unroll=True)
        for side, which, target in ((0, core, first), (1, other, second)):
            total = None
            for hits, rel in zip(window_hits[side], these):
                one = jnp.dot(hits, lead[rows(rel, which), :], preferred_element_type=F32)
                total = one if total is None else total + one
            picked[target, :256] = total.astype(BF)
        picked[first, 256:] = cross_in[k, window(k, core), 256:]
        picked[second, 256:] = window_in[k, :, 256:]

        def hidden(n, carry):
            columns = pl.ds(pl.multiple_of(n * 256, 256), 256)
            x = picked[:count, :]
            g = jnp.dot(x, wg[:, columns], preferred_element_type=F32)
            u = jnp.dot(x, wu[:, columns], preferred_element_type=F32)
            act[:count, columns] = (g / (1.0 + jnp.exp(-g)) * u).astype(BF)
            return carry

        lax.fori_loop(0, EF // 256, hidden, 0, unroll=True)

        def scatter(hits, o):
            return jnp.dot(hits, o, preferred_element_type=F32).astype(BF)

        def outputs(columns):
            o = jnp.dot(act[:count, :], wd[:, columns], preferred_element_type=F32)
            o = (o * gate_all).astype(BF)
            for hits, rel in zip(own_across, these):
                own[both(rel), columns] = scatter(hits, o[:mine])
            return o

        o = outputs(slice(0, 256))
        for side, which, target in ((0, core, first), (1, other, second)):
            for hits, rel in zip(window_across[side], these):
                lead[rows(rel, which), :] = scatter(hits, o[target])

        def spread(n, carry):
            columns = pl.ds(pl.multiple_of(n * 256, 256), 256)
            o = outputs(columns)
            result_own[k, :, columns] = o[first]
            result_peer[k, :, columns] = o[second]
            return carry

        lax.fori_loop(1, D // 256, spread, 0, unroll=True)
        for rel in these:
            share(21 + rel % NZ, own.at[rows(rel, other)], own_peer.at[kept(rel)], returned)
            share(29 + rel % NZ, lead.at[rows(rel, other)], lead_peer.at[kept(rel)], returned)
        share(37 + k, result_peer.at[k, :, rest()], result_in.at[k, :, rest()], returned)

    def cross_back(k):
        for copy in crossing_sent[k]:
            copy.wait_send()
        shared(37 + k, result_in.at[k, :, rest()])

        def tile(n, carry):
            columns = pl.ds(pl.multiple_of(n * 256, 256), 256)
            if block_rows(k) == WINDOW:
                value = result_own[k, :, columns].astype(F32) + result_in[k, :, columns].astype(F32)
                cross_out[k, :WINDOW, columns] = value.astype(BF)
                return carry
            cross_out[k, window(k, core), columns] = result_own[k, :, columns]
            target = pl.ds(pl.multiple_of(80 * other, 16), 64)
            cross_out[k, target, columns] = result_in[k, pl.ds(pl.multiple_of(16 * other, 16), 64), columns]
            a = result_own[k, pl.ds(pl.multiple_of(64 * other, 16), 16), columns]
            b = result_in[k, pl.ds(pl.multiple_of(64 * core, 16), 16), columns]
            cross_out[k, 64:80, columns] = (a.astype(F32) + b.astype(F32)).astype(BF)
            return carry

        for part in (0, 1):
            start, width = COMPACT[part]
            lax.fori_loop(start // 256, (start + width) // 256, tile, 0)
            go(returned, cross_copy(cross_out, back_in, k, part, rcs, rcr))

    def ring_ref(stream, direction, k):
        if stream == 2:
            return lead_ring.at[direction * 4 + k]
        return own_ring.at[direction * 4 + k, :, cols(WIDE[stream])]

    def ring_take(stream, direction, k):
        ref = ring_ref(stream, direction, k)
        remote(
            ref, ref, rzs.at[stream, direction, k], rzr.at[stream, direction, k], at.up()
        ).wait_recv()
        return ref

    def gathered(rel, columns, with_cross, ring_parts):
        value = own[rows(rel), columns].astype(F32) + own_peer[kept(rel), columns].astype(F32)
        if with_cross:
            k = abs(rel)
            value = value + jnp.dot(
                spreads[rel % NZ, :, : block_rows(k)], back_in[k, : block_rows(k), columns],
                preferred_element_type=F32,
            )
        for slot in ring_parts:
            value = value + own_ring[slot, :, columns].astype(F32)
        return value

    def ring_give(stream, direction, k):
        if k > HOPS[stream][direction]:
            return
        rel = 4 if k == 4 else (-k if direction == 0 else k)
        chained = k + 1 <= HOPS[stream][direction]
        if chained:
            ring_take(stream, direction, k)
        slots = [direction * 4 + k] if chained else []
        if stream == 2:
            value = lead[rows(rel), :].astype(F32) + lead_peer[kept(rel), :].astype(F32)
            for slot in slots:
                value = value + lead_ring[slot].astype(F32)
            lead[rows(rel), :] = value.astype(BF)
        else:
            def tile(n, carry, with_cross=True):
                columns = pl.ds(pl.multiple_of(n * 256, 256), 256)
                own[rows(rel), columns] = gathered(rel, columns, with_cross, slots).astype(BF)
                return carry

            if stream == 0:
                tile(0, 0, False)
            lax.fori_loop(stream * 4 + (stream == 0), stream * 4 + 4, tile, 0)
        to = at.down() if direction == 0 else at.up()
        go(returned, remote(
            stream_ref(stream, rel), ring_ref(stream, direction, k - 1),
            rzs.at[stream, direction, k - 1], rzr.at[stream, direction, k - 1], to,
        ))

    def from_peer(k):
        for rel in rels(k):
            shared(21 + rel % NZ, own_peer.at[kept(rel)])
            shared(29 + rel % NZ, lead_peer.at[kept(rel)])

    loads[0].wait()
    pl.semaphore_wait(barrier, 4)
    lead_first = remote(own.at[rows(0), cols(Cols.LEAD)], lead.at[rows(0)], ls.at[0], lr.at[0], at.cross())
    go(sent[0], lead_first)
    for stream in (0, 1):
        for direction in (0, 1):
            hop(stream, direction, 1)
    share(0, own.at[rows(0)], own.at[rows(0)], sent[0])
    cross(0, 0)
    cross(0, 1)
    lead_first.wait_recv()
    for direction in (0, 1):
        hop(2, direction, 1)
    share(8, lead.at[rows(0)], lead.at[rows(0)], sent[0])

    for k in range(5):
        if k < 4:
            ring(k + 1)
        if k == 0:
            for load in loads[1:]:
                load.wait()
        column(k)
        gather_done(k)
        process(k)
        if k == 3:
            cross_back(3)

    cross_back(4)
    for k in (4, 3, 2, 1):
        from_peer(k)
        for direction in (0, 1):
            ring_give(2, direction, k)
        if k <= 3:
            cross_back(k - 1)
        for part in (0, 1):
            cross_copy(cross_out, back_in, k, part, rcs, rcr).wait_recv()
            for direction in (0, 1):
                ring_give(part, direction, k)
    from_peer(0)
    for direction in (0, 1):
        ring_take(2, direction, 0)
    value = lead[rows(0), :].astype(F32) + lead_peer[kept(0), :].astype(F32)
    lead[rows(0), :] = (value + lead_ring[0].astype(F32) + lead_ring[4].astype(F32)).astype(BF)
    last = remote(lead.at[rows(0)], lead_last, ls.at[1], lr.at[1], at.cross())
    last.start()
    for part in (0, 1):
        cross_copy(cross_out, back_in, 0, part, rcs, rcr).wait_recv()
        for direction in (0, 1):
            ring_take(part, direction, 0)

        def tile(n, carry):
            columns = pl.ds(pl.multiple_of(n * 256, 256), 256)
            value = gathered(0, columns, True, (0, 4))
            out_ref[:, columns] = (residual_ref[:, columns] + value).astype(BF)
            return carry

        lax.fori_loop(1 if part == 0 else 4, part * 4 + 4, tile, 0)
    last.wait()
    value = gathered(0, slice(0, 256), False, (0, 4)) + lead_last[...].astype(F32)
    out_ref[:, :256] = (residual_ref[:, :256] + value).astype(BF)
    for copy in returned:
        copy.wait_send()


VMEM = pl.BlockSpec(memory_space=pltpu.VMEM)
ANY = pl.BlockSpec(memory_space=pl.ANY)


def body(
    hidden_in, query, keyval, out_proj, norm_gain, expert_ids, gate_weights, w_gate, w_up, w_down
):
    names = jnp.arange(EXPERTS, dtype=jnp.int32)[:, None, None]
    gates = jnp.sum(
        jnp.where(expert_ids[0].T[None] == names, gate_weights[0].T[None], 0.0), axis=1
    )
    gates = jnp.broadcast_to(gates[:, None, :], (EXPERTS, 8, TOK))

    residual, normed, routed, cross_routed = pl.pallas_call(
        attention_kernel,
        out_shape=(
            jax.ShapeDtypeStruct((TOK, D), F32),
            jax.ShapeDtypeStruct((TOK, D), BF),
            jax.ShapeDtypeStruct((EXPERTS, 8, TOK), F32),
            jax.ShapeDtypeStruct((NZ, 2, 8, TOK), F32),
        ),
        in_specs=[ANY, ANY, ANY, ANY, VMEM, VMEM],
        out_specs=(VMEM, VMEM, VMEM, VMEM),
        scratch_shapes=[
            pltpu.VMEM((QH * HD, RING), BF),
            pltpu.VMEM((4, QH * HD, QUARTER), BF),
            pltpu.VMEM((QH * TOK, HD), BF),
            pltpu.VMEM((NCTX * TOK, 2 * KVH * HD), BF),
            pltpu.VMEM((2 * TOK, 2 * TOK), F32),
            pltpu.VMEM((NZ, TOK, 4 * HD), BF),
            pltpu.VMEM((TOK, D), F32),
            pltpu.VMEM((TOK, D), BF),
            *GATHER_SEMS,
            pltpu.SemaphoreType.DMA((NCTX,)),
            pltpu.SemaphoreType.DMA((NCTX,)),
            pltpu.SemaphoreType.DMA((EXPERTS,)),
            pltpu.SemaphoreType.DMA((EXPERTS,)),
            pltpu.SemaphoreType.DMA((16, 5)),
            pltpu.SemaphoreType.DMA((16, 5)),
            pltpu.SemaphoreType.DMA((16,)),
            pltpu.SemaphoreType.DMA((16,)),
            pltpu.SemaphoreType.DMA((NZ,)),
            pltpu.SemaphoreType.DMA((NZ,)),
            pltpu.SemaphoreType.DMA((QH + 9,)),
        ],
        compiler_params=pltpu.CompilerParams(
            collective_id=0, has_side_effects=True, vmem_limit_bytes=62 << 20
        ),
        name="attend_project",
    )(hidden_in[0], query[0], keyval[0], out_proj, norm_gain.reshape(1, D), gates)

    result = pl.pallas_call(
        expert_kernel,
        out_shape=jax.ShapeDtypeStruct((TOK, D), BF),
        in_specs=[ANY, ANY, VMEM, VMEM, ANY, ANY, ANY],
        out_specs=VMEM,
        scratch_shapes=[
            pltpu.VMEM((NZ * 2 * TOK, D), BF),
            pltpu.VMEM((NZ * 2 * TOK, 256), BF),
            pltpu.VMEM((NZ * TOK, D), BF),
            pltpu.VMEM((NZ * TOK, 256), BF),
            pltpu.VMEM((8, TOK, D), BF),
            pltpu.VMEM((8, TOK, 256), BF),
            pltpu.VMEM((TOK, 256), BF),
            pltpu.VMEM((5, ROWS, D), BF),
            pltpu.VMEM((5, ROWS, D), BF),
            pltpu.VMEM((5, WINDOW, D), BF),
            pltpu.VMEM((5, WINDOW, D), BF),
            pltpu.VMEM((5, WINDOW, D), BF),
            pltpu.VMEM((5, WINDOW, D), BF),
            pltpu.VMEM((5, ROWS, D), BF),
            pltpu.VMEM((NZ, ROWS, TOK), BF),
            pltpu.VMEM((NZ, TOK, ROWS), BF),
            pltpu.VMEM((D, EF), BF),
            pltpu.VMEM((D, EF), BF),
            pltpu.VMEM((EF, D), BF),
            pltpu.VMEM((ROWS + 2 * WINDOW, D), BF),
            pltpu.VMEM((ROWS + 2 * WINDOW, EF), BF),
            pltpu.VMEM((TOK, D), F32),
            pltpu.SemaphoreType.DMA((3, 2, 5)),
            pltpu.SemaphoreType.DMA((3, 2, 5)),
            pltpu.SemaphoreType.DMA((3, 2, 4)),
            pltpu.SemaphoreType.DMA((3, 2, 4)),
            pltpu.SemaphoreType.DMA((5, 2)),
            pltpu.SemaphoreType.DMA((5, 2)),
            pltpu.SemaphoreType.DMA((5, 2)),
            pltpu.SemaphoreType.DMA((5, 2)),
            pltpu.SemaphoreType.DMA((2,)),
            pltpu.SemaphoreType.DMA((2,)),
            pltpu.SemaphoreType.DMA((42,)),
            pltpu.SemaphoreType.DMA((42,)),
            pltpu.SemaphoreType.DMA((5,)),
        ],
        compiler_params=pltpu.CompilerParams(
            collective_id=1, has_side_effects=True, vmem_limit_bytes=62 << 20
        ),
        name="experts",
    )(normed, residual, routed, cross_routed, w_gate[0], w_up[0], w_down[0])
    return result[None]


def solution(mesh):
    in_specs = (
        P("exp", "ctx", None),
        P("exp", "ctx", None),
        P("exp", "ctx", None),
        P("exp", None),
        P(),
        P("exp", "ctx", None),
        P("exp", "ctx", None),
        P("exp", None, None),
        P("exp", None, None),
        P("exp", None, None),
    )
    out_specs = P("exp", "ctx", None)
    return jax.shard_map(body, mesh=mesh, in_specs=in_specs, out_specs=out_specs, check_vma=False)
```

```python
import functools
import math

import jax
import jax.numpy as jnp
from jax import lax
from jax.experimental import pallas as pl
from jax.experimental.pallas import tpu as pltpu
from jax.sharding import PartitionSpec as P

D = 2048
QH = 32
KVH = 2
HD = 128
EF = 768
TOP = 8
TOK = 128
EXPERTS = 32
CAP = 34
ROWS = 144
HALF = 64
DIRECT = 512
QUARTER = 256
RING = DIRECT + 2 * QUARTER
SIDE = 4
NZ = 8
NCTX = 8
MESH = pl.DeviceIdType.MESH
BF = jnp.bfloat16
F32 = jnp.float32

A0, A1, B0 = 0, 1, 2
STREAM = ((0, 0), (1, 0), (0, 1))
HOPS = ((4, 3), (3, 4), (4, 3))


class Place:
    def __init__(self):
        ctx, exp = lax.axis_index("ctx"), lax.axis_index("exp")
        self.ctx, self.exp = ctx, exp
        self.xlo, self.y = ctx // 4, ctx % 4
        self.z, self.xhi, self.core = exp // 4, (exp // 2) % 2, exp % 2

    def device(self, xlo, z, xhi, core):
        return {"ctx": xlo * 4 + self.y, "exp": z * 4 + xhi * 2 + core}

    def up(self):
        return self.device(self.xlo, (self.z + 1) % NZ, self.xhi, self.core)

    def down(self):
        return self.device(self.xlo, (self.z + NZ - 1) % NZ, self.xhi, self.core)

    def cross(self):
        return self.device(1 - self.xlo, self.z, 1 - self.xhi, self.core)

    def peer(self):
        return self.device(self.xlo, self.z, self.xhi, 1 - self.core)

    def plane(self, rel):
        return (self.z + rel + NZ) % NZ

    def column(self, col):
        return self.xhi if col == 0 else 1 - self.xhi

    def slot(self, rel, col, core=None):
        core = self.core if core is None else core
        return self.plane(rel) * 4 + self.column(col) * 2 + core


def rels(k):
    return (0,) if k == 0 else ((4,) if k == 4 else (-k, k))


def remote(src, dst, send, recv, device):
    return pltpu.make_async_remote_copy(
        src_ref=src, dst_ref=dst, send_sem=send, recv_sem=recv, device_id=device, device_id_type=MESH
    )


class Gather:
    def __init__(self, at, buf, zs, zr, cs, cr, ps, pr):
        self.at, self.buf = at, buf
        self.zs, self.zr, self.cs, self.cr, self.ps, self.pr = zs, zr, cs, cr, ps, pr
        self.sent = {k: [] for k in range(5)}

    def rows(self, rel, col, half, core=None):
        start = self.at.slot(rel, col, core) * TOK + half * HALF
        return self.buf.at[pl.ds(pl.multiple_of(start, HALF), HALF)]

    def go(self, k, copy):
        copy.start()
        self.sent[k].append(copy)

    def hop(self, stream, direction, k):
        col, half = STREAM[stream]
        if k > HOPS[stream][direction]:
            return
        rel = -(k - 1) if direction == 0 else k - 1
        ref = self.rows(rel, col, half)
        to = self.at.up() if direction == 0 else self.at.down()
        self.go(abs(rel), remote(ref, ref, self.zs.at[stream, direction, k], self.zr.at[stream, direction, k], to))

    def crossing(self, rel, half):
        ref = self.rows(rel, 0, half)
        index = rel % NZ if half == 1 else NZ
        return remote(ref, ref, self.cs.at[index], self.cr.at[index], self.at.cross())

    def crossed(self, rel, half):
        ref = self.rows(rel, 1, half)
        index = rel % NZ if half == 1 else NZ
        remote(ref, ref, self.cs.at[index], self.cr.at[index], self.at.cross()).wait_recv()

    def block(self, rel, col, core=None):
        return self.buf.at[pl.ds(pl.multiple_of(self.at.slot(rel, col, core) * TOK, TOK), TOK)]

    def share(self, rel, col):
        ref = self.block(rel, col)
        index = (rel % NZ) * 2 + col
        self.go(abs(rel), remote(ref, ref, self.ps.at[index], self.pr.at[index], self.at.peer()))

    def begin(self):
        self.go(0, self.crossing(0, 0))
        for stream in (B0, A0):
            for direction in (0, 1):
                self.hop(stream, direction, 1)
        self.go(0, self.crossing(0, 1))
        self.share(0, 0)

    def begin_column(self):
        self.crossed(0, 0)
        for direction in (0, 1):
            self.hop(A1, direction, 1)

    def ring(self, k):
        for stream in (B0, A0, A1):
            col, half = STREAM[stream]
            for direction in (0, 1):
                if k > HOPS[stream][direction]:
                    continue
                rel = -k if direction == 0 else k
                rel = 4 if k == 4 else rel
                ref = self.rows(rel, col, half)
                sem = self.zr.at[stream, direction, k]
                remote(ref, ref, self.zs.at[stream, direction, k], sem, self.at.up()).wait_recv()
                self.hop(stream, direction, k + 1)
                if stream == B0:
                    self.go(k, self.crossing(rel, 1))
                if stream == A0:
                    self.share(rel, 0)

    def column(self, k):
        for rel in rels(k):
            self.crossed(rel, 1)
            self.share(rel, 1)

    def shared(self, k):
        for rel in rels(k):
            for col in (0, 1):
                ref = self.block(rel, col, 1 - self.at.core)
                index = (rel % NZ) * 2 + col
                remote(ref, ref, self.ps.at[index], self.pr.at[index], self.at.peer()).wait_recv()

    def settle(self, k):
        for copy in self.sent[k]:
            copy.wait_send()


GATHER_SEMS = [
    pltpu.SemaphoreType.DMA((3, 2, 5)),
    pltpu.SemaphoreType.DMA((3, 2, 5)),
    pltpu.SemaphoreType.DMA((9,)),
    pltpu.SemaphoreType.DMA((9,)),
    pltpu.SemaphoreType.DMA((16,)),
    pltpu.SemaphoreType.DMA((16,)),
]


class Around:
    def __init__(self, at, ring, rest, ys, yr, ps, pr):
        self.at, self.ring, self.rest = at, ring, rest
        self.ys, self.yr, self.ps, self.pr = ys, yr, ps, pr
        self.sent = []

    def device(self, off):
        if off == SIDE:
            return {"ctx": (1 - self.at.xlo) * 4 + self.at.y, "exp": self.at.exp}
        return {"ctx": self.at.xlo * 4 + (self.at.y + off) % 4, "exp": self.at.exp}

    def columns(self, off):
        if off >= SIDE:
            side = (self.at.xlo + self.at.xhi + off - SIDE) % 2
            return pl.ds(pl.multiple_of(DIRECT + side * QUARTER, QUARTER), QUARTER)
        start = DIRECT + 2 * QUARTER + (self.at.y + off) % 4 * QUARTER
        return pl.ds(pl.multiple_of(start, QUARTER), QUARTER)

    def rows(self, rel, col, core=None):
        return pl.ds(pl.multiple_of(self.at.slot(rel, col, core) * TOK, TOK), TOK)

    def copy(self, src, rel, col, off, to):
        index = (rel % NZ) * 2 + col
        dst = self.rest.at[off - 1, self.rows(rel, col)]
        return remote(src, dst, self.ys.at[index, off], self.yr.at[index, off], self.device(to))

    def go(self, copy):
        copy.start()
        self.sent.append(copy)

    def give(self, rel, col):
        src = self.ring.at[self.rows(rel, col), pl.ds(DIRECT + QUARTER, QUARTER)]
        self.go(self.copy(src, rel, col, 1, 3))
        self.go(self.copy(src, rel, col, 3, 1))
        if rel == 4:
            self.go(self.copy(src, rel, col, 2, 2))
        side = self.ring.at[self.rows(rel, col), pl.ds(DIRECT, QUARTER)]
        self.go(self.copy(side, rel, col, SIDE, SIDE))

    def arrived(self, rel, col, off):
        here = self.rest.at[off - 1, self.rows(rel, col)]
        self.copy(here, rel, col, off, 1).wait_recv()

    def forward(self, rel, col):
        self.arrived(rel, col, 1)
        self.arrived(rel, col, 3)
        if rel == 4:
            return
        off, to = (3, 1) if col == 0 else (1, 3)
        self.go(self.copy(self.rest.at[off - 1, self.rows(rel, col)], rel, col, 2, to))

    def share(self, rel, col):
        if (rel, col) != (0, 0):
            self.arrived(rel, col, 2)
            self.arrived(rel, col, SIDE)
        ref = self.rest.at[:, self.rows(rel, col)]
        index = (rel % NZ) * 2 + col
        self.go(remote(ref, ref, self.ps.at[index], self.pr.at[index], self.at.peer()))

    def shared(self, k):
        for rel in rels(k):
            for col in (0, 1):
                ref = self.rest.at[:, self.rows(rel, col, 1 - self.at.core)]
                index = (rel % NZ) * 2 + col
                remote(ref, ref, self.ps.at[index], self.pr.at[index], self.at.peer()).wait_recv()

    def settle(self):
        for copy in self.sent:
            copy.wait_send()


def attention_kernel(
    hidden_hbm, query_hbm, kv_hbm, proj_hbm, gain_ref, gates_ref,
    residual_ref, normed_ref, gates_out, cross_gates_out,
    ring, rest, heads, kvs, visible, mixed, total, hidden,
    zs, zr, cs, cr, ps, pr, ks, kr, gs, gr, ys, yr, yps, ypr, g2s, g2r, own_sem,
):
    at = Place()
    position = at.ctx
    place = pl.ds(pl.multiple_of(at.exp * TOK, TOK), TOK)
    loads = [
        (kv_hbm, kvs.at[pl.ds(pl.multiple_of(position * TOK, TOK), TOK)]),
        (proj_hbm.at[:, pl.ds(0, DIRECT)], ring.at[place, pl.ds(0, DIRECT)]),
    ]
    around = Around(at, ring, rest, ys, yr, yps, ypr)
    for off in range(6):
        if off == 0:
            to = ring.at[place, pl.ds(DIRECT + QUARTER, QUARTER)]
        elif off == SIDE:
            to = ring.at[place, pl.ds(DIRECT, QUARTER)]
        else:
            to = rest.at[off - 1 if off < SIDE else SIDE - 1, place]
        loads.append((proj_hbm.at[:, around.columns(off)], to))
    for h in range(QH):
        loads.append((query_hbm.at[:, pl.ds(h * HD, HD)], heads.at[pl.ds(h * TOK, TOK)]))
    loads.append((hidden_hbm, hidden))
    loads = [pltpu.make_async_copy(src, dst, own_sem.at[i]) for i, (src, dst) in enumerate(loads)]
    for load in loads:
        load.start()

    def gate_target(off):
        other = (at.exp + off) % EXPERTS
        other_hi = (other // 2) % 2
        return other, {"ctx": ((at.xlo + at.xhi + other_hi) % 2) * 4 + at.y, "exp": other}

    barrier = pltpu.get_barrier_semaphore()

    def greet(off, carry):
        _, device = gate_target(off)
        pl.semaphore_signal(barrier, inc=1, device_id=device, device_id_type=MESH)
        return carry

    lax.fori_loop(1, EXPERTS, greet, 0)
    for off in range(1, NCTX):
        device = {"ctx": (position + off) % NCTX, "exp": at.exp}
        pl.semaphore_signal(barrier, inc=1, device_id=device, device_id_type=MESH)

    gates_out[pl.ds(at.exp, 1)] = gates_ref[pl.ds(at.exp, 1)]

    def partner_gates(off):
        plane = (at.z + off) % NZ
        src = gates_ref.at[pl.ds(plane * 4 + (1 - at.xhi) * 2, 2)]
        to = at.device(at.xlo, plane, at.xhi, at.core)
        return remote(src, cross_gates_out.at[at.z], g2s.at[off], g2r.at[off], to)

    cross_gates_out[pl.ds(at.z, 1)] = gates_ref[pl.ds(at.z * 4 + (1 - at.xhi) * 2, 2)][None]

    @pl.when(position % 2 == 0)
    def _():
        kvs[pl.ds(pl.multiple_of((position + 1) * TOK, TOK), TOK), :] = jnp.zeros((TOK, 2 * KVH * HD), BF)

    for load in loads[:8]:
        load.wait()
    pl.semaphore_wait(barrier, EXPERTS - 1 + NCTX - 1)

    gather = Gather(at, ring, zs, zr, cs, cr, ps, pr)
    gather.begin()

    mine = kvs.at[pl.ds(pl.multiple_of(position * TOK, TOK), TOK)]

    def kv_copy(off):
        device = {"ctx": (position + off) % NCTX, "exp": at.exp}
        return remote(mine, mine, ks.at[off], kr.at[off], device)

    for off in range(1, NCTX):
        pl.when(position + off < NCTX)(lambda off=off: kv_copy(off).start())

    def send_gates(off, carry):
        other, device = gate_target(off)
        remote(gates_ref.at[other], gates_out.at[at.exp], gs.at[off], gr.at[off], device).start()
        return carry

    lax.fori_loop(1, EXPERTS, send_gates, 0)
    for off in range(1, NZ):
        partner_gates(off).start()
    gather.begin_column()
    around.share(0, 0)
    for load in loads[8:]:
        load.wait()

    def kv_arrived(off):
        ref = kvs.at[pl.ds(pl.multiple_of((position + NCTX - off) % NCTX * TOK, TOK), TOK)]
        remote(ref, ref, ks.at[off], kr.at[off], {"ctx": (position + off) % NCTX, "exp": at.exp}).wait_recv()

    scale = HD ** (-0.5) * math.log2(math.e)
    last = position // 2
    row_pos = position * TOK + lax.broadcasted_iota(jnp.int32, (2 * TOK, 2 * TOK), 0) % TOK
    key_pos = last * 2 * TOK + lax.broadcasted_iota(jnp.int32, (2 * TOK, 2 * TOK), 1)
    visible[...] = jnp.where(row_pos >= key_pos, 0.0, 1.0)

    def attend(pairs, chunk, carry):
        lane = pl.multiple_of((chunk // 8) * HD, HD)
        q = heads[pl.ds(pl.multiple_of(chunk * 2 * TOK, 2 * TOK), 2 * TOK), :]
        parts, running = [], None
        for pair in range(pairs):
            keys = kvs[pair * 2 * TOK : (pair + 1) * 2 * TOK, pl.ds(lane, HD)]
            s = lax.dot_general(q, keys, (((1,), (1,)), ((), ())), preferred_element_type=F32)
            if pair == pairs - 1:
                s = jnp.where(visible[...] == 0.0, s, -1e30)
            parts.append(s)
            top = jnp.maximum(s[:, :TOK], s[:, TOK:])
            running = top if running is None else jnp.maximum(running, top)
        row_max = jnp.max(running, axis=1, keepdims=True)
        row_sum, acc = None, None
        for pair in range(pairs):
            weight = jnp.exp2((parts[pair] - row_max) * scale)
            values = kvs[pair * 2 * TOK : (pair + 1) * 2 * TOK, pl.ds(pl.multiple_of(lane + KVH * HD, HD), HD)]
            part = jnp.dot(weight.astype(BF), values, preferred_element_type=F32)
            both = weight[:, :TOK] + weight[:, TOK:]
            acc = part if acc is None else acc + part
            row_sum = both if row_sum is None else row_sum + both
        out = (acc / jnp.sum(row_sum, axis=1, keepdims=True)).astype(BF)
        plane, side = chunk // 2, chunk % 2
        for i in range(2):
            columns = pl.ds(pl.multiple_of((side * 2 + i) * HD, HD), HD)
            mixed[plane, :, columns] = out[i * TOK : (i + 1) * TOK]
        return carry

    def some(pairs, first, end):
        lax.fori_loop(first, end, functools.partial(attend, pairs), 0)

    def attend_some(first, end):
        for pairs in range(1, NCTX // 2 + 1):
            pl.when(last == pairs - 1)(
                lambda pairs=pairs: some(pairs, first, end)
            )

    def give(k, col):
        for rel in rels(k):
            around.give(rel, col)

    def forward(k, col):
        for rel in rels(k):
            around.forward(rel, col)

    def share(k):
        for rel in rels(k):
            for col in (0, 1):
                if (rel, col) != (0, 0):
                    around.share(rel, col)

    def project(k):
        gather.shared(k)
        around.shared(k)
        for rel in rels(k):
            plane = at.plane(rel)
            rows = pl.ds(pl.multiple_of(plane * 4 * TOK, 4 * TOK), 4 * TOK)

            def tile(n, carry):
                columns = pl.ds(pl.multiple_of(n * 512, 512), 512)
                total[:, columns] += jnp.dot(mixed[plane], ring[rows, columns], preferred_element_type=F32)
                return carry

            lax.fori_loop(0, DIRECT // 512, tile, 0, unroll=True)
            for off in range(6):
                if off in (0, SIDE):
                    start = DIRECT + QUARTER if off == 0 else DIRECT
                    part = ring[rows, start : start + QUARTER]
                else:
                    part = rest[off - 1 if off < SIDE else SIDE - 1, rows, :]
                columns = around.columns(off)
                total[:, columns] += jnp.dot(mixed[plane], part, preferred_element_type=F32)

    gather.column(0)
    give(0, 1)
    gather.ring(1)
    give(1, 0)
    for off in range(1, NCTX):
        pl.when(position - off >= 0)(lambda off=off: kv_arrived(off))

    attend_some(0, 5)
    gather.column(1)
    give(1, 1)
    forward(0, 1)
    forward(1, 0)
    gather.ring(2)
    give(2, 0)
    forward(1, 1)
    attend_some(5, 10)
    gather.column(2)
    give(2, 1)
    forward(2, 0)
    share(0)
    gather.ring(3)
    give(3, 0)
    forward(2, 1)
    share(1)
    attend_some(10, 16)
    total[...] = hidden[...].astype(F32)
    project(0)
    gather.column(3)
    give(3, 1)
    forward(3, 0)
    project(1)
    gather.ring(4)
    give(4, 0)
    forward(3, 1)
    gather.column(4)
    give(4, 1)
    share(2)
    project(2)
    forward(4, 0)
    share(3)
    forward(4, 1)
    share(4)
    project(3)
    project(4)

    def norm(i, carry):
        rows = pl.ds(pl.multiple_of(i * 16, 16), 16)
        r = total[rows, :]
        inverse = lax.rsqrt(jnp.mean(r * r, axis=-1, keepdims=True) + 1e-06)
        normed_ref[rows, :] = (r * inverse * gain_ref[...].astype(F32)[None]).astype(BF)
        residual_ref[rows, :] = r
        return carry

    lax.fori_loop(0, TOK // 16, norm, 0, unroll=4)

    def take_gates(off, carry):
        other, device = gate_target(off)
        origin = (at.exp + EXPERTS - off) % EXPERTS
        copy = remote(gates_ref.at[other], gates_out.at[origin], gs.at[off], gr.at[off], device)
        copy.wait_send()
        copy.wait_recv()
        return carry

    lax.fori_loop(1, EXPERTS, take_gates, 0)
    for off in range(1, NZ):
        ref = cross_gates_out.at[(at.z + NZ - off) % NZ]
        remote(ref, ref, g2s.at[off], g2r.at[off], at.up()).wait_recv()
        partner_gates(off).wait_send()
    for off in range(1, NCTX):
        pl.when(position + off < NCTX)(lambda off=off: kv_copy(off).wait_send())
    around.settle()
    for k in range(5):
        gather.settle(k)


class Cols:
    LEAD = (0, 256)
    LOW = (0, 1024)
    HIGH = (1024, 1024)
    LOW_REST = (256, 768)


WIDE = (Cols.LOW, Cols.HIGH)
COMPACT = (Cols.LOW_REST, Cols.HIGH)
WINDOW = 80


def block_rows(k):
    return WINDOW if k in (0, 4) else ROWS


def expert_kernel(
    normed_hbm, residual_hbm, gates_ref, cross_gates_ref, gate_hbm, up_hbm, down_hbm,
    out_ref,
    own, lead, own_peer, lead_peer, own_ring, lead_ring, lead_last,
    cross_out, cross_in, window_in, result_own, result_peer, result_in, back_in, picks, spreads,
    wg, wu, wd, picked, act, residual_ref,
    zs, zr, rzs, rzr, cs, cr, rcs, rcr, ls, lr, ps, pr, wsem,
):
    at = Place()
    core, other = at.core, 1 - at.core

    def rows(rel, which=None):
        which = core if which is None else which
        return pl.ds(pl.multiple_of(at.plane(rel) * 2 * TOK + which * TOK, TOK), TOK)

    def both(rel):
        return pl.ds(pl.multiple_of(at.plane(rel) * 2 * TOK, 2 * TOK), 2 * TOK)

    def kept(rel):
        return pl.ds(pl.multiple_of(at.plane(rel) * TOK, TOK), TOK)

    def cols(part):
        return pl.ds(part[0], part[1])

    loads = (
        (normed_hbm, own.at[rows(0)]), (gate_hbm, wg), (up_hbm, wu), (down_hbm, wd),
        (residual_hbm, residual_ref),
    )
    loads = [pltpu.make_async_copy(src, dst, wsem.at[i]) for i, (src, dst) in enumerate(loads)]
    for load in loads:
        load.start()
    barrier = pltpu.get_barrier_semaphore()
    for device in (at.up(), at.down(), at.cross(), at.peer()):
        pl.semaphore_signal(barrier, inc=1, device_id=device, device_id_type=MESH)

    before = (
        lax.broadcasted_iota(jnp.int32, (TOK, TOK), 0) < lax.broadcasted_iota(jnp.int32, (TOK, TOK), 1)
    ).astype(BF)

    def place(gate, offset):
        named = gate > 0.0
        rank = jnp.dot(named.astype(BF), before, preferred_element_type=F32)
        where = jnp.where(named, rank + jnp.asarray(offset).astype(F32), -1.0)
        return where[0:1], where.T[:, 0:1]

    def numbers(count):
        return lax.broadcasted_iota(jnp.int32, (count, TOK), 0).astype(F32)

    def numbers_across(count):
        return lax.broadcasted_iota(jnp.int32, (TOK, count), 1).astype(F32)

    def one_hot(hit):
        return jnp.where(hit, 1.0, 0.0).astype(BF)

    for k in range(5):
        for i, rel in enumerate(rels(k)):
            first, first_across = place(cross_gates_ref[at.plane(rel), 0], CAP * i)
            second, second_across = place(cross_gates_ref[at.plane(rel), 1], CAP * i + CAP * len(rels(k)))
            row = numbers(block_rows(k))
            picks[rel % NZ, : block_rows(k), :] = one_hot((row == first) | (row == second))
            row = numbers_across(block_rows(k))
            spreads[rel % NZ, :, : block_rows(k)] = one_hot((row == first_across) | (row == second_across))

    sent = {k: [] for k in range(5)}
    crossing_sent = {k: [] for k in range(5)}
    returned = []

    def go(log, copy):
        copy.start()
        log.append(copy)

    def stream_ref(stream, rel):
        return lead.at[rows(rel)] if stream == 2 else own.at[rows(rel), cols(WIDE[stream])]

    def hop(stream, direction, k):
        if k > HOPS[stream][direction]:
            return
        rel = -(k - 1) if direction == 0 else k - 1
        ref = stream_ref(stream, rel)
        to = at.up() if direction == 0 else at.down()
        go(sent[abs(rel)], remote(ref, ref, zs.at[stream, direction, k], zr.at[stream, direction, k], to))

    def share(index, src, dst, log):
        go(log, remote(src, dst, ps.at[index], pr.at[index], at.peer()))

    def shared(index, ref):
        remote(ref, ref, ps.at[index], pr.at[index], at.peer()).wait_recv()

    def cross_copy(src, dst, k, part, send, recv):
        these = (pl.ds(0, block_rows(k)), cols(COMPACT[part]))
        return remote(src.at[(k, *these)], dst.at[(k, *these)], send.at[k, part], recv.at[k, part], at.cross())

    def cross(k, part):
        start, width = COMPACT[part]

        def tile(n, carry):
            columns = pl.ds(pl.multiple_of(start + n * 256, 256), 256)
            total = None
            for rel in rels(k):
                one = jnp.dot(
                    picks[rel % NZ, : block_rows(k), :], own[rows(rel), columns], preferred_element_type=F32
                )
                total = one if total is None else total + one
            cross_out[k, : block_rows(k), columns] = total.astype(BF)
            return carry

        lax.fori_loop(0, width // 256, tile, 0)
        go(crossing_sent[k], cross_copy(cross_out, cross_in, k, part, cs, cr))

    def ring(k):
        for stream in (0, 1, 2):
            for direction in (0, 1):
                if k > HOPS[stream][direction]:
                    continue
                rel = 4 if k == 4 else (-k if direction == 0 else k)
                ref = stream_ref(stream, rel)
                remote(
                    ref, ref, zs.at[stream, direction, k], zr.at[stream, direction, k], at.up()
                ).wait_recv()
                hop(stream, direction, k + 1)
                if stream == 2:
                    share(8 + rel % NZ, lead.at[rows(rel)], lead.at[rows(rel)], sent[k])
            if stream < 2:
                cross(k, stream)
        for rel in rels(k):
            share(rel % NZ, own.at[rows(rel)], own.at[rows(rel)], sent[k])

    def window(k, which):
        start = which * 64 if block_rows(k) == ROWS else which * 0
        return pl.ds(pl.multiple_of(start, 16), WINDOW)

    def rest():
        return pl.ds(256, D - 256)

    def column(k):
        for part in (0, 1):
            cross_copy(cross_out, cross_in, k, part, cs, cr).wait_recv()
        share(16 + k, cross_in.at[k, window(k, other), rest()], window_in.at[k, :, rest()], returned)

    def gather_done(k):
        for rel in rels(k):
            shared(rel % NZ, own.at[rows(rel, other)])
            shared(8 + rel % NZ, lead.at[rows(rel, other)])
        shared(16 + k, window_in.at[k, :, rest()])
        for copy in sent[k]:
            copy.wait_send()

    def process(k):
        these = rels(k)
        pair = len(these) == 2
        mine = ROWS if pair else WINDOW
        count = mine + 2 * WINDOW
        first, second = slice(mine, mine + WINDOW), slice(mine + WINDOW, count)

        def gate(rel, col, which):
            return gates_ref[at.slot(rel, col, which)]

        own_hits, own_across, gate_mine = [], [], 0.0
        for i, rel in enumerate(these):
            hits, across = [], []
            for which in (0, 1):
                g = gate(rel, 0, which)
                line, standing = place(g, CAP * (2 * i + which))
                hit = numbers(mine) == line
                gate_mine = gate_mine + jnp.sum(jnp.where(hit, g[0:1], 0.0), axis=1, keepdims=True)
                hits.append(one_hot(hit))
                across.append(one_hot(numbers_across(mine) == standing))
            own_hits.append(jnp.concatenate(hits, axis=1))
            own_across.append(jnp.concatenate(across, axis=0))
        window_hits, window_across, gate_windows = [], [], []
        offset = 4 * core if pair else CAP * core
        for which in (core, other):
            hits, across, total = [], [], 0.0
            for i, rel in enumerate(these):
                g = gate(rel, 1, which)
                line, standing = place(g, offset + CAP * i)
                hit = numbers(WINDOW) == line
                total = total + jnp.sum(jnp.where(hit, g[0:1], 0.0), axis=1, keepdims=True)
                hits.append(one_hot(hit))
                across.append(one_hot(numbers_across(WINDOW) == standing))
            window_hits.append(hits)
            window_across.append(across)
            gate_windows.append(total)
        gate_all = jnp.concatenate([gate_mine, *gate_windows], axis=0)

        def pick(n, carry):
            columns = pl.ds(pl.multiple_of(n * 256, 256), 256)
            total = None
            for hits, rel in zip(own_hits, these):
                one = jnp.dot(hits, own[both(rel), columns], preferred_element_type=F32)
                total = one if total is None else total + one
            picked[:mine, columns] = total.astype(BF)
            return carry

        lax.fori_loop(0, D // 256, pick, 0, unroll=True)
        for side, which, target in ((0, core, first), (1, other, second)):
            total = None
            for hits, rel in zip(window_hits[side], these):
                one = jnp.dot(hits, lead[rows(rel, which), :], preferred_element_type=F32)
                total = one if total is None else total + one
            picked[target, :256] = total.astype(BF)
        picked[first, 256:] = cross_in[k, window(k, core), 256:]
        picked[second, 256:] = window_in[k, :, 256:]

        def hidden(n, carry):
            columns = pl.ds(pl.multiple_of(n * 256, 256), 256)
            x = picked[:count, :]
            g = jnp.dot(x, wg[:, columns], preferred_element_type=F32)
            u = jnp.dot(x, wu[:, columns], preferred_element_type=F32)
            act[:count, columns] = (g / (1.0 + jnp.exp(-g)) * u).astype(BF)
            return carry

        lax.fori_loop(0, EF // 256, hidden, 0, unroll=True)

        def scatter(hits, o):
            return jnp.dot(hits, o, preferred_element_type=F32).astype(BF)

        def outputs(columns):
            o = jnp.dot(act[:count, :], wd[:, columns], preferred_element_type=F32)
            o = (o * gate_all).astype(BF)
            for hits, rel in zip(own_across, these):
                own[both(rel), columns] = scatter(hits, o[:mine])
            return o

        o = outputs(slice(0, 256))
        for side, which, target in ((0, core, first), (1, other, second)):
            for hits, rel in zip(window_across[side], these):
                lead[rows(rel, which), :] = scatter(hits, o[target])

        def spread(n, carry):
            columns = pl.ds(pl.multiple_of(n * 256, 256), 256)
            o = outputs(columns)
            result_own[k, :, columns] = o[first]
            result_peer[k, :, columns] = o[second]
            return carry

        lax.fori_loop(1, D // 256, spread, 0, unroll=True)
        for rel in these:
            share(21 + rel % NZ, own.at[rows(rel, other)], own_peer.at[kept(rel)], returned)
            share(29 + rel % NZ, lead.at[rows(rel, other)], lead_peer.at[kept(rel)], returned)
        share(37 + k, result_peer.at[k, :, rest()], result_in.at[k, :, rest()], returned)

    def cross_back(k):
        for copy in crossing_sent[k]:
            copy.wait_send()
        shared(37 + k, result_in.at[k, :, rest()])

        def tile(n, carry):
            columns = pl.ds(pl.multiple_of(n * 256, 256), 256)
            if block_rows(k) == WINDOW:
                value = result_own[k, :, columns].astype(F32) + result_in[k, :, columns].astype(F32)
                cross_out[k, :WINDOW, columns] = value.astype(BF)
                return carry
            cross_out[k, window(k, core), columns] = result_own[k, :, columns]
            target = pl.ds(pl.multiple_of(80 * other, 16), 64)
            cross_out[k, target, columns] = result_in[k, pl.ds(pl.multiple_of(16 * other, 16), 64), columns]
            a = result_own[k, pl.ds(pl.multiple_of(64 * other, 16), 16), columns]
            b = result_in[k, pl.ds(pl.multiple_of(64 * core, 16), 16), columns]
            cross_out[k, 64:80, columns] = (a.astype(F32) + b.astype(F32)).astype(BF)
            return carry

        for part in (0, 1):
            start, width = COMPACT[part]
            lax.fori_loop(start // 256, (start + width) // 256, tile, 0)
            go(returned, cross_copy(cross_out, back_in, k, part, rcs, rcr))

    def ring_ref(stream, direction, k):
        if stream == 2:
            return lead_ring.at[direction * 4 + k]
        return own_ring.at[direction * 4 + k, :, cols(WIDE[stream])]

    def ring_take(stream, direction, k):
        ref = ring_ref(stream, direction, k)
        remote(
            ref, ref, rzs.at[stream, direction, k], rzr.at[stream, direction, k], at.up()
        ).wait_recv()
        return ref

    def gathered(rel, columns, with_cross, ring_parts):
        value = own[rows(rel), columns].astype(F32) + own_peer[kept(rel), columns].astype(F32)
        if with_cross:
            k = abs(rel)
            value = value + jnp.dot(
                spreads[rel % NZ, :, : block_rows(k)], back_in[k, : block_rows(k), columns],
                preferred_element_type=F32,
            )
        for slot in ring_parts:
            value = value + own_ring[slot, :, columns].astype(F32)
        return value

    def ring_give(stream, direction, k):
        if k > HOPS[stream][direction]:
            return
        rel = 4 if k == 4 else (-k if direction == 0 else k)
        chained = k + 1 <= HOPS[stream][direction]
        if chained:
            ring_take(stream, direction, k)
        slots = [direction * 4 + k] if chained else []
        if stream == 2:
            value = lead[rows(rel), :].astype(F32) + lead_peer[kept(rel), :].astype(F32)
            for slot in slots:
                value = value + lead_ring[slot].astype(F32)
            lead[rows(rel), :] = value.astype(BF)
        else:
            def tile(n, carry, with_cross=True):
                columns = pl.ds(pl.multiple_of(n * 256, 256), 256)
                own[rows(rel), columns] = gathered(rel, columns, with_cross, slots).astype(BF)
                return carry

            if stream == 0:
                tile(0, 0, False)
            lax.fori_loop(stream * 4 + (stream == 0), stream * 4 + 4, tile, 0)
        to = at.down() if direction == 0 else at.up()
        go(returned, remote(
            stream_ref(stream, rel), ring_ref(stream, direction, k - 1),
            rzs.at[stream, direction, k - 1], rzr.at[stream, direction, k - 1], to,
        ))

    def from_peer(k):
        for rel in rels(k):
            shared(21 + rel % NZ, own_peer.at[kept(rel)])
            shared(29 + rel % NZ, lead_peer.at[kept(rel)])

    loads[0].wait()
    pl.semaphore_wait(barrier, 4)
    lead_first = remote(own.at[rows(0), cols(Cols.LEAD)], lead.at[rows(0)], ls.at[0], lr.at[0], at.cross())
    go(sent[0], lead_first)
    for stream in (0, 1):
        for direction in (0, 1):
            hop(stream, direction, 1)
    share(0, own.at[rows(0)], own.at[rows(0)], sent[0])
    cross(0, 0)
    cross(0, 1)
    lead_first.wait_recv()
    for direction in (0, 1):
        hop(2, direction, 1)
    share(8, lead.at[rows(0)], lead.at[rows(0)], sent[0])

    for k in range(3):
        ring(k + 1)
        if k == 0:
            for load in loads[1:]:
                load.wait()
        column(k)
        gather_done(k)
        if k == 2:
            ring(4)
        process(k)
    column(3)
    column(4)
    for k in (4, 3):
        gather_done(k)
        process(k)
        cross_back(k)
    for k in (4, 3, 2, 1):
        from_peer(k)
        for direction in (0, 1):
            ring_give(2, direction, k)
        if k <= 3:
            cross_back(k - 1)
        for part in (0, 1):
            cross_copy(cross_out, back_in, k, part, rcs, rcr).wait_recv()
            for direction in (0, 1):
                ring_give(part, direction, k)
    from_peer(0)
    for direction in (0, 1):
        ring_take(2, direction, 0)
    value = lead[rows(0), :].astype(F32) + lead_peer[kept(0), :].astype(F32)
    lead[rows(0), :] = (value + lead_ring[0].astype(F32) + lead_ring[4].astype(F32)).astype(BF)
    last = remote(lead.at[rows(0)], lead_last, ls.at[1], lr.at[1], at.cross())
    last.start()
    for part in (0, 1):
        cross_copy(cross_out, back_in, 0, part, rcs, rcr).wait_recv()
        for direction in (0, 1):
            ring_take(part, direction, 0)

        def tile(n, carry):
            columns = pl.ds(pl.multiple_of(n * 256, 256), 256)
            value = gathered(0, columns, True, (0, 4))
            out_ref[:, columns] = (residual_ref[:, columns] + value).astype(BF)
            return carry

        lax.fori_loop(1 if part == 0 else 4, part * 4 + 4, tile, 0)
    last.wait()
    value = gathered(0, slice(0, 256), False, (0, 4)) + lead_last[...].astype(F32)
    out_ref[:, :256] = (residual_ref[:, :256] + value).astype(BF)
    for copy in returned:
        copy.wait_send()


VMEM = pl.BlockSpec(memory_space=pltpu.VMEM)
ANY = pl.BlockSpec(memory_space=pl.ANY)


def body(
    hidden_in, query, keyval, out_proj, norm_gain, expert_ids, gate_weights, w_gate, w_up, w_down
):
    names = jnp.arange(EXPERTS, dtype=jnp.int32)[:, None, None]
    gates = jnp.sum(
        jnp.where(expert_ids[0].T[None] == names, gate_weights[0].T[None], 0.0), axis=1
    )
    gates = jnp.broadcast_to(gates[:, None, :], (EXPERTS, 8, TOK))

    residual, normed, routed, cross_routed = pl.pallas_call(
        attention_kernel,
        out_shape=(
            jax.ShapeDtypeStruct((TOK, D), F32),
            jax.ShapeDtypeStruct((TOK, D), BF),
            jax.ShapeDtypeStruct((EXPERTS, 8, TOK), F32),
            jax.ShapeDtypeStruct((NZ, 2, 8, TOK), F32),
        ),
        in_specs=[ANY, ANY, ANY, ANY, VMEM, VMEM],
        out_specs=(VMEM, VMEM, VMEM, VMEM),
        scratch_shapes=[
            pltpu.VMEM((QH * HD, RING), BF),
            pltpu.VMEM((4, QH * HD, QUARTER), BF),
            pltpu.VMEM((QH * TOK, HD), BF),
            pltpu.VMEM((NCTX * TOK, 2 * KVH * HD), BF),
            pltpu.VMEM((2 * TOK, 2 * TOK), F32),
            pltpu.VMEM((NZ, TOK, 4 * HD), BF),
            pltpu.VMEM((TOK, D), F32),
            pltpu.VMEM((TOK, D), BF),
            *GATHER_SEMS,
            pltpu.SemaphoreType.DMA((NCTX,)),
            pltpu.SemaphoreType.DMA((NCTX,)),
            pltpu.SemaphoreType.DMA((EXPERTS,)),
            pltpu.SemaphoreType.DMA((EXPERTS,)),
            pltpu.SemaphoreType.DMA((16, 5)),
            pltpu.SemaphoreType.DMA((16, 5)),
            pltpu.SemaphoreType.DMA((16,)),
            pltpu.SemaphoreType.DMA((16,)),
            pltpu.SemaphoreType.DMA((NZ,)),
            pltpu.SemaphoreType.DMA((NZ,)),
            pltpu.SemaphoreType.DMA((QH + 9,)),
        ],
        compiler_params=pltpu.CompilerParams(
            collective_id=0, has_side_effects=True, vmem_limit_bytes=62 << 20
        ),
        name="attend_project",
    )(hidden_in[0], query[0], keyval[0], out_proj, norm_gain, gates)

    result = pl.pallas_call(
        expert_kernel,
        out_shape=jax.ShapeDtypeStruct((TOK, D), BF),
        in_specs=[ANY, ANY, VMEM, VMEM, ANY, ANY, ANY],
        out_specs=VMEM,
        scratch_shapes=[
            pltpu.VMEM((NZ * 2 * TOK, D), BF),
            pltpu.VMEM((NZ * 2 * TOK, 256), BF),
            pltpu.VMEM((NZ * TOK, D), BF),
            pltpu.VMEM((NZ * TOK, 256), BF),
            pltpu.VMEM((8, TOK, D), BF),
            pltpu.VMEM((8, TOK, 256), BF),
            pltpu.VMEM((TOK, 256), BF),
            pltpu.VMEM((5, ROWS, D), BF),
            pltpu.VMEM((5, ROWS, D), BF),
            pltpu.VMEM((5, WINDOW, D), BF),
            pltpu.VMEM((5, WINDOW, D), BF),
            pltpu.VMEM((5, WINDOW, D), BF),
            pltpu.VMEM((5, WINDOW, D), BF),
            pltpu.VMEM((5, ROWS, D), BF),
            pltpu.VMEM((NZ, ROWS, TOK), BF),
            pltpu.VMEM((NZ, TOK, ROWS), BF),
            pltpu.VMEM((D, EF), BF),
            pltpu.VMEM((D, EF), BF),
            pltpu.VMEM((EF, D), BF),
            pltpu.VMEM((ROWS + 2 * WINDOW, D), BF),
            pltpu.VMEM((ROWS + 2 * WINDOW, EF), BF),
            pltpu.VMEM((TOK, D), F32),
            pltpu.SemaphoreType.DMA((3, 2, 5)),
            pltpu.SemaphoreType.DMA((3, 2, 5)),
            pltpu.SemaphoreType.DMA((3, 2, 4)),
            pltpu.SemaphoreType.DMA((3, 2, 4)),
            pltpu.SemaphoreType.DMA((5, 2)),
            pltpu.SemaphoreType.DMA((5, 2)),
            pltpu.SemaphoreType.DMA((5, 2)),
            pltpu.SemaphoreType.DMA((5, 2)),
            pltpu.SemaphoreType.DMA((2,)),
            pltpu.SemaphoreType.DMA((2,)),
            pltpu.SemaphoreType.DMA((42,)),
            pltpu.SemaphoreType.DMA((42,)),
            pltpu.SemaphoreType.DMA((5,)),
        ],
        compiler_params=pltpu.CompilerParams(
            collective_id=1, has_side_effects=True, vmem_limit_bytes=62 << 20
        ),
        name="experts",
    )(normed, residual, routed, cross_routed, w_gate[0], w_up[0], w_down[0])
    return result[None]


def solution(mesh):
    in_specs = (
        P("exp", "ctx", None),
        P("exp", "ctx", None),
        P("exp", "ctx", None),
        P("exp", None),
        P(),
        P("exp", "ctx", None),
        P("exp", "ctx", None),
        P("exp", None, None),
        P("exp", None, None),
        P("exp", None, None),
    )
    out_specs = P("exp", "ctx", None)
    return jax.shard_map(body, mesh=mesh, in_specs=in_specs, out_specs=out_specs, check_vma=False)
```

```python
import functools
import math

import jax
import jax.numpy as jnp
from jax import lax
from jax.experimental import pallas as pl
from jax.experimental.pallas import tpu as pltpu
from jax.sharding import PartitionSpec as P

D = 2048
QH = 32
KVH = 2
HD = 128
EF = 768
TOP = 8
TOK = 128
EXPERTS = 32
CAP = 34
ROWS = 144
HALF = 64
DIRECT = 512
QUARTER = 256
RING = DIRECT + 2 * QUARTER
SIDE = 4
NZ = 8
NCTX = 8
MESH = pl.DeviceIdType.MESH
BF = jnp.bfloat16
F32 = jnp.float32

A0, A1, B0 = 0, 1, 2
STREAM = ((0, 0), (1, 0), (0, 1))
HOPS = ((4, 3), (3, 4), (4, 3))


class Place:
    def __init__(self):
        ctx, exp = lax.axis_index("ctx"), lax.axis_index("exp")
        self.ctx, self.exp = ctx, exp
        self.xlo, self.y = ctx // 4, ctx % 4
        self.z, self.xhi, self.core = exp // 4, (exp // 2) % 2, exp % 2

    def device(self, xlo, z, xhi, core):
        return {"ctx": xlo * 4 + self.y, "exp": z * 4 + xhi * 2 + core}

    def up(self):
        return self.device(self.xlo, (self.z + 1) % NZ, self.xhi, self.core)

    def down(self):
        return self.device(self.xlo, (self.z + NZ - 1) % NZ, self.xhi, self.core)

    def cross(self):
        return self.device(1 - self.xlo, self.z, 1 - self.xhi, self.core)

    def peer(self):
        return self.device(self.xlo, self.z, self.xhi, 1 - self.core)

    def plane(self, rel):
        return (self.z + rel + NZ) % NZ

    def column(self, col):
        return self.xhi if col == 0 else 1 - self.xhi

    def slot(self, rel, col, core=None):
        core = self.core if core is None else core
        return self.plane(rel) * 4 + self.column(col) * 2 + core


def rels(k):
    return (0,) if k == 0 else ((4,) if k == 4 else (-k, k))


def remote(src, dst, send, recv, device):
    return pltpu.make_async_remote_copy(
        src_ref=src, dst_ref=dst, send_sem=send, recv_sem=recv, device_id=device, device_id_type=MESH
    )


class Gather:
    def __init__(self, at, buf, zs, zr, cs, cr, ps, pr):
        self.at, self.buf = at, buf
        self.zs, self.zr, self.cs, self.cr, self.ps, self.pr = zs, zr, cs, cr, ps, pr
        self.sent = {k: [] for k in range(5)}

    def rows(self, rel, col, half, core=None):
        start = self.at.slot(rel, col, core) * TOK + half * HALF
        return self.buf.at[pl.ds(pl.multiple_of(start, HALF), HALF)]

    def go(self, k, copy):
        copy.start()
        self.sent[k].append(copy)

    def hop(self, stream, direction, k):
        col, half = STREAM[stream]
        if k > HOPS[stream][direction]:
            return
        rel = -(k - 1) if direction == 0 else k - 1
        ref = self.rows(rel, col, half)
        to = self.at.up() if direction == 0 else self.at.down()
        self.go(abs(rel), remote(ref, ref, self.zs.at[stream, direction, k], self.zr.at[stream, direction, k], to))

    def crossing(self, rel, half):
        ref = self.rows(rel, 0, half)
        index = rel % NZ if half == 1 else NZ
        return remote(ref, ref, self.cs.at[index], self.cr.at[index], self.at.cross())

    def crossed(self, rel, half):
        ref = self.rows(rel, 1, half)
        index = rel % NZ if half == 1 else NZ
        remote(ref, ref, self.cs.at[index], self.cr.at[index], self.at.cross()).wait_recv()

    def block(self, rel, col, core=None):
        return self.buf.at[pl.ds(pl.multiple_of(self.at.slot(rel, col, core) * TOK, TOK), TOK)]

    def share(self, rel, col):
        ref = self.block(rel, col)
        index = (rel % NZ) * 2 + col
        self.go(abs(rel), remote(ref, ref, self.ps.at[index], self.pr.at[index], self.at.peer()))

    def begin(self):
        self.go(0, self.crossing(0, 0))
        for stream in (B0, A0):
            for direction in (0, 1):
                self.hop(stream, direction, 1)
        self.go(0, self.crossing(0, 1))
        self.share(0, 0)

    def begin_column(self):
        self.crossed(0, 0)
        for direction in (0, 1):
            self.hop(A1, direction, 1)

    def ring(self, k):
        for stream in (B0, A0, A1):
            col, half = STREAM[stream]
            for direction in (0, 1):
                if k > HOPS[stream][direction]:
                    continue
                rel = -k if direction == 0 else k
                rel = 4 if k == 4 else rel
                ref = self.rows(rel, col, half)
                sem = self.zr.at[stream, direction, k]
                remote(ref, ref, self.zs.at[stream, direction, k], sem, self.at.up()).wait_recv()
                self.hop(stream, direction, k + 1)
                if stream == B0:
                    self.go(k, self.crossing(rel, 1))
                if stream == A0:
                    self.share(rel, 0)

    def column(self, k):
        for rel in rels(k):
            self.crossed(rel, 1)
            self.share(rel, 1)

    def shared(self, k):
        for rel in rels(k):
            for col in (0, 1):
                ref = self.block(rel, col, 1 - self.at.core)
                index = (rel % NZ) * 2 + col
                remote(ref, ref, self.ps.at[index], self.pr.at[index], self.at.peer()).wait_recv()

    def settle(self, k):
        for copy in self.sent[k]:
            copy.wait_send()


GATHER_SEMS = [
    pltpu.SemaphoreType.DMA((3, 2, 5)),
    pltpu.SemaphoreType.DMA((3, 2, 5)),
    pltpu.SemaphoreType.DMA((9,)),
    pltpu.SemaphoreType.DMA((9,)),
    pltpu.SemaphoreType.DMA((16,)),
    pltpu.SemaphoreType.DMA((16,)),
]


class Around:
    def __init__(self, at, ring, rest, ys, yr, ps, pr):
        self.at, self.ring, self.rest = at, ring, rest
        self.ys, self.yr, self.ps, self.pr = ys, yr, ps, pr
        self.sent = []

    def device(self, off):
        if off == SIDE:
            return {"ctx": (1 - self.at.xlo) * 4 + self.at.y, "exp": self.at.exp}
        return {"ctx": self.at.xlo * 4 + (self.at.y + off) % 4, "exp": self.at.exp}

    def columns(self, off):
        if off >= SIDE:
            side = (self.at.xlo + self.at.xhi + off - SIDE) % 2
            return pl.ds(pl.multiple_of(DIRECT + side * QUARTER, QUARTER), QUARTER)
        start = DIRECT + 2 * QUARTER + (self.at.y + off) % 4 * QUARTER
        return pl.ds(pl.multiple_of(start, QUARTER), QUARTER)

    def rows(self, rel, col, core=None):
        return pl.ds(pl.multiple_of(self.at.slot(rel, col, core) * TOK, TOK), TOK)

    def copy(self, src, rel, col, off, to):
        index = (rel % NZ) * 2 + col
        dst = self.rest.at[off - 1, self.rows(rel, col)]
        return remote(src, dst, self.ys.at[index, off], self.yr.at[index, off], self.device(to))

    def go(self, copy):
        copy.start()
        self.sent.append(copy)

    def give(self, rel, col):
        src = self.ring.at[self.rows(rel, col), pl.ds(DIRECT + QUARTER, QUARTER)]
        self.go(self.copy(src, rel, col, 1, 3))
        self.go(self.copy(src, rel, col, 3, 1))
        if rel == 4:
            self.go(self.copy(src, rel, col, 2, 2))
        side = self.ring.at[self.rows(rel, col), pl.ds(DIRECT, QUARTER)]
        self.go(self.copy(side, rel, col, SIDE, SIDE))

    def arrived(self, rel, col, off):
        here = self.rest.at[off - 1, self.rows(rel, col)]
        self.copy(here, rel, col, off, 1).wait_recv()

    def forward(self, rel, col):
        self.arrived(rel, col, 1)
        self.arrived(rel, col, 3)
        if rel == 4:
            return
        off, to = (3, 1) if col == 0 else (1, 3)
        self.go(self.copy(self.rest.at[off - 1, self.rows(rel, col)], rel, col, 2, to))

    def share(self, rel, col):
        if (rel, col) != (0, 0):
            self.arrived(rel, col, 2)
            self.arrived(rel, col, SIDE)
        ref = self.rest.at[:, self.rows(rel, col)]
        index = (rel % NZ) * 2 + col
        self.go(remote(ref, ref, self.ps.at[index], self.pr.at[index], self.at.peer()))

    def shared(self, k):
        for rel in rels(k):
            for col in (0, 1):
                ref = self.rest.at[:, self.rows(rel, col, 1 - self.at.core)]
                index = (rel % NZ) * 2 + col
                remote(ref, ref, self.ps.at[index], self.pr.at[index], self.at.peer()).wait_recv()

    def settle(self):
        for copy in self.sent:
            copy.wait_send()


def attention_kernel(
    hidden_hbm, query_hbm, kv_hbm, proj_hbm, gain_ref, gates_ref,
    residual_ref, normed_ref, gates_out, cross_gates_out,
    ring, rest, heads, kvs, visible, mixed, total, hidden,
    zs, zr, cs, cr, ps, pr, ks, kr, gs, gr, ys, yr, yps, ypr, g2s, g2r, own_sem,
):
    at = Place()
    position = at.ctx
    place = pl.ds(pl.multiple_of(at.exp * TOK, TOK), TOK)
    loads = [
        (kv_hbm, kvs.at[pl.ds(pl.multiple_of(position * TOK, TOK), TOK)]),
        (proj_hbm.at[:, pl.ds(0, DIRECT)], ring.at[place, pl.ds(0, DIRECT)]),
    ]
    around = Around(at, ring, rest, ys, yr, yps, ypr)
    for off in range(6):
        if off == 0:
            to = ring.at[place, pl.ds(DIRECT + QUARTER, QUARTER)]
        elif off == SIDE:
            to = ring.at[place, pl.ds(DIRECT, QUARTER)]
        else:
            to = rest.at[off - 1 if off < SIDE else SIDE - 1, place]
        loads.append((proj_hbm.at[:, around.columns(off)], to))
    for h in range(QH):
        loads.append((query_hbm.at[:, pl.ds(h * HD, HD)], heads.at[pl.ds(h * TOK, TOK)]))
    loads.append((hidden_hbm, hidden))
    loads = [pltpu.make_async_copy(src, dst, own_sem.at[i]) for i, (src, dst) in enumerate(loads)]
    for load in loads:
        load.start()

    def gate_target(off):
        other = (at.exp + off) % EXPERTS
        other_hi = (other // 2) % 2
        return other, {"ctx": ((at.xlo + at.xhi + other_hi) % 2) * 4 + at.y, "exp": other}

    barrier = pltpu.get_barrier_semaphore()

    def greet(off, carry):
        _, device = gate_target(off)
        pl.semaphore_signal(barrier, inc=1, device_id=device, device_id_type=MESH)
        return carry

    lax.fori_loop(1, EXPERTS, greet, 0)
    for off in range(1, NCTX):
        device = {"ctx": (position + off) % NCTX, "exp": at.exp}
        pl.semaphore_signal(barrier, inc=1, device_id=device, device_id_type=MESH)

    gates_out[pl.ds(at.exp, 1)] = gates_ref[pl.ds(at.exp, 1)]

    def partner_gates(off):
        plane = (at.z + off) % NZ
        src = gates_ref.at[pl.ds(plane * 4 + (1 - at.xhi) * 2, 2)]
        to = at.device(at.xlo, plane, at.xhi, at.core)
        return remote(src, cross_gates_out.at[at.z], g2s.at[off], g2r.at[off], to)

    cross_gates_out[pl.ds(at.z, 1)] = gates_ref[pl.ds(at.z * 4 + (1 - at.xhi) * 2, 2)][None]

    @pl.when(position % 2 == 0)
    def _():
        kvs[pl.ds(pl.multiple_of((position + 1) * TOK, TOK), TOK), :] = jnp.zeros((TOK, 2 * KVH * HD), BF)

    for load in loads[:8]:
        load.wait()
    pl.semaphore_wait(barrier, EXPERTS - 1 + NCTX - 1)

    gather = Gather(at, ring, zs, zr, cs, cr, ps, pr)
    gather.begin()

    mine = kvs.at[pl.ds(pl.multiple_of(position * TOK, TOK), TOK)]

    def kv_copy(off):
        device = {"ctx": (position + off) % NCTX, "exp": at.exp}
        return remote(mine, mine, ks.at[off], kr.at[off], device)

    for off in range(1, NCTX):
        pl.when(position + off < NCTX)(lambda off=off: kv_copy(off).start())

    def send_gates(off, carry):
        other, device = gate_target(off)
        remote(gates_ref.at[other], gates_out.at[at.exp], gs.at[off], gr.at[off], device).start()
        return carry

    lax.fori_loop(1, EXPERTS, send_gates, 0)
    for off in range(1, NZ):
        partner_gates(off).start()
    gather.begin_column()
    around.share(0, 0)
    for load in loads[8:]:
        load.wait()

    def kv_arrived(off):
        ref = kvs.at[pl.ds(pl.multiple_of((position + NCTX - off) % NCTX * TOK, TOK), TOK)]
        remote(ref, ref, ks.at[off], kr.at[off], {"ctx": (position + off) % NCTX, "exp": at.exp}).wait_recv()

    scale = HD ** (-0.5) * math.log2(math.e)
    last = position // 2
    row_pos = position * TOK + lax.broadcasted_iota(jnp.int32, (2 * TOK, 2 * TOK), 0) % TOK
    key_pos = last * 2 * TOK + lax.broadcasted_iota(jnp.int32, (2 * TOK, 2 * TOK), 1)
    visible[...] = jnp.where(row_pos >= key_pos, 0.0, 1.0)

    def attend(pairs, chunk, carry):
        lane = pl.multiple_of((chunk // 8) * HD, HD)
        q = heads[pl.ds(pl.multiple_of(chunk * 2 * TOK, 2 * TOK), 2 * TOK), :]
        parts, running = [], None
        for pair in range(pairs):
            keys = kvs[pair * 2 * TOK : (pair + 1) * 2 * TOK, pl.ds(lane, HD)]
            s = lax.dot_general(q, keys, (((1,), (1,)), ((), ())), preferred_element_type=F32)
            if pair == pairs - 1:
                s = jnp.where(visible[...] == 0.0, s, -1e30)
            parts.append(s)
            top = jnp.maximum(s[:, :TOK], s[:, TOK:])
            running = top if running is None else jnp.maximum(running, top)
        row_max = jnp.max(running, axis=1, keepdims=True)
        row_sum, acc = None, None
        for pair in range(pairs):
            weight = jnp.exp2((parts[pair] - row_max) * scale)
            values = kvs[pair * 2 * TOK : (pair + 1) * 2 * TOK, pl.ds(pl.multiple_of(lane + KVH * HD, HD), HD)]
            part = jnp.dot(weight.astype(BF), values, preferred_element_type=F32)
            both = weight[:, :TOK] + weight[:, TOK:]
            acc = part if acc is None else acc + part
            row_sum = both if row_sum is None else row_sum + both
        out = (acc / jnp.sum(row_sum, axis=1, keepdims=True)).astype(BF)
        plane, side = chunk // 2, chunk % 2
        for i in range(2):
            columns = pl.ds(pl.multiple_of((side * 2 + i) * HD, HD), HD)
            mixed[plane, :, columns] = out[i * TOK : (i + 1) * TOK]
        return carry

    def some(pairs, first, end):
        lax.fori_loop(first, end, functools.partial(attend, pairs), 0)

    def attend_some(first, end):
        for pairs in range(1, NCTX // 2 + 1):
            pl.when(last == pairs - 1)(
                lambda pairs=pairs: some(pairs, first, end)
            )

    def give(k, col):
        for rel in rels(k):
            around.give(rel, col)

    def forward(k, col):
        for rel in rels(k):
            around.forward(rel, col)

    def share(k):
        for rel in rels(k):
            for col in (0, 1):
                if (rel, col) != (0, 0):
                    around.share(rel, col)

    def project(k):
        gather.shared(k)
        around.shared(k)
        for rel in rels(k):
            plane = at.plane(rel)
            rows = pl.ds(pl.multiple_of(plane * 4 * TOK, 4 * TOK), 4 * TOK)

            def tile(n, carry):
                columns = pl.ds(pl.multiple_of(n * 512, 512), 512)
                total[:, columns] += jnp.dot(mixed[plane], ring[rows, columns], preferred_element_type=F32)
                return carry

            lax.fori_loop(0, DIRECT // 512, tile, 0, unroll=True)
            for off in range(6):
                if off in (0, SIDE):
                    start = DIRECT + QUARTER if off == 0 else DIRECT
                    part = ring[rows, start : start + QUARTER]
                else:
                    part = rest[off - 1 if off < SIDE else SIDE - 1, rows, :]
                columns = around.columns(off)
                total[:, columns] += jnp.dot(mixed[plane], part, preferred_element_type=F32)

    gather.column(0)
    give(0, 1)
    gather.ring(1)
    give(1, 0)
    for off in range(1, NCTX):
        pl.when(position - off >= 0)(lambda off=off: kv_arrived(off))

    attend_some(0, 5)
    gather.column(1)
    give(1, 1)
    forward(0, 1)
    forward(1, 0)
    gather.ring(2)
    give(2, 0)
    forward(1, 1)
    attend_some(5, 10)
    gather.column(2)
    give(2, 1)
    forward(2, 0)
    share(0)
    gather.ring(3)
    give(3, 0)
    forward(2, 1)
    share(1)
    attend_some(10, 16)
    total[...] = hidden[...].astype(F32)
    project(0)
    gather.column(3)
    give(3, 1)
    forward(3, 0)
    project(1)
    gather.ring(4)
    give(4, 0)
    forward(3, 1)
    gather.column(4)
    give(4, 1)
    share(2)
    project(2)
    forward(4, 0)
    share(3)
    forward(4, 1)
    share(4)
    project(3)
    project(4)

    def norm(i, carry):
        rows = pl.ds(pl.multiple_of(i * 16, 16), 16)
        r = total[rows, :]
        inverse = lax.rsqrt(jnp.mean(r * r, axis=-1, keepdims=True) + 1e-06)
        normed_ref[rows, :] = (r * inverse * gain_ref[...].astype(F32)[None]).astype(BF)
        residual_ref[rows, :] = r
        return carry

    lax.fori_loop(0, TOK // 16, norm, 0, unroll=4)

    def take_gates(off, carry):
        other, device = gate_target(off)
        origin = (at.exp + EXPERTS - off) % EXPERTS
        copy = remote(gates_ref.at[other], gates_out.at[origin], gs.at[off], gr.at[off], device)
        copy.wait_send()
        copy.wait_recv()
        return carry

    lax.fori_loop(1, EXPERTS, take_gates, 0)
    for off in range(1, NZ):
        ref = cross_gates_out.at[(at.z + NZ - off) % NZ]
        remote(ref, ref, g2s.at[off], g2r.at[off], at.up()).wait_recv()
        partner_gates(off).wait_send()
    for off in range(1, NCTX):
        pl.when(position + off < NCTX)(lambda off=off: kv_copy(off).wait_send())
    around.settle()
    for k in range(5):
        gather.settle(k)


class Cols:
    LEAD = (0, 256)
    LOW = (0, 1024)
    HIGH = (1024, 1024)
    LOW_REST = (256, 768)


WIDE = (Cols.LOW, Cols.HIGH)
COMPACT = (Cols.LOW_REST, Cols.HIGH)
WINDOW = 80


def block_rows(k):
    return WINDOW if k in (0, 4) else ROWS


def expert_kernel(
    normed_hbm, residual_hbm, gates_ref, cross_gates_ref, gate_hbm, up_hbm, down_hbm,
    out_ref,
    own, lead, own_peer, lead_peer, own_ring, lead_ring, lead_last,
    cross_out, cross_in, window_in, result_own, result_peer, result_in, back_in, picks, spreads,
    wg, wu, wd, picked, act, residual_ref,
    zs, zr, rzs, rzr, cs, cr, rcs, rcr, ls, lr, ps, pr, wsem,
):
    at = Place()
    core, other = at.core, 1 - at.core

    def rows(rel, which=None):
        which = core if which is None else which
        return pl.ds(pl.multiple_of(at.plane(rel) * 2 * TOK + which * TOK, TOK), TOK)

    def both(rel):
        return pl.ds(pl.multiple_of(at.plane(rel) * 2 * TOK, 2 * TOK), 2 * TOK)

    def kept(rel):
        return pl.ds(pl.multiple_of(at.plane(rel) * TOK, TOK), TOK)

    def cols(part):
        return pl.ds(part[0], part[1])

    loads = (
        (normed_hbm, own.at[rows(0)]), (gate_hbm, wg), (up_hbm, wu), (down_hbm, wd),
        (residual_hbm, residual_ref),
    )
    loads = [pltpu.make_async_copy(src, dst, wsem.at[i]) for i, (src, dst) in enumerate(loads)]
    for load in loads:
        load.start()
    barrier = pltpu.get_barrier_semaphore()
    for device in (at.up(), at.down(), at.cross(), at.peer()):
        pl.semaphore_signal(barrier, inc=1, device_id=device, device_id_type=MESH)

    before = (
        lax.broadcasted_iota(jnp.int32, (TOK, TOK), 0) < lax.broadcasted_iota(jnp.int32, (TOK, TOK), 1)
    ).astype(BF)

    def place(gate, offset):
        named = gate > 0.0
        rank = jnp.dot(named.astype(BF), before, preferred_element_type=F32)
        where = jnp.where(named, rank + jnp.asarray(offset).astype(F32), -1.0)
        return where[0:1], where.T[:, 0:1]

    def numbers(count):
        return lax.broadcasted_iota(jnp.int32, (count, TOK), 0).astype(F32)

    def numbers_across(count):
        return lax.broadcasted_iota(jnp.int32, (TOK, count), 1).astype(F32)

    def one_hot(hit):
        return jnp.where(hit, 1.0, 0.0).astype(BF)

    def prepare(k):
        for i, rel in enumerate(rels(k)):
            first, first_across = place(cross_gates_ref[at.plane(rel), 0], CAP * i)
            second, second_across = place(cross_gates_ref[at.plane(rel), 1], CAP * i + CAP * len(rels(k)))
            row = numbers(block_rows(k))
            picks[rel % NZ, : block_rows(k), :] = one_hot((row == first) | (row == second))
            row = numbers_across(block_rows(k))
            spreads[rel % NZ, :, : block_rows(k)] = one_hot((row == first_across) | (row == second_across))

    sent = {k: [] for k in range(5)}
    crossing_sent = {k: [] for k in range(5)}
    returned = []

    def go(log, copy):
        copy.start()
        log.append(copy)

    def stream_ref(stream, rel):
        return lead.at[rows(rel)] if stream == 2 else own.at[rows(rel), cols(WIDE[stream])]

    def hop(stream, direction, k):
        if k > HOPS[stream][direction]:
            return
        rel = -(k - 1) if direction == 0 else k - 1
        ref = stream_ref(stream, rel)
        to = at.up() if direction == 0 else at.down()
        go(sent[abs(rel)], remote(ref, ref, zs.at[stream, direction, k], zr.at[stream, direction, k], to))

    def share(index, src, dst, log):
        go(log, remote(src, dst, ps.at[index], pr.at[index], at.peer()))

    def shared(index, ref):
        remote(ref, ref, ps.at[index], pr.at[index], at.peer()).wait_recv()

    def cross_copy(src, dst, k, part, send, recv):
        these = (pl.ds(0, block_rows(k)), cols(COMPACT[part]))
        return remote(src.at[(k, *these)], dst.at[(k, *these)], send.at[k, part], recv.at[k, part], at.cross())

    def cross(k, part):
        start, width = COMPACT[part]

        def tile(n, carry):
            columns = pl.ds(pl.multiple_of(start + n * 256, 256), 256)
            total = None
            for rel in rels(k):
                one = jnp.dot(
                    picks[rel % NZ, : block_rows(k), :], own[rows(rel), columns], preferred_element_type=F32
                )
                total = one if total is None else total + one
            cross_out[k, : block_rows(k), columns] = total.astype(BF)
            return carry

        lax.fori_loop(0, width // 256, tile, 0)
        go(crossing_sent[k], cross_copy(cross_out, cross_in, k, part, cs, cr))

    def ring(k):
        for stream in (0, 1, 2):
            for direction in (0, 1):
                if k > HOPS[stream][direction]:
                    continue
                rel = 4 if k == 4 else (-k if direction == 0 else k)
                ref = stream_ref(stream, rel)
                remote(
                    ref, ref, zs.at[stream, direction, k], zr.at[stream, direction, k], at.up()
                ).wait_recv()
                hop(stream, direction, k + 1)
                if stream == 2:
                    share(8 + rel % NZ, lead.at[rows(rel)], lead.at[rows(rel)], sent[k])
            if stream < 2:
                cross(k, stream)
        for rel in rels(k):
            share(rel % NZ, own.at[rows(rel)], own.at[rows(rel)], sent[k])

    def window(k, which):
        start = which * 64 if block_rows(k) == ROWS else which * 0
        return pl.ds(pl.multiple_of(start, 16), WINDOW)

    def rest():
        return pl.ds(256, D - 256)

    def column(k):
        for part in (0, 1):
            cross_copy(cross_out, cross_in, k, part, cs, cr).wait_recv()
        share(16 + k, cross_in.at[k, window(k, other), rest()], window_in.at[k, :, rest()], returned)

    def gather_done(k):
        for rel in rels(k):
            shared(rel % NZ, own.at[rows(rel, other)])
            shared(8 + rel % NZ, lead.at[rows(rel, other)])
        shared(16 + k, window_in.at[k, :, rest()])
        for copy in sent[k]:
            copy.wait_send()

    def process(k):
        these = rels(k)
        pair = len(these) == 2
        mine = ROWS if pair else WINDOW
        count = mine + 2 * WINDOW
        first, second = slice(mine, mine + WINDOW), slice(mine + WINDOW, count)

        def gate(rel, col, which):
            return gates_ref[at.slot(rel, col, which)]

        own_hits, own_across, gate_mine = [], [], 0.0
        for i, rel in enumerate(these):
            hits, across = [], []
            for which in (0, 1):
                g = gate(rel, 0, which)
                line, standing = place(g, CAP * (2 * i + which))
                hit = numbers(mine) == line
                gate_mine = gate_mine + jnp.sum(jnp.where(hit, g[0:1], 0.0), axis=1, keepdims=True)
                hits.append(one_hot(hit))
                across.append(one_hot(numbers_across(mine) == standing))
            own_hits.append(jnp.concatenate(hits, axis=1))
            own_across.append(jnp.concatenate(across, axis=0))
        window_hits, window_across, gate_windows = [], [], []
        offset = 4 * core if pair else CAP * core
        for which in (core, other):
            hits, across, total = [], [], 0.0
            for i, rel in enumerate(these):
                g = gate(rel, 1, which)
                line, standing = place(g, offset + CAP * i)
                hit = numbers(WINDOW) == line
                total = total + jnp.sum(jnp.where(hit, g[0:1], 0.0), axis=1, keepdims=True)
                hits.append(one_hot(hit))
                across.append(one_hot(numbers_across(WINDOW) == standing))
            window_hits.append(hits)
            window_across.append(across)
            gate_windows.append(total)
        gate_all = jnp.concatenate([gate_mine, *gate_windows], axis=0)

        def pick(n, carry):
            columns = pl.ds(pl.multiple_of(n * 256, 256), 256)
            total = None
            for hits, rel in zip(own_hits, these):
                one = jnp.dot(hits, own[both(rel), columns], preferred_element_type=F32)
                total = one if total is None else total + one
            picked[:mine, columns] = total.astype(BF)
            return carry

        lax.fori_loop(0, D // 256, pick, 0, unroll=True)
        for side, which, target in ((0, core, first), (1, other, second)):
            total = None
            for hits, rel in zip(window_hits[side], these):
                one = jnp.dot(hits, lead[rows(rel, which), :], preferred_element_type=F32)
                total = one if total is None else total + one
            picked[target, :256] = total.astype(BF)
        picked[first, 256:] = cross_in[k, window(k, core), 256:]
        picked[second, 256:] = window_in[k, :, 256:]

        def hidden(n, carry):
            columns = pl.ds(pl.multiple_of(n * 256, 256), 256)
            x = picked[:count, :]
            g = jnp.dot(x, wg[:, columns], preferred_element_type=F32)
            u = jnp.dot(x, wu[:, columns], preferred_element_type=F32)
            act[:count, columns] = (g / (1.0 + jnp.exp(-g)) * u).astype(BF)
            return carry

        lax.fori_loop(0, EF // 256, hidden, 0, unroll=True)

        def scatter(hits, o):
            return jnp.dot(hits, o, preferred_element_type=F32).astype(BF)

        def outputs(columns):
            o = jnp.dot(act[:count, :], wd[:, columns], preferred_element_type=F32)
            o = (o * gate_all).astype(BF)
            for hits, rel in zip(own_across, these):
                own[both(rel), columns] = scatter(hits, o[:mine])
            return o

        o = outputs(slice(0, 256))
        for side, which, target in ((0, core, first), (1, other, second)):
            for hits, rel in zip(window_across[side], these):
                lead[rows(rel, which), :] = scatter(hits, o[target])

        def spread(n, carry):
            columns = pl.ds(pl.multiple_of(n * 256, 256), 256)
            o = outputs(columns)
            result_own[k, :, columns] = o[first]
            result_peer[k, :, columns] = o[second]
            return carry

        lax.fori_loop(1, D // 256, spread, 0, unroll=True)
        for rel in these:
            share(21 + rel % NZ, own.at[rows(rel, other)], own_peer.at[kept(rel)], returned)
            share(29 + rel % NZ, lead.at[rows(rel, other)], lead_peer.at[kept(rel)], returned)
        share(37 + k, result_peer.at[k, :, rest()], result_in.at[k, :, rest()], returned)

    def cross_back(k):
        for copy in crossing_sent[k]:
            copy.wait_send()
        shared(37 + k, result_in.at[k, :, rest()])

        def tile(n, carry):
            columns = pl.ds(pl.multiple_of(n * 256, 256), 256)
            if block_rows(k) == WINDOW:
                value = result_own[k, :, columns].astype(F32) + result_in[k, :, columns].astype(F32)
                cross_out[k, :WINDOW, columns] = value.astype(BF)
                return carry
            cross_out[k, window(k, core), columns] = result_own[k, :, columns]
            target = pl.ds(pl.multiple_of(80 * other, 16), 64)
            cross_out[k, target, columns] = result_in[k, pl.ds(pl.multiple_of(16 * other, 16), 64), columns]
            a = result_own[k, pl.ds(pl.multiple_of(64 * other, 16), 16), columns]
            b = result_in[k, pl.ds(pl.multiple_of(64 * core, 16), 16), columns]
            cross_out[k, 64:80, columns] = (a.astype(F32) + b.astype(F32)).astype(BF)
            return carry

        for part in (0, 1):
            start, width = COMPACT[part]
            lax.fori_loop(start // 256, (start + width) // 256, tile, 0)
            go(returned, cross_copy(cross_out, back_in, k, part, rcs, rcr))

    def ring_ref(stream, direction, k):
        if stream == 2:
            return lead_ring.at[direction * 4 + k]
        return own_ring.at[direction * 4 + k, :, cols(WIDE[stream])]

    def ring_take(stream, direction, k):
        ref = ring_ref(stream, direction, k)
        remote(
            ref, ref, rzs.at[stream, direction, k], rzr.at[stream, direction, k], at.up()
        ).wait_recv()
        return ref

    def gathered(rel, columns, with_cross, ring_parts):
        value = own[rows(rel), columns].astype(F32) + own_peer[kept(rel), columns].astype(F32)
        if with_cross:
            k = abs(rel)
            value = value + jnp.dot(
                spreads[rel % NZ, :, : block_rows(k)], back_in[k, : block_rows(k), columns],
                preferred_element_type=F32,
            )
        for slot in ring_parts:
            value = value + own_ring[slot, :, columns].astype(F32)
        return value

    def ring_give(stream, direction, k):
        if k > HOPS[stream][direction]:
            return
        rel = 4 if k == 4 else (-k if direction == 0 else k)
        chained = k + 1 <= HOPS[stream][direction]
        if chained:
            ring_take(stream, direction, k)
        slots = [direction * 4 + k] if chained else []
        if stream == 2:
            value = lead[rows(rel), :].astype(F32) + lead_peer[kept(rel), :].astype(F32)
            for slot in slots:
                value = value + lead_ring[slot].astype(F32)
            lead[rows(rel), :] = value.astype(BF)
        else:
            def tile(n, carry, with_cross=True):
                columns = pl.ds(pl.multiple_of(n * 256, 256), 256)
                own[rows(rel), columns] = gathered(rel, columns, with_cross, slots).astype(BF)
                return carry

            if stream == 0:
                tile(0, 0, False)
            lax.fori_loop(stream * 4 + (stream == 0), stream * 4 + 4, tile, 0)
        to = at.down() if direction == 0 else at.up()
        go(returned, remote(
            stream_ref(stream, rel), ring_ref(stream, direction, k - 1),
            rzs.at[stream, direction, k - 1], rzr.at[stream, direction, k - 1], to,
        ))

    def from_peer(k):
        for rel in rels(k):
            shared(21 + rel % NZ, own_peer.at[kept(rel)])
            shared(29 + rel % NZ, lead_peer.at[kept(rel)])

    loads[0].wait()
    pl.semaphore_wait(barrier, 4)
    lead_first = remote(own.at[rows(0), cols(Cols.LEAD)], lead.at[rows(0)], ls.at[0], lr.at[0], at.cross())
    go(sent[0], lead_first)
    for stream in (0, 1):
        for direction in (0, 1):
            hop(stream, direction, 1)
    share(0, own.at[rows(0)], own.at[rows(0)], sent[0])
    prepare(0)
    cross(0, 0)
    cross(0, 1)
    lead_first.wait_recv()
    for direction in (0, 1):
        hop(2, direction, 1)
    share(8, lead.at[rows(0)], lead.at[rows(0)], sent[0])
    for k in range(1, 5):
        prepare(k)

    for k in range(3):
        ring(k + 1)
        if k == 0:
            for load in loads[1:]:
                load.wait()
        column(k)
        gather_done(k)
        if k == 2:
            ring(4)
        process(k)
    column(3)
    column(4)
    for k in (4, 3):
        gather_done(k)
        process(k)
        cross_back(k)
    for k in (4, 3, 2, 1):
        from_peer(k)
        for direction in (0, 1):
            ring_give(2, direction, k)
        if k <= 3:
            cross_back(k - 1)
        for part in (0, 1):
            cross_copy(cross_out, back_in, k, part, rcs, rcr).wait_recv()
            for direction in (0, 1):
                ring_give(part, direction, k)
    from_peer(0)
    for direction in (0, 1):
        ring_take(2, direction, 0)
    value = lead[rows(0), :].astype(F32) + lead_peer[kept(0), :].astype(F32)
    lead[rows(0), :] = (value + lead_ring[0].astype(F32) + lead_ring[4].astype(F32)).astype(BF)
    last = remote(lead.at[rows(0)], lead_last, ls.at[1], lr.at[1], at.cross())
    last.start()
    for part in (0, 1):
        cross_copy(cross_out, back_in, 0, part, rcs, rcr).wait_recv()
        for direction in (0, 1):
            ring_take(part, direction, 0)

        def tile(n, carry):
            columns = pl.ds(pl.multiple_of(n * 256, 256), 256)
            value = gathered(0, columns, True, (0, 4))
            out_ref[:, columns] = (residual_ref[:, columns] + value).astype(BF)
            return carry

        lax.fori_loop(1 if part == 0 else 4, part * 4 + 4, tile, 0)
    last.wait()
    value = gathered(0, slice(0, 256), False, (0, 4)) + lead_last[...].astype(F32)
    out_ref[:, :256] = (residual_ref[:, :256] + value).astype(BF)
    for copy in returned:
        copy.wait_send()


VMEM = pl.BlockSpec(memory_space=pltpu.VMEM)
ANY = pl.BlockSpec(memory_space=pl.ANY)


def body(
    hidden_in, query, keyval, out_proj, norm_gain, expert_ids, gate_weights, w_gate, w_up, w_down
):
    names = jnp.arange(EXPERTS, dtype=jnp.int32)[:, None, None]
    gates = jnp.sum(
        jnp.where(expert_ids[0].T[None] == names, gate_weights[0].T[None], 0.0), axis=1
    )
    gates = jnp.broadcast_to(gates[:, None, :], (EXPERTS, 8, TOK))

    residual, normed, routed, cross_routed = pl.pallas_call(
        attention_kernel,
        out_shape=(
            jax.ShapeDtypeStruct((TOK, D), F32),
            jax.ShapeDtypeStruct((TOK, D), BF),
            jax.ShapeDtypeStruct((EXPERTS, 8, TOK), F32),
            jax.ShapeDtypeStruct((NZ, 2, 8, TOK), F32),
        ),
        in_specs=[ANY, ANY, ANY, ANY, VMEM, VMEM],
        out_specs=(VMEM, VMEM, VMEM, VMEM),
        scratch_shapes=[
            pltpu.VMEM((QH * HD, RING), BF),
            pltpu.VMEM((4, QH * HD, QUARTER), BF),
            pltpu.VMEM((QH * TOK, HD), BF),
            pltpu.VMEM((NCTX * TOK, 2 * KVH * HD), BF),
            pltpu.VMEM((2 * TOK, 2 * TOK), F32),
            pltpu.VMEM((NZ, TOK, 4 * HD), BF),
            pltpu.VMEM((TOK, D), F32),
            pltpu.VMEM((TOK, D), BF),
            *GATHER_SEMS,
            pltpu.SemaphoreType.DMA((NCTX,)),
            pltpu.SemaphoreType.DMA((NCTX,)),
            pltpu.SemaphoreType.DMA((EXPERTS,)),
            pltpu.SemaphoreType.DMA((EXPERTS,)),
            pltpu.SemaphoreType.DMA((16, 5)),
            pltpu.SemaphoreType.DMA((16, 5)),
            pltpu.SemaphoreType.DMA((16,)),
            pltpu.SemaphoreType.DMA((16,)),
            pltpu.SemaphoreType.DMA((NZ,)),
            pltpu.SemaphoreType.DMA((NZ,)),
            pltpu.SemaphoreType.DMA((QH + 9,)),
        ],
        compiler_params=pltpu.CompilerParams(
            collective_id=0, has_side_effects=True, vmem_limit_bytes=62 << 20
        ),
        name="attend_project",
    )(hidden_in[0], query[0], keyval[0], out_proj, norm_gain, gates)

    result = pl.pallas_call(
        expert_kernel,
        out_shape=jax.ShapeDtypeStruct((TOK, D), BF),
        in_specs=[ANY, ANY, VMEM, VMEM, ANY, ANY, ANY],
        out_specs=VMEM,
        scratch_shapes=[
            pltpu.VMEM((NZ * 2 * TOK, D), BF),
            pltpu.VMEM((NZ * 2 * TOK, 256), BF),
            pltpu.VMEM((NZ * TOK, D), BF),
            pltpu.VMEM((NZ * TOK, 256), BF),
            pltpu.VMEM((8, TOK, D), BF),
            pltpu.VMEM((8, TOK, 256), BF),
            pltpu.VMEM((TOK, 256), BF),
            pltpu.VMEM((5, ROWS, D), BF),
            pltpu.VMEM((5, ROWS, D), BF),
            pltpu.VMEM((5, WINDOW, D), BF),
            pltpu.VMEM((5, WINDOW, D), BF),
            pltpu.VMEM((5, WINDOW, D), BF),
            pltpu.VMEM((5, WINDOW, D), BF),
            pltpu.VMEM((5, ROWS, D), BF),
            pltpu.VMEM((NZ, ROWS, TOK), BF),
            pltpu.VMEM((NZ, TOK, ROWS), BF),
            pltpu.VMEM((D, EF), BF),
            pltpu.VMEM((D, EF), BF),
            pltpu.VMEM((EF, D), BF),
            pltpu.VMEM((ROWS + 2 * WINDOW, D), BF),
            pltpu.VMEM((ROWS + 2 * WINDOW, EF), BF),
            pltpu.VMEM((TOK, D), F32),
            pltpu.SemaphoreType.DMA((3, 2, 5)),
            pltpu.SemaphoreType.DMA((3, 2, 5)),
            pltpu.SemaphoreType.DMA((3, 2, 4)),
            pltpu.SemaphoreType.DMA((3, 2, 4)),
            pltpu.SemaphoreType.DMA((5, 2)),
            pltpu.SemaphoreType.DMA((5, 2)),
            pltpu.SemaphoreType.DMA((5, 2)),
            pltpu.SemaphoreType.DMA((5, 2)),
            pltpu.SemaphoreType.DMA((2,)),
            pltpu.SemaphoreType.DMA((2,)),
            pltpu.SemaphoreType.DMA((42,)),
            pltpu.SemaphoreType.DMA((42,)),
            pltpu.SemaphoreType.DMA((5,)),
        ],
        compiler_params=pltpu.CompilerParams(
            collective_id=1, has_side_effects=True, vmem_limit_bytes=62 << 20
        ),
        name="experts",
    )(normed, residual, routed, cross_routed, w_gate[0], w_up[0], w_down[0])
    return result[None]


def solution(mesh):
    in_specs = (
        P("exp", "ctx", None),
        P("exp", "ctx", None),
        P("exp", "ctx", None),
        P("exp", None),
        P(),
        P("exp", "ctx", None),
        P("exp", "ctx", None),
        P("exp", None, None),
        P("exp", None, None),
        P("exp", None, None),
    )
    out_specs = P("exp", "ctx", None)
    return jax.shard_map(body, mesh=mesh, in_specs=in_specs, out_specs=out_specs, check_vma=False)
```
